128 devices in a mesh: gx: 8 (over z_lo, x), gy: 4 (over y), gz: 4 (over z_hi, core).
Axes of the slice: x: 4, y: 4, z: 4 (z_hi: 2, z_lo: 2; z = z_hi * 2 + z_lo), core: 2. Of those that a mesh axis runs over, the one named last changes fastest.
Arguments:
- force: float32 [3, 128, 32, 512], P(None, 'gx', 'gy', 'gz')
- kappa: float32 [128, 32, 512], P('gx', 'gy', 'gz'), may hold values from 0.5 to 4
- mortar_blocks: float32 [8, 4, 4, 192, 4096], P('gx', 'gy', 'gz'), may hold values from -0.375 to 0.375
- mortar_index: int32 [8, 4, 4, 48, 4], P('gx', 'gy', 'gz'), may hold values from 0 to 47, as said below
- mortar_count: int32 [8, 4, 4, 48], P('gx', 'gy', 'gz'), may hold values from 1 to 4, as said below
- agg_map: int32 [128, 32, 512], P('gx', 'gy', 'gz'), may hold values from 0 to 511
- coarse_matrix: float32 [8, 4, 512, 512], P('gx', 'gy', 'gz'), may hold values from -0.125 to 0.125
- coarse_diag: float32 [8, 4, 512], P('gx', 'gy', 'gz'), may hold values from 1 to 3
Outputs:
- velocity: float32 [3, 128, 32, 512], P(None, 'gx', 'gy', 'gz')
- multipliers: float32 [8, 3, 32, 512], P('gx', None, 'gy', 'gz')
The draws below stay inside these ranges and needn't reach their ends.
Inputs may be any that keep to these rules, and one draw needn't show every extreme that they name: `mortar_index`: entry k of block j's list is block (j + s + k) modulo 48, for a shift s of -3 to 0 drawn for each block; the entries of one list are distinct. `mortar_count`: some block of every device uses all 4 entries.
All inputs are finite; a program needn't handle non-finite values.
Results may differ from the reference program's by a relative error of at most 0.0003.
Values sent between devices are 32-bit elements; how exact they have to be, the bound alone decides.
No kernel may reach another device: no remote copies, remote signals or barrier semaphores. Data moves between devices by JAX's collectives and lax.ppermute only.
A program may use at most 64 MiB of HBM per device.

```python
import math
import jax
import jax.numpy as jnp
from jax import lax

CX = 16
CY = 8
CZ = 128
BLK = 64
KMAX = 4
NAGG = 512
NPRE = 2
NPOST = 2
NCOARSE = 4
NBLK = 48
NX = 128
NY = 32
NZ = 512
N_GX = 8
N_GY = 4
N_GZ = 4


def draw_force(key, part):
    key = jax.random.fold_in(key, 11)
    layout = (3, NX, NY, NZ)
    return 4.0 * jax.random.truncated_normal(key, -4.0, 4.0, layout, jnp.float32)


def draw_mortar_index(key, part):
    key = jax.random.fold_in(key, 12)
    layout = (NX // CX, NY // CY, NZ // CZ, NBLK, KMAX)
    offset = jax.random.randint(key, layout[:4] + (1,), 1 - KMAX, 1, jnp.int32)
    slot_ids = lax.broadcasted_iota(jnp.int32, layout, 3) + lax.broadcasted_iota(jnp.int32, layout, 4) + offset
    return jnp.mod(slot_ids + NBLK, NBLK).astype(jnp.int32)


def draw_mortar_count(key, part):
    key = jax.random.fold_in(key, 13)
    device_dims = (NX // CX, NY // CY, NZ // CZ, 1)
    layout = (NX // CX, NY // CY, NZ // CZ, NBLK)
    heavy_key, block_key, peak_key = jax.random.split(key, 3)
    heaviness = jax.random.randint(heavy_key, device_dims, 0, KMAX, jnp.int32)
    counts = jnp.minimum(1 + heaviness + jax.random.randint(block_key, layout, 0, 2, jnp.int32), KMAX)
    peak_slot = jax.random.randint(peak_key, device_dims, 0, NBLK, jnp.int32)
    return jnp.where(lax.broadcasted_iota(jnp.int32, layout, 3) == peak_slot, KMAX, counts).astype(jnp.int32)


def set_ends(result, key, smallest, top_value):
    extent = result.shape
    place = [jax.random.randint(jax.random.fold_in(key, axis), (), 0, extent[axis]) for axis in range(len(extent))]
    result = result.at[tuple(place)].set(smallest)
    longest = extent.index(max(extent))
    place[longest] = (place[longest] + 1) % extent[longest]
    return result.at[tuple(place)].set(top_value)


def shard_levels(rng, shape, cuts, low, largest):
    gain = 1.0
    for position, shards_of in cuts:
        steps = jax.random.uniform(jax.random.fold_in(jax.random.fold_in(rng, 6), position), (shards_of,), jnp.float32, low / len(cuts), largest / len(cuts))
        gain = gain * jnp.repeat(jnp.exp(steps), shape[position] // shards_of).reshape((-1,) + (1,) * (len(shape) - 1 - position))
    return gain


def normal_values(rng, dims, scale, most, cuts=(), kind=jnp.bfloat16):
    result = scale * jax.random.normal(rng, dims, jnp.float32)
    if cuts:
        result = result * shard_levels(rng, dims, cuts, -0.22, 0.18)
    return jnp.clip(result, -most, most).astype(kind)


def setup_inputs(seed: int = 0) -> dict:
    keys = jax.random.split(jax.random.key(seed), 9)
    force = draw_force(jax.random.fold_in(keys[8], 71), 0)
    kappa = jnp.clip(0.5 + 3.5 * jax.random.uniform(keys[1], (NX, NY, NZ), jnp.float32) ** shard_levels(keys[1], (NX, NY, NZ), ((0, 8), (1, 4), (2, 4)), -0.2, 0.2), 0.5, 4.0)
    mortar_blocks = normal_values(keys[2], (N_GX, N_GY, N_GZ, NBLK * KMAX, BLK * BLK), (BLK * KMAX) ** -0.5, 0.375, ((0, 8), (1, 4), (2, 4)), jnp.float32)
    mortar_index = draw_mortar_index(jax.random.fold_in(keys[8], 71), 0)
    mortar_count = draw_mortar_count(jax.random.fold_in(keys[8], 71), 0)
    agg_map = set_ends(jax.random.randint(keys[5], (NX, NY, NZ), 0, NAGG), jax.random.fold_in(keys[5], 1), 0, NAGG - 1).astype(jnp.int32)
    coarse_matrix = normal_values(keys[6], (N_GX, N_GY, NAGG, NAGG), (4 * NAGG) ** -0.5, 0.125, ((0, 8), (1, 4), (2, 4)), jnp.float32)
    coarse_diag = jnp.clip(jnp.exp(math.log(3.0) - 1.0986123 * jax.random.uniform(keys[7], (N_GX, N_GY, NAGG), jnp.float32) ** shard_levels(keys[7], (N_GX, N_GY, NAGG), ((0, 8), (1, 4), (2, 4)), -0.2, 0.2)), 1.0, 3.0)
    return {"force": force, "kappa": kappa, "mortar_blocks": mortar_blocks, "mortar_index": mortar_index, "mortar_count": mortar_count, "agg_map": agg_map, "coarse_matrix": coarse_matrix, "coarse_diag": coarse_diag}


TOP_PRECISION = lax.Precision.HIGHEST
RELAX_ALPHA = 1.5
SCHUR_THETA = 0.4
COARSE_OMEGA = 0.8
PROLONG_GAIN = 0.5


def operate(vector_field, weight):
    slab_view = vector_field.reshape(3, N_GX, CX, NY, NZ)
    zero_plane = jnp.zeros_like(slab_view[:, :, :1])
    beside = jnp.concatenate([zero_plane, slab_view[:, :, :-1]], 2) + jnp.concatenate([slab_view[:, :, 1:], zero_plane], 2)
    beside = beside.reshape(3, NX, NY, NZ)
    padded = jnp.pad(vector_field, ((0, 0), (0, 0), (1, 1), (1, 1)))
    beside = beside + padded[:, :, 2:, 1:-1] + padded[:, :, :-2, 1:-1]
    beside = beside + padded[:, :, 1:-1, 2:] + padded[:, :, 1:-1, :-2]
    return weight * vector_field - beside


def to_blocks(planes):
    ordered = planes.reshape(3, N_GX, N_GY, CY, N_GZ, CZ).transpose(1, 2, 4, 0, 3, 5)
    return ordered.reshape(N_GX * N_GY * N_GZ, NBLK, BLK)


def from_blocks(blocks):
    ordered = blocks.reshape(N_GX, N_GY, N_GZ, 3, CY, CZ).transpose(3, 0, 1, 4, 2, 5)
    return ordered.reshape(3, N_GX, NY, NZ)


def used_entries(block_count):
    return (jnp.arange(KMAX)[None, :] < block_count[:, None]).astype(jnp.float32)


def project_one(pieces):
    matrices, block_index, block_count, traces = pieces
    chosen = traces[block_index] * used_entries(block_count)[:, :, None]
    return jnp.einsum("jkrc,jkc->jr", matrices, chosen, precision=TOP_PRECISION)


def project_back(pieces):
    matrices, block_index, block_count, values = pieces
    block_terms = jnp.einsum("jkrc,jr->jkc", matrices, values, precision=TOP_PRECISION)
    block_terms = block_terms * used_entries(block_count)[:, :, None]
    return jax.ops.segment_sum(block_terms.reshape(NBLK * KMAX, BLK), block_index.reshape(NBLK * KMAX), NBLK)


def roll_slabs(blocks, shift_by):
    grouped = blocks.reshape(N_GX, N_GY * N_GZ, NBLK, BLK)
    return jnp.roll(grouped, shift_by, axis=0).reshape(N_GX * N_GY * N_GZ, NBLK, BLK)


def apply_mortar(vector_field, mortar):
    slab_view = vector_field.reshape(3, N_GX, CX, NY, NZ)
    uppers = roll_slabs(to_blocks(slab_view[:, :, -1]), 1)
    projected = lax.map(project_one, mortar + (uppers,))
    jump_blocks = to_blocks(slab_view[:, :, 0]) - projected
    return from_blocks(jump_blocks).transpose(1, 0, 2, 3)


def apply_transpose(multipliers, mortar):
    planes = multipliers.transpose(1, 0, 2, 3)
    values = to_blocks(planes)
    pulled = roll_slabs(lax.map(project_back, mortar + (values,)), -1)
    slab_view = jnp.zeros((3, N_GX, CX, NY, NZ), jnp.float32)
    slab_view = slab_view.at[:, :, 0].set(planes)
    slab_view = slab_view.at[:, :, -1].set(-from_blocks(pulled))
    return slab_view.reshape(3, NX, NY, NZ)


def smooth_sweep(velocity, multipliers, force, weight, mortar):
    scaled = RELAX_ALPHA * weight
    face_scale = (SCHUR_THETA * RELAX_ALPHA) * weight.reshape(N_GX, CX, NY, NZ)[:, 0][:, None]
    residual = force - operate(velocity, weight) - apply_transpose(multipliers, mortar)
    step_one = residual / scaled
    schur_rhs = apply_mortar(velocity + step_one, mortar)
    increment = face_scale * schur_rhs
    schur_image = apply_mortar(apply_transpose(increment, mortar) / scaled, mortar)
    increment = increment + face_scale * (schur_rhs - schur_image)
    velocity = velocity + (residual - apply_transpose(increment, mortar)) / scaled
    return velocity, multipliers + increment


def coarse_correct(residual, agg_map, coarse_matrix, coarse_diag):
    group_total = N_GX * N_GY
    group_cells = CX * CY * NZ
    ordered = residual.reshape(3, N_GX, CX, N_GY, CY, NZ).transpose(0, 1, 3, 2, 4, 5).reshape(3, group_total * group_cells)
    members = agg_map.reshape(N_GX, CX, N_GY, CY, NZ).transpose(0, 2, 1, 3, 4).reshape(group_total, group_cells)
    labels = members + NAGG * jnp.arange(group_total, dtype=jnp.int32)[:, None]
    labels = labels.astype(jnp.int32).reshape(group_total * group_cells)
    totals = jax.vmap(lambda values: jax.ops.segment_sum(values, labels, group_total * NAGG))(ordered)
    rest_gain = (group_cells / NAGG) ** -0.5
    coarse_rhs = totals.reshape(3, group_total, NAGG).transpose(1, 0, 2) * rest_gain
    matrices = coarse_matrix.reshape(group_total, NAGG, NAGG)
    scales = coarse_diag.reshape(group_total, 1, NAGG)
    iterate = jnp.zeros((group_total, 3, NAGG), jnp.float32)
    for sweep_index in range(NCOARSE):
        product = scales * iterate + jnp.einsum("gab,gcb->gca", matrices, iterate, precision=TOP_PRECISION)
        iterate = iterate + COARSE_OMEGA * (coarse_rhs - product) / scales
    spread = jax.vmap(lambda iterate_rows, member_ids: jnp.take(iterate_rows, member_ids, axis=1))(iterate, members)
    spread = spread.reshape(N_GX, N_GY, 3, CX, CY, NZ).transpose(2, 0, 3, 1, 4, 5).reshape(3, NX, NY, NZ)
    return PROLONG_GAIN * spread


def reference(force, kappa, mortar_blocks, mortar_index, mortar_count, agg_map, coarse_matrix, coarse_diag):
    device_total = N_GX * N_GY * N_GZ
    weight = 6.0 + kappa
    mortar = (mortar_blocks.reshape(device_total, NBLK, KMAX, BLK, BLK),
              mortar_index.reshape(device_total, NBLK, KMAX),
              mortar_count.reshape(device_total, NBLK))
    velocity = jnp.zeros((3, NX, NY, NZ), jnp.float32)
    multipliers = jnp.zeros((N_GX, 3, NY, NZ), jnp.float32)
    for sweep_index in range(NPRE):
        velocity, multipliers = smooth_sweep(velocity, multipliers, force, weight, mortar)
    residual = force - operate(velocity, weight) - apply_transpose(multipliers, mortar)
    velocity = velocity + coarse_correct(residual, agg_map, coarse_matrix, coarse_diag)
    for sweep_index in range(NPOST):
        velocity, multipliers = smooth_sweep(velocity, multipliers, force, weight, mortar)
    return velocity, multipliers
```

```python
import functools

import jax
import jax.numpy as jnp
from jax import lax
from jax.experimental import pallas as pl
from jax.experimental.pallas import tpu as pltpu
from jax.sharding import PartitionSpec as P

BLK = 64
NAGG = 512
TAIL = 7
HEAD = 15
NP = TAIL + HEAD
NF = 3 * NP
LINES = 72
LOW = TAIL
UPP = TAIL - 1
RET = 4
COARSE_OMEGA = 0.8
PROLONG_GAIN = 0.5
F32 = jnp.float32
BF16 = jnp.bfloat16

VMEM = pl.BlockSpec(memory_space=pltpu.VMEM)
SMEM = pl.BlockSpec(memory_space=pltpu.SMEM)


def call(body, outs, scratch=(), n_smem=0, n_in=0, aliases=None, limit=40):
    return pl.pallas_call(
        body,
        out_shape=[jax.ShapeDtypeStruct(s, d) for s, d in outs],
        in_specs=[SMEM] * n_smem + [VMEM] * n_in,
        out_specs=[VMEM] * len(outs),
        scratch_shapes=list(scratch),
        input_output_aliases=aliases or {},
        compiler_params=pltpu.CompilerParams(vmem_limit_bytes=limit * 1024 * 1024),
    )


def prepare_kernel(blocks, by_col, by_row, piece):
    zero = jnp.zeros((8, 128), F32)

    def chunk(i, _):
        piece[...] = blocks[:, pl.ds(pl.multiple_of(i * 128, 128), 128)]
        for tile in range(2):
            rows = []
            for k in (2 * tile, 2 * tile + 1):
                for par in range(2):
                    rows += [piece[pl.ds(4 * par + k, 24, stride=8), :], zero]
            turned = jnp.concatenate(rows, 0).T
            for half in range(2):
                part = turned[64 * half : 64 * half + 64]
                by_row[tile, pl.ds(pl.multiple_of(i * 128 + 64 * half, 64), 64), :] = part
                by_col[tile, pl.ds(2 * i + half, 64, stride=64), :] = part
        return 0

    lax.fori_loop(0, 32, chunk, 0)


def weigh(matrices, rows, wide):
    def body(i, accs):
        first, second = accs
        at = pl.multiple_of(i * 64, 64)
        one = rows[0, pl.ds(i, 1), :]
        two = rows[1, pl.ds(i, 1), :] if wide else one
        first = first + matrices[0, pl.ds(at, 64), :] * one
        second = second + matrices[1, pl.ds(at, 64), :] * two
        return first, second

    zero = jnp.zeros((64, 128), F32)
    return lax.fori_loop(0, 64, body, (zero, zero), unroll=8)


def split(x):
    high = x.astype(BF16)
    return high, (x - high.astype(F32)).astype(BF16)


def project(by_col, spots, used, work, values):
    for tile in range(2):
        lanes = slice(128 * tile, 128 * tile + 128)
        for g in range(8):
            rows = slice(8 * g, 8 * g + 8)
            picked = jnp.take_along_axis(values[rows], spots[:, lanes], axis=1, mode="promise_in_bounds")
            work[tile, rows, :] = picked * used[:, lanes]
    first, second = weigh(by_col, work, True)
    total = first + second
    return total + pltpu.roll(total, 64, 1)


def project_back(by_row, place, work, values):
    work[0] = values
    first, second = weigh(by_row, work, False)
    high, low = split(jnp.concatenate([first, second], 1))
    both = lax.dot_general(
        jnp.concatenate([high, low], 0), place[...], (((1,), (1,)), ((), ())), preferred_element_type=F32
    )
    return both[0:64] + both[64:128]


def turn(lower, upper):
    left = lax.broadcasted_iota(jnp.int32, (24, 128), 1) < 64
    even = jnp.where(left, lower, pltpu.roll(upper, 64, 1))
    odd = jnp.where(left, pltpu.roll(lower, 64, 1), upper)
    zero = jnp.zeros((8, 128), F32)
    turned = jnp.concatenate([even, zero, odd, zero, even, zero, odd, zero], 0).T
    return turned[0:64], turned[64:128]


def turn_back(lower, upper):
    left = lax.broadcasted_iota(jnp.int32, (24, 128), 1) < 64
    rows = jnp.concatenate([lower, upper], 0).T
    even, odd = rows[0:24], rows[32:56]
    return (
        jnp.where(left, even, pltpu.roll(odd, 64, 1)),
        jnp.where(left, pltpu.roll(even, 64, 1), odd),
    )


def solve_interface(lower, upper, face, inverse, mortar, work):
    by_col, by_row, spots, used, place = mortar
    low_t, upp_t = turn(lower, upper)
    rhs = low_t - project(by_col, spots, used, work, upp_t)
    first = face * rhs
    back = project_back(by_row, place, work, first) * inverse
    rest = 0.6 * rhs - project(by_col, spots, used, work, back)
    increment = first + face * rest
    return turn_back(increment, project_back(by_row, place, work, increment))


def tall(plane):
    return jnp.concatenate([plane] * 3, 0)


class Halo:
    def __init__(self, flags, y_first, y_second, z_first, z_second):
        y_even, z_even = flags[0] == 1, flags[1] == 1
        self.y_low = jnp.where(y_even, y_second[...], y_first[...]) * flags[2].astype(F32)
        self.y_high = jnp.where(y_even, y_first[...], y_second[...]) * flags[3].astype(F32)
        self.z_low = jnp.where(z_even, z_second[0:8], z_first[0:8]) * flags[4].astype(F32)
        self.z_high = jnp.where(z_even, z_first[0:8], z_second[0:8]) * flags[5].astype(F32)


def residual_of(p, c, force, weight, velocity, halo):
    i = 3 * p + c
    sub = lax.broadcasted_iota(jnp.int32, (8, 128), 0)
    lane = lax.broadcasted_iota(jnp.int32, (8, 128), 1)
    v = velocity[p, c]
    total = force[p, c] - weight[p] * v
    if p not in (0, LOW):
        total = total + velocity[p - 1, c]
    if p not in (NP - 1, UPP):
        total = total + velocity[p + 1, c]
    total = total + jnp.where(sub == 0, halo.y_low[i : i + 1], pltpu.roll(v, 1, 0))
    total = total + jnp.where(sub == 7, halo.y_high[i : i + 1], pltpu.roll(v, 7, 0))
    total = total + jnp.where(lane == 0, pltpu.roll(halo.z_low, (128 - i) % 128, 1), pltpu.roll(v, 1, 1))
    total = total + jnp.where(lane == 127, pltpu.roll(halo.z_high, 127 - i, 1), pltpu.roll(v, 127, 1))
    return total


def write_lines(flags, get, y_first, y_second):
    y_even = flags[0] == 1
    for i in range(NF):
        v = get(i // 3, i % 3)
        top, bottom = v[0:1], v[7:8]
        y_first[i : i + 1] = jnp.where(y_even, bottom, top)
        y_second[i : i + 1] = jnp.where(y_even, top, bottom)
    rest = jnp.zeros((LINES - NF, 128), F32)
    y_first[NF:LINES] = rest
    y_second[NF:LINES] = rest


def columns(get):
    lane = lax.broadcasted_iota(jnp.int32, (8, 128), 1)
    first = jnp.zeros((8, 128), F32)
    last = first
    for i in range(NF):
        v = get(i // 3, i % 3)
        first = jnp.where(lane == i, pltpu.roll(v, i, 1) if i else v, first)
        last = jnp.where(lane == i, pltpu.roll(v, i + 1, 1), last)
    return first, last


def write_columns(flags, get, z_first, z_second, row=0):
    z_even = flags[1] == 1
    first, last = columns(get)
    z_first[row : row + 8] = jnp.where(z_even, last, first)
    z_second[row : row + 8] = jnp.where(z_even, first, last)


def first_sweep_kernel(
    flags, force_in, kappa_in, agg_in, tail, by_col, by_row, spots, used, place,
    force, weight, inverse, agg, velocity, mult, mult_up, face, inverse_t, y1, y2, z1, z2, work,
):
    for p in range(NP):
        here = p - TAIL
        kappa = tail[p, 3] if here < 0 else kappa_in[here]
        w = 6.0 + kappa
        weight[p] = w
        inverse[p] = 1.0 / (1.5 * w)
        agg[p] = tail[p, 4].astype(jnp.int32) if here < 0 else agg_in[here]
        for c in range(3):
            f = tail[p, c] if here < 0 else force_in[c, here]
            force[p, c] = f
            velocity[p, c] = f * inverse[p]
    low_w, upp_inv = turn(tall(weight[LOW]), tall(inverse[UPP]))
    face[...] = 0.6 * low_w
    inverse_t[...] = upp_inv
    lower = velocity[LOW].reshape(24, 128)
    upper = velocity[UPP].reshape(24, 128)
    increment, pulled = solve_interface(
        lower, upper, face[...], upp_inv, (by_col, by_row, spots, used, place), work
    )
    mult[...] = increment.reshape(3, 8, 128)
    mult_up[...] = pulled.reshape(3, 8, 128)
    velocity[LOW] = (lower - increment * tall(inverse[LOW])).reshape(3, 8, 128)
    velocity[UPP] = (upper + pulled * tall(inverse[UPP])).reshape(3, 8, 128)
    get = lambda p, c: velocity[p, c]
    write_lines(flags, get, y1, y2)
    write_columns(flags, get, z1, z2)
    write_columns(flags, lambda p, c: agg[p].astype(F32), z1, z2, 8)


def sweep(
    flags, force, weight, inverse, velocity, mult, mult_up, face, inverse_t, by_col, by_row, spots, used, place,
    halo, work, out, out_mult, out_up,
):
    def residuals(p):
        return jnp.concatenate([residual_of(p, c, force, weight, velocity, halo) for c in range(3)], 0)

    res_low = residuals(LOW) - mult[...].reshape(24, 128)
    res_upp = residuals(UPP) + mult_up[...].reshape(24, 128)
    inv_low, inv_upp = tall(inverse[LOW]), tall(inverse[UPP])
    lower = velocity[LOW].reshape(24, 128) + res_low * inv_low
    upper = velocity[UPP].reshape(24, 128) + res_upp * inv_upp
    increment, pulled = solve_interface(
        lower, upper, face[...], inverse_t[...], (by_col, by_row, spots, used, place), work
    )
    out_mult[...] = mult[...] + increment.reshape(3, 8, 128)
    out_up[...] = mult_up[...] + pulled.reshape(3, 8, 128)
    for p in range(NP):
        if p in (LOW, UPP):
            continue
        for c in range(3):
            out[p, c] = velocity[p, c] + residual_of(p, c, force, weight, velocity, halo) * inverse[p]
    out[LOW] = (lower - increment * inv_low).reshape(3, 8, 128)
    out[UPP] = (upper + pulled * inv_upp).reshape(3, 8, 128)


def second_sweep_kernel(
    flags, force, weight, inverse, velocity, mult, mult_up, face, inverse_t, by_col, by_row, spots, used, place,
    y1, y2, z1, z2, out, out_mult, out_up, oy1, oy2, oz1, oz2, work,
):
    halo = Halo(flags, y1, y2, z1, z2)
    sweep(
        flags, force, weight, inverse, velocity, mult, mult_up, face, inverse_t, by_col, by_row, spots, used, place,
        halo, work, out, out_mult, out_up,
    )
    get = lambda p, c: out[p, c]
    write_lines(flags, get, oy1, oy2)
    write_columns(flags, get, oz1, oz2)


def third_sweep_kernel(
    flags, force, weight, inverse, velocity, mult, mult_up, face, inverse_t, by_col, by_row, spots, used, place,
    y1, y2, z_low, z_high, out, out_mult, out_up, oy1, oy2, oz1, oz2, work,
):
    halo = Halo(flags, y1, y2, z_low, z_high)
    halo.z_low, halo.z_high = z_low[...], z_high[...]
    sweep(
        flags, force, weight, inverse, velocity, mult, mult_up, face, inverse_t, by_col, by_row, spots, used, place,
        halo, work, out, out_mult, out_up,
    )
    get = lambda p, c: out[p, c]
    write_lines(flags, get, oy1, oy2)
    write_columns(flags, get, oz1, oz2)


def last_sweep_kernel(
    flags, force, weight, inverse, velocity, mult, mult_up, face, inverse_t, by_col, by_row, spots, used, place,
    y1, y2, z1, z2, head, tail, out_mult, out, out_up, work,
):
    halo = Halo(flags, y1, y2, z1, z2)
    sweep(
        flags, force, weight, inverse, velocity, mult, mult_up, face, inverse_t, by_col, by_row, spots, used, place,
        halo, work, out, out_mult, out_up,
    )
    for c in range(3):
        for p in range(16 - RET):
            head[c, p] = out[LOW + p, c]
        for p in range(RET):
            tail[c, p] = out[TAIL - RET + p, c]


def restrict_kernel(
    flags, force, weight, velocity, mult, mult_up, agg, y1, y2, z1, z2, own, prev, res,
):
    halo = Halo(flags, y1, y2, z1, z2)
    for p in range(TAIL - 3, NP - 2):
        for c in range(3):
            r = residual_of(p, c, force, weight, velocity, halo)
            if p == LOW:
                r = r - mult[c]
            if p == UPP:
                r = r + mult_up[c]
            res[p, c] = r
    down = lax.broadcasted_iota(jnp.int32, (128, 128), 0)
    sub = lax.broadcasted_iota(jnp.int32, (8, 128), 0)

    def plane(p, total):
        labels = agg[p]
        lows = labels & 127
        highs = lax.shift_right_logical(labels, 7)
        values = []
        for c in range(3):
            r = res[p, c]
            high = r.astype(BF16).astype(F32)
            values.append((high, r - high))
        for pair in range(4):
            tables, terms = [], []
            for y in (2 * pair, 2 * pair + 1):
                tables.append(jnp.where(down == lows[y : y + 1], 1.0, 0.0).astype(BF16))
                here = highs[y : y + 1] == (sub & 3)
                rows = [
                    jnp.where(here, jnp.where(sub < 4, high[y : y + 1], low[y : y + 1]), 0.0)
                    for high, low in values
                ]
                terms.append(jnp.concatenate(rows, 0).astype(BF16))
            total = total + lax.dot_general(
                jnp.concatenate(terms, 1), jnp.concatenate(tables, 1), (((1,), (1,)), ((), ())),
                preferred_element_type=F32,
            )
        return total

    empty = jnp.zeros((24, 128), F32)
    prev[...] = lax.fori_loop(TAIL - 3, TAIL, plane, empty)
    own[...] = lax.fori_loop(LOW, NP - 2, plane, empty)


def split_matrix_kernel(rows, high, low, scale):
    for block in range(4):
        at = slice(block * 128, block * 128 + 128)
        a = rows[block, 0:128, :].T
        h = a.astype(BF16)
        high[:, at] = h
        low[:, at] = (a - h.astype(F32)).astype(BF16)
        scale[:, at] = jnp.broadcast_to(rows[block, 128:129, 0:128], (8, 128))


def solve_kernel(own, other, high, low, scale, out, rhs):
    total = own[...] + other[...]
    rhs[...] = jnp.zeros((8, NAGG), F32)
    for c in range(3):
        for h in range(4):
            at = 8 * c + h
            rhs[c : c + 1, 128 * h : 128 * h + 128] = total[at : at + 1] + total[at + 4 : at + 5]
    gain = (16 * 8 * 512 / NAGG) ** -0.5
    step = COARSE_OMEGA / scale[...]
    start = (rhs[...] * gain) * step
    x = start
    for _ in range(3):
        xh, xl = split(x)
        both = jnp.concatenate([xh, xl], 0)
        first = jnp.dot(both, high[...], preferred_element_type=F32)
        second = jnp.dot(xh, low[...], preferred_element_type=F32)
        product = first[0:8] + first[8:16] + second
        x = (1.0 - COARSE_OMEGA) * x + (start - step * product)
    out[...] = x


def spread_kernel(
    flags, velocity, agg, iterate, below, z1, z2, az1, az2, out, y1, y2, z_low, z_high,
):
    def table(ref):
        return [
            [jnp.broadcast_to(ref[c : c + 1, 128 * h : 128 * h + 128], (8, 128)) * PROLONG_GAIN for h in range(4)]
            for c in range(3)
        ]

    own, prev = table(iterate), table(below)

    def pick(rows, lows, highs):
        got = [jnp.take_along_axis(row, lows, axis=1, mode="promise_in_bounds") for row in rows]
        return jnp.where(
            highs < 2, jnp.where(highs == 0, got[0], got[1]), jnp.where(highs == 2, got[2], got[3])
        )

    for p in range(NP):
        lows = agg[p] & 127
        highs = lax.shift_right_logical(agg[p], 7)
        for c in range(3):
            out[p, c] = velocity[p, c] + pick((prev if p < TAIL else own)[c], lows, highs)
    write_lines(flags, lambda p, c: out[p, c], y1, y2)
    z_even = flags[1] == 1
    lane = lax.broadcasted_iota(jnp.int32, (8, 128), 1)
    comp = lax.rem(lane, 3)
    for side, (v_even, v_odd, a_even, a_odd, flag, dest) in enumerate(
        ((z2, z1, az2, az1, 4, z_low), (z1, z2, az1, az2, 5, z_high))
    ):
        values = jnp.where(z_even, v_even[0:8], v_odd[0:8])
        labels = jnp.where(z_even, a_even[8:16], a_odd[8:16]).astype(jnp.int32)
        lows = labels & 127
        highs = lax.shift_right_logical(labels, 7)
        extra = jnp.zeros((8, 128), F32)
        for c in range(3):
            got = jnp.where(lane < 3 * TAIL, pick(prev[c], lows, highs), pick(own[c], lows, highs))
            extra = jnp.where(comp == c, got, extra)
        dest[...] = (values + extra) * flags[flag].astype(F32)


def ring(axis, by):
    n = lax.axis_size(axis)
    return [(i, (i + by) % n) for i in range(n)]


def swaps(axis, first):
    n = lax.axis_size(axis)
    pairs = []
    for i in range(first, first + n, 2):
        a, b = i % n, (i + 1) % n
        pairs += [(a, b), (b, a)]
    return pairs


def trade(y1, y2, z1=None, z2=None):
    got = [lax.ppermute(y1, "gy", swaps("gy", 0))]
    if z1 is not None:
        got_z = [lax.ppermute(z1, "gz", swaps("gz", 0))]
    got.append(lax.ppermute(y2, "gy", swaps("gy", 1)))
    if z1 is not None:
        got_z.append(lax.ppermute(z2, "gz", swaps("gz", 1)))
        got = got + got_z
    return got


def shards(force, kappa, mortar_blocks, mortar_index, mortar_count, agg_map, coarse_matrix, coarse_diag):
    gy, gz = lax.axis_index("gy"), lax.axis_index("gz")
    ny, nz = lax.axis_size("gy"), lax.axis_size("gz")
    flags = jnp.stack(
        [gy % 2 == 0, gz % 2 == 0, gy > 0, gy < ny - 1, gz > 0, gz < nz - 1]
    ).astype(jnp.int32)
    start = force.shape[1] - TAIL
    tail_in = jnp.concatenate(
        [
            jnp.transpose(force[:, start:], (1, 0, 2, 3)),
            kappa[start:, None],
            agg_map[start:, None].astype(F32),
        ],
        1,
    )
    tail_in = lax.ppermute(tail_in, "gx", ring("gx", 1))

    index = mortar_index.reshape(24, 2, 4)
    count = mortar_count.reshape(24, 2, 1)
    spots = (index % 2) * 32 + index // 2
    used = (jnp.arange(4)[None, None, :] < count).astype(F32)

    def lanes(x):
        x = jnp.pad(jnp.transpose(x, (2, 1, 0)), ((0, 0), (0, 0), (0, 8)))
        return jnp.broadcast_to(x.reshape(1, 256), (8, 256))

    spots, used = lanes(spots), lanes(used)
    place = jnp.where(
        lax.broadcasted_iota(jnp.int32, (128, 256), 0) % 64 == spots[0:1], used[0:1], 0.0
    ).astype(BF16)
    by_col, by_row = call(
        prepare_kernel, [((2, 4096, 128), F32)] * 2, [pltpu.VMEM((192, 128), F32)], n_in=1
    )(mortar_blocks.reshape(192, 4096))
    mortar = (by_col, by_row, spots, used, place)

    rows = jnp.concatenate(
        [coarse_matrix[0, 0], jnp.pad(coarse_diag[0], ((0, 7), (0, NAGG - 128)))], 0
    )
    rows = lax.all_gather(rows, "gz")
    k_high, k_low, scale = call(
        split_matrix_kernel, [((NAGG, NAGG), BF16), ((NAGG, NAGG), BF16), ((8, NAGG), F32)], n_in=1
    )(rows)

    field = ((NP, 3, 8, 128), F32)
    plane = ((3, 8, 128), F32)
    y_msg, z_msg = ((LINES, 128), F32), ((8, 128), F32)
    work = [pltpu.VMEM((2, 64, 128), F32)]
    out = call(
        first_sweep_kernel,
        [field, ((NP, 8, 128), F32), ((NP, 8, 128), F32), ((NP, 8, 128), jnp.int32), field, plane, plane,
         ((64, 128), F32), ((64, 128), F32), y_msg, y_msg, ((16, 128), F32), ((16, 128), F32)],
        work, 1, 9,
    )(flags, force, kappa, agg_map, tail_in, *mortar)
    force_e, weight, inverse, agg, velocity, mult, mult_up, face, inverse_t = out[:9]
    got = trade(*out[9:])
    az1, az2 = got[2], got[3]
    velocity, mult, mult_up, *msgs = call(
        second_sweep_kernel, [field, plane, plane, y_msg, y_msg, z_msg, z_msg], work, 1, 17
    )(flags, force_e, weight, inverse, velocity, mult, mult_up, face, inverse_t, *mortar, *got)
    got = trade(*msgs)
    own, prev = call(
        restrict_kernel, [((24, 128), F32)] * 2, [pltpu.VMEM((NP, 3, 8, 128), F32)], 1, 10
    )(flags, force_e, weight, velocity, mult, mult_up, agg, *got)
    total = own + lax.ppermute(prev, "gx", ring("gx", -1))
    total = total + lax.ppermute(total, "gz", swaps("gz", 0))
    other = lax.ppermute(total, "gz", ring("gz", 2))
    iterate = call(solve_kernel, [((8, NAGG), F32)], [pltpu.VMEM((8, NAGG), F32)], 0, 5)(
        total, other, k_high, k_low, scale
    )[0]
    below = lax.ppermute(iterate, "gx", ring("gx", 1))
    velocity, y1, y2, z_low, z_high = call(
        spread_kernel, [field, y_msg, y_msg, z_msg, z_msg], (), 1, 8
    )(flags, velocity, agg, iterate, below, got[2], got[3], az1, az2)
    got = trade(y1, y2)
    velocity, mult, mult_up, *msgs = call(
        third_sweep_kernel, [field, plane, plane, y_msg, y_msg, z_msg, z_msg], work, 1, 17
    )(flags, force_e, weight, inverse, velocity, mult, mult_up, face, inverse_t, *mortar, *got, z_low, z_high)
    got = trade(*msgs)
    head, tail, mult = call(
        last_sweep_kernel, [((3, 16 - RET, 8, 128), F32), ((3, RET, 8, 128), F32), plane],
        [pltpu.VMEM((NP, 3, 8, 128), F32), pltpu.VMEM((3, 8, 128), F32)] + work, 1, 17
    )(flags, force_e, weight, inverse, velocity, mult, mult_up, face, inverse_t, *mortar, *got)
    tail = lax.ppermute(tail, "gx", ring("gx", -1))
    return jnp.concatenate([head, tail], 1), mult[None]


def solution(mesh):
    in_specs = (
        P(None, "gx", "gy", "gz"),
        P("gx", "gy", "gz"),
        P("gx", "gy", "gz", None, None),
        P("gx", "gy", "gz", None, None),
        P("gx", "gy", "gz", None),
        P("gx", "gy", "gz"),
        P("gx", "gy", "gz", None),
        P("gx", "gy", "gz"),
    )
    out_specs = (P(None, "gx", "gy", "gz"), P("gx", None, "gy", "gz"))
    return jax.shard_map(shards, mesh=mesh, in_specs=in_specs, out_specs=out_specs, check_vma=False)
```

```python
import functools

import jax
import jax.numpy as jnp
from jax import lax
from jax.experimental import pallas as pl
from jax.experimental.pallas import tpu as pltpu
from jax.sharding import PartitionSpec as P

BLK = 64
NAGG = 512
TAIL = 7
HEAD = 15
NP = TAIL + HEAD
ROWS = 24
LINES = 3 * ROWS
LOW = TAIL
UPP = TAIL - 1
RET = 4
COARSE_OMEGA = 0.8
PROLONG_GAIN = 0.5
F32 = jnp.float32
BF16 = jnp.bfloat16

VMEM = pl.BlockSpec(memory_space=pltpu.VMEM)
SMEM = pl.BlockSpec(memory_space=pltpu.SMEM)
HBM = pl.BlockSpec(memory_space=pltpu.HBM)


def keep(x):
    return pltpu.with_memory_space_constraint(x, pltpu.VMEM)


def call(body, outs, scratch=(), n_smem=0, n_in=0, n_far=0, limit=12, results=()):
    kernel = pl.pallas_call(
        body,
        out_shape=[jax.ShapeDtypeStruct(s, d) if i in results else pltpu.VMEM(s, d) for i, (s, d) in enumerate(outs)],
        in_specs=[SMEM] * n_smem + [VMEM] * n_in + [HBM] * n_far,
        out_specs=[VMEM] * len(outs),
        scratch_shapes=list(scratch),
        compiler_params=pltpu.CompilerParams(vmem_limit_bytes=limit * 1024 * 1024),
    )

    def run(*args):
        near = n_smem + n_in
        far = [pltpu.with_memory_space_constraint(x, pltpu.HBM) for x in args[near:]]
        held = [keep(x) for x in args[n_smem:near]]
        return kernel(*args[:n_smem], *held, *far)

    return run


def prepare_kernel(flags, blocks, index, count, by_row, spots, place, near, piece, lists, index_near, count_near, sems):
    copies = [
        pltpu.make_async_copy(blocks.at[:, pl.ds(1024 * i, 1024)], near.at[i], sems.at[i]) for i in range(4)
    ]
    for copy in copies:
        copy.start()
    zero = jnp.zeros((8, 128), F32)
    lane = lax.broadcasted_iota(jnp.int32, (8, 128), 1)
    spot = lane & 31
    source = jnp.where(spot < 24, 2 * spot + (lax.shift_right_logical(lane, 5) & 1), 0)
    lists[...] = jnp.zeros((8, 128), jnp.int32)
    small = [
        pltpu.make_async_copy(index, index_near, sems.at[4]),
        pltpu.make_async_copy(count, count_near, sems.at[5]),
    ]
    for copy in small:
        copy.start()
    for copy in small:
        copy.wait()
    lists[0:4, 0:48] = index_near[...]
    lists[4:5, 0:48] = count_near[...]

    def pick(row):
        full = jnp.broadcast_to(lists[row : row + 1, :], (8, 128))
        return jnp.take_along_axis(full, source, axis=1, mode="promise_in_bounds")

    used = pick(4)
    down = lax.broadcasted_iota(jnp.int32, (128, 128), 0) & 63
    for tile in range(2):
        k = 2 * tile + lax.shift_right_logical(lane, 6)
        block = jnp.where(lane < 64, pick(2 * tile), pick(2 * tile + 1))
        at = (block & 1) * 32 + lax.shift_right_logical(block, 1)
        live = (k < used) & (spot < 24)
        at = jnp.where(live, at, 31)
        spots[:, 128 * tile : 128 * tile + 128] = at
        hit = (down == at[0:1]) & (at[0:1] != 31)
        place[:, 128 * tile : 128 * tile + 128] = jnp.where(hit, 1.0, 0.0).astype(BF16)

    for i, copy in enumerate(copies):
        copy.wait()

        def chunk(g, _):
            for s in range(2):
                at = pl.multiple_of((2 * g + s) * 128, 128)
                piece[s] = near[i, :, pl.ds(at, 128)]
                for tile in range(2):
                    rows = []
                    for k in (2 * tile, 2 * tile + 1):
                        for par in range(2):
                            rows += [piece[s, pl.ds(4 * par + k, 24, stride=8), :], zero]
                    by_row[tile, pl.ds(1024 * i + at, 128), :] = jnp.concatenate(rows, 0).T
            return 0

        lax.fori_loop(0, 4, chunk, 0)


def split(x):
    high = x.astype(BF16)
    return high, (x - high.astype(F32)).astype(BF16)


def fold(parts):
    sub = lax.broadcasted_iota(jnp.int32, (8, 128), 0)
    m = sub < 4
    a = [
        jnp.where(m, parts[i], parts[i + 4]) + pltpu.roll(jnp.where(m, parts[i + 4], parts[i]), 4, 0)
        for i in range(4)
    ]
    m = (sub & 2) == 0
    a = [
        jnp.where(m, a[i], pltpu.roll(a[i + 2], 2, 0)) + jnp.where(m, pltpu.roll(a[i], 6, 0), a[i + 2])
        for i in range(2)
    ]
    m = (sub & 1) == 0
    return jnp.where(m, a[0], pltpu.roll(a[1], 1, 0)) + jnp.where(m, pltpu.roll(a[0], 7, 0), a[1])


def project(by_row, spots, values):
    total = None
    for tile in range(2):
        picked = [
            jnp.take_along_axis(
                values[8 * g : 8 * g + 8], spots[:, 128 * tile : 128 * tile + 128], axis=1,
                mode="promise_in_bounds",
            )
            for g in range(8)
        ]
        rows = []
        for group in range(8):
            parts = []
            for s in range(8):
                base = 64 * (8 * group + s)
                terms = [by_row[tile, base + 8 * g : base + 8 * g + 8, :] * picked[g] for g in range(8)]
                while len(terms) > 1:
                    terms = [terms[i] + terms[i + 1] for i in range(0, len(terms), 2)]
                parts.append(terms[0])
            rows.append(fold(parts))
        part = jnp.concatenate(rows, 0)
        total = part if total is None else total + part
    return total + pltpu.roll(total, 64, 1)


def project_back(by_row, place, values):
    first = second = jnp.zeros((64, 128), F32)
    for i in range(64):
        row = jnp.broadcast_to(values[i : i + 1], (64, 128))
        first = first + by_row[0, 64 * i : 64 * i + 64, :] * row
        second = second + by_row[1, 64 * i : 64 * i + 64, :] * row
    high, low = split(jnp.concatenate([first, second], 1))
    both = lax.dot_general(
        jnp.concatenate([high, low], 0), place[...], (((1,), (1,)), ((), ())), preferred_element_type=F32
    )
    return both[0:64] + both[64:128]


def turn(lower, upper):
    left = lax.broadcasted_iota(jnp.int32, (24, 128), 1) < 64
    even = jnp.where(left, lower, pltpu.roll(upper, 64, 1))
    odd = jnp.where(left, pltpu.roll(lower, 64, 1), upper)
    zero = jnp.zeros((8, 128), F32)
    turned = jnp.concatenate([even, zero, odd, zero, even, zero, odd, zero], 0).T
    return turned[0:64], turned[64:128]


def turn_back(lower, upper):
    left = lax.broadcasted_iota(jnp.int32, (24, 128), 1) < 64
    rows = jnp.concatenate([lower, upper], 0).T
    even, odd = rows[0:24], rows[32:56]
    return (
        jnp.where(left, even, pltpu.roll(odd, 64, 1)),
        jnp.where(left, pltpu.roll(even, 64, 1), odd),
    )


def solve_interface(lower, upper, face, inverse, mortar):
    by_row, spots, place = mortar
    low_t, upp_t = turn(lower, upper)
    rhs = low_t - project(by_row, spots, upp_t)
    first = face * rhs
    back = project_back(by_row, place, first) * inverse
    rest = 0.6 * rhs - project(by_row, spots, back)
    increment = first + face * rest
    return turn_back(increment, project_back(by_row, place, increment))


def tall(plane):
    return jnp.concatenate([plane] * 3, 0)


def yes(flags, row, shape):
    line = jnp.concatenate([flags[row : row + 1, :]] * (shape[1] // 128), 1)
    return jnp.broadcast_to(line, shape) == 1


def sides(flags, y_first, y_second, z_first, z_second):
    tall_shape, zero = (LINES, 128), jnp.zeros((LINES, 128), F32)
    y_even, z_even = yes(flags, 0, tall_shape), yes(flags, 1, (8, 128))
    a, b, c, d = y_first[0:LINES], y_second[0:LINES], z_first[0:8], z_second[0:8]
    return (
        jnp.where(yes(flags, 2, tall_shape), jnp.where(y_even, b, a), zero),
        jnp.where(yes(flags, 3, tall_shape), jnp.where(y_even, a, b), zero),
        jnp.where(yes(flags, 4, (8, 128)), jnp.where(z_even, d, c), zero[0:8]),
        jnp.where(yes(flags, 5, (8, 128)), jnp.where(z_even, c, d), zero[0:8]),
    )


def place_of(p, c):
    return ROWS * c + p


def residual_of(p, c, force, weight, velocity, halo):
    y_low, y_high, z_low, z_high = halo
    i = place_of(p, c)
    sub = lax.broadcasted_iota(jnp.int32, (8, 128), 0)
    lane = lax.broadcasted_iota(jnp.int32, (8, 128), 1)
    v = velocity[p, c]
    total = force[p, c] - weight[p] * v
    if p not in (0, LOW):
        total = total + velocity[p - 1, c]
    if p not in (NP - 1, UPP):
        total = total + velocity[p + 1, c]
    total = total + jnp.where(sub == 0, y_low[i : i + 1], pltpu.roll(v, 1, 0))
    total = total + jnp.where(sub == 7, y_high[i : i + 1], pltpu.roll(v, 7, 0))
    total = total + jnp.where(lane == 0, pltpu.roll(z_low, (128 - i) % 128, 1), pltpu.roll(v, 1, 1))
    total = total + jnp.where(lane == 127, pltpu.roll(z_high, 127 - i, 1), pltpu.roll(v, 127, 1))
    return total


def write_lines(flags, get, y_first, y_second, row=0, count=3):
    y_even = yes(flags, 0, (1, 128))
    for c in range(count):
        for p in range(NP):
            v = get(p, c)
            i = row + place_of(p, c)
            y_first[i : i + 1] = jnp.where(y_even, v[7:8], v[0:1])
            y_second[i : i + 1] = jnp.where(y_even, v[0:1], v[7:8])
        i = row + place_of(NP, c)
        y_first[i : i + ROWS - NP] = jnp.zeros((ROWS - NP, 128), F32)
        y_second[i : i + ROWS - NP] = jnp.zeros((ROWS - NP, 128), F32)


def write_columns(flags, get, z_first, z_second, row=0):
    z_even = yes(flags, 1, (8, 128))
    lane = lax.broadcasted_iota(jnp.int32, (8, 128), 1)
    first = jnp.zeros((8, 128), F32)
    last = first
    for c in range(3):
        for p in range(NP):
            v, i = get(p, c), place_of(p, c)
            first = jnp.where(lane == i, pltpu.roll(v, i, 1) if i else v, first)
            last = jnp.where(lane == i, pltpu.roll(v, i + 1, 1), last)
    z_first[row : row + 8] = jnp.where(z_even, last, first)
    z_second[row : row + 8] = jnp.where(z_even, first, last)


def first_sweep_kernel(
    flags, force_in, kappa_in, agg_in, tail, by_row, spots, place,
    force, weight, inverse, agg, velocity, mult, mult_up, face, inverse_t, y1, y2, z1, z2,
):
    for p in range(NP):
        here = p - TAIL
        kappa = tail[p, 3] if here < 0 else kappa_in[here]
        w = 6.0 + kappa
        weight[p] = w
        inverse[p] = 1.0 / (1.5 * w)
        agg[p] = tail[p, 4].astype(jnp.int32) if here < 0 else agg_in[here]
        for c in range(3):
            f = tail[p, c] if here < 0 else force_in[c, here]
            force[p, c] = f
            velocity[p, c] = f * inverse[p]
    low_w, upp_inv = turn(tall(weight[LOW]), tall(inverse[UPP]))
    face[...] = 0.6 * low_w
    inverse_t[...] = upp_inv
    lower = velocity[LOW].reshape(24, 128)
    upper = velocity[UPP].reshape(24, 128)
    increment, pulled = solve_interface(
        lower, upper, face[...], upp_inv, (by_row, spots, place)
    )
    mult[...] = increment.reshape(3, 8, 128)
    mult_up[...] = pulled.reshape(3, 8, 128)
    velocity[LOW] = (lower - increment * tall(inverse[LOW])).reshape(3, 8, 128)
    velocity[UPP] = (upper + pulled * tall(inverse[UPP])).reshape(3, 8, 128)
    get = lambda p, c: velocity[p, c]
    write_lines(flags, get, y1, y2)
    write_columns(flags, get, z1, z2)
    label = lambda p, c: agg[p].astype(F32)
    write_lines(flags, label, y1, y2, LINES, 1)
    write_columns(flags, label, z1, z2, 8)


def sweep(
    flags, force, weight, inverse, velocity, mult, mult_up, face, inverse_t, by_row, spots, place,
    halo, out, out_mult, out_up,
):
    def residuals(p):
        return jnp.concatenate([residual_of(p, c, force, weight, velocity, halo) for c in range(3)], 0)

    res_low = residuals(LOW) - mult[...].reshape(24, 128)
    res_upp = residuals(UPP) + mult_up[...].reshape(24, 128)
    inv_low, inv_upp = tall(inverse[LOW]), tall(inverse[UPP])
    lower = velocity[LOW].reshape(24, 128) + res_low * inv_low
    upper = velocity[UPP].reshape(24, 128) + res_upp * inv_upp
    increment, pulled = solve_interface(
        lower, upper, face[...], inverse_t[...], (by_row, spots, place)
    )
    out_mult[...] = mult[...] + increment.reshape(3, 8, 128)
    out_up[...] = mult_up[...] + pulled.reshape(3, 8, 128)
    for p in range(NP):
        if p in (LOW, UPP):
            continue
        for c in range(3):
            out[p, c] = velocity[p, c] + residual_of(p, c, force, weight, velocity, halo) * inverse[p]
    out[LOW] = (lower - increment * inv_low).reshape(3, 8, 128)
    out[UPP] = (upper + pulled * inv_upp).reshape(3, 8, 128)


def second_sweep_kernel(
    flags, force, weight, inverse, velocity, mult, mult_up, face, inverse_t, by_row, spots, place,
    y1, y2, z1, z2, out, out_mult, out_up, oy1, oy2, oz1, oz2,
):
    halo = sides(flags, y1, y2, z1, z2)
    sweep(
        flags, force, weight, inverse, velocity, mult, mult_up, face, inverse_t, by_row, spots, place,
        halo, out, out_mult, out_up,
    )
    get = lambda p, c: out[p, c]
    write_lines(flags, get, oy1, oy2)
    write_columns(flags, get, oz1, oz2)


def third_sweep_kernel(
    flags, force, weight, inverse, old, mult, mult_up, face, inverse_t, by_row, spots, place,
    y1, y2, z1, z2, ay1, ay2, az1, az2, agg, iterate, got, swapped,
    out, out_mult, out_up, oy1, oy2, oz1, oz2, velocity,
):
    core_zero = yes(flags, 1, (24, NAGG))
    a = jnp.where(core_zero, got[...], swapped[...])
    b = jnp.where(core_zero, swapped[...], got[...])
    own, prev = table(iterate[...]), table(a[0:8])
    low, low_prev = table(b[0:8]), table(b[8:16])
    high, high_prev = table(a[8:16]), table(a[16:24])
    for p in range(NP):
        at = where_in(agg[p])
        for c in range(3):
            velocity[p, c] = old[p, c] + pick((prev if p < TAIL else own)[c], at)

    y_low, y_high, z_low, z_high = sides(flags, y1, y2, z1, z2)
    y_even, z_even = yes(flags, 0, (ROWS, 128)), yes(flags, 1, (8, 128))
    ay1, ay2, az1, az2 = ay1[LINES : LINES + ROWS], ay2[LINES : LINES + ROWS], az1[8:16], az2[8:16]
    sub = lax.broadcasted_iota(jnp.int32, (8, 128), 0)
    lane = lax.broadcasted_iota(jnp.int32, (8, 128), 1)

    def lines(values, labels, mine, below, flag):
        labels = labels.astype(jnp.int32)
        parts = []
        for c in range(3):
            for block in range(ROWS // 8):
                at = where_in(labels[8 * block : 8 * block + 8])
                extra = pick(mine[c], at)
                if block == 0:
                    extra = jnp.where(sub < TAIL, pick(below[c], at), extra)
                row = place_of(8 * block, c)
                parts.append(jnp.where(yes(flags, flag, (8, 128)), values[row : row + 8] + extra, 0.0))
        return jnp.concatenate(parts, 0)

    def column(values, labels, flag):
        at = where_in(labels.astype(jnp.int32))
        extra = jnp.zeros((8, 128), F32)
        for c in range(3):
            here = lane - ROWS * c
            extra = jnp.where((here >= 0) & (here < TAIL), pick(prev[c], at), extra)
            extra = jnp.where((here >= TAIL) & (here < NP), pick(own[c], at), extra)
        return jnp.where(yes(flags, flag, (8, 128)), values + extra, 0.0)

    halo = (
        lines(y_low, jnp.where(y_even, ay2, ay1), low, low_prev, 2),
        lines(y_high, jnp.where(y_even, ay1, ay2), high, high_prev, 3),
        column(z_low, jnp.where(z_even, az2, az1), 4),
        column(z_high, jnp.where(z_even, az1, az2), 5),
    )
    sweep(
        flags, force, weight, inverse, velocity, mult, mult_up, face, inverse_t, by_row, spots, place,
        halo, out, out_mult, out_up,
    )
    get = lambda p, c: out[p, c]
    write_lines(flags, get, oy1, oy2)
    write_columns(flags, get, oz1, oz2)


def last_sweep_kernel(
    flags, force, weight, inverse, velocity, mult, mult_up, face, inverse_t, by_row, spots, place,
    y1, y2, z1, z2, head, tail, out_mult, out, out_up,
):
    halo = sides(flags, y1, y2, z1, z2)
    sweep(
        flags, force, weight, inverse, velocity, mult, mult_up, face, inverse_t, by_row, spots, place,
        halo, out, out_mult, out_up,
    )
    for c in range(3):
        for p in range(16 - RET):
            head[c, p] = out[LOW + p, c]
        for p in range(RET):
            tail[c, p] = out[TAIL - RET + p, c]


def restrict_kernel(
    flags, force, weight, velocity, mult, mult_up, agg, diag, y1, y2, z1, z2, out, res,
):
    halo = sides(flags, y1, y2, z1, z2)
    for p in range(TAIL - 3, NP - 2):
        for c in range(3):
            r = residual_of(p, c, force, weight, velocity, halo)
            if p == LOW:
                r = r - mult[c]
            if p == UPP:
                r = r + mult_up[c]
            res[p, c] = r
    down = lax.broadcasted_iota(jnp.int32, (64, 128), 0)
    sub = lax.broadcasted_iota(jnp.int32, (8, 128), 0)

    def plane(p, total):
        labels = agg[p]
        lows = labels & 63
        highs = lax.shift_right_logical(labels, 6)
        values = []
        for c in range(3):
            r = res[p, c]
            high = r.astype(BF16).astype(F32)
            values += [high, r - high]
        for pair in range(4):
            tables, terms = [], []
            for y in (2 * pair, 2 * pair + 1):
                tables.append(jnp.where(down == lows[y : y + 1], 1.0, 0.0).astype(BF16))
                here = highs[y : y + 1] == sub
                terms.append(jnp.concatenate([jnp.where(here, v[y : y + 1], 0.0) for v in values], 0).astype(BF16))
            total = total + lax.dot_general(
                jnp.concatenate(tables, 1), jnp.concatenate(terms, 1), (((1,), (1,)), ((), ())),
                preferred_element_type=F32,
            )
        return total

    def four(i, total):
        for s in range(4):
            total = plane(LOW + 4 * i + s, total)
        return total

    below = jnp.zeros((64, 48), F32)
    for p in range(TAIL - 3, TAIL):
        below = plane(p, below)
    own = lax.fori_loop(0, 3, four, plane(NP - 3, jnp.zeros((64, 48), F32)))
    both = jnp.concatenate([own, below], 0)
    turned = jnp.concatenate([both, jnp.zeros((128, 80), F32)], 1).T
    for c in range(3):
        out[8 * c : 8 * c + 8] = turned[16 * c : 16 * c + 8] + turned[16 * c + 8 : 16 * c + 16]
    out[24:32] = jnp.where(sub == flags[6:7], jnp.broadcast_to(diag[...], (8, 128)), 0.0)


def gather_sums_kernel(flags, mine, first, second, kept, passed):
    core_zero = yes(flags, 1, (32, 128))
    across = jnp.where(core_zero, first[...], second[...])
    above = jnp.where(core_zero, second[...], first[...])
    kept[...] = mine[...] + across
    lane = lax.broadcasted_iota(jnp.int32, (24, 128), 1)
    passed[...] = jnp.where(lane < 64, pltpu.roll(above[0:24], 64, 1), 0.0)


def add_kernel(one, two, out):
    out[...] = one[...] + two[...]


def join_kernel(a, b, c, after, out):
    out[0:8], out[8:16], out[16:24] = a[...], b[...], c[...]


def add(one, two):
    return call(add_kernel, [(one.shape, F32)], n_in=2)(one, two)[0]


def pack_kernel(force, kappa, agg, out, force_near, kappa_near, agg_near, flags, sems):
    copies = [
        pltpu.make_async_copy(far, near, sems.at[i])
        for i, (far, near) in enumerate(((force, force_near), (kappa, kappa_near), (agg, agg_near)))
    ]
    for copy in copies:
        copy.start()
    gy, gz = lax.axis_index("gy"), lax.axis_index("gz")
    ny, nz = lax.axis_size("gy"), lax.axis_size("gz")
    facts = (gy % 2 == 0, gz % 2 == 0, gy > 0, gy < ny - 1, gz > 0, gz < nz - 1, gz, gz)
    for row, fact in enumerate(facts):
        flags[row : row + 1, :] = jnp.full((1, 128), fact.astype(jnp.int32), jnp.int32)
    for copy in copies:
        copy.wait()
    start = kappa.shape[0] - TAIL
    for p in range(TAIL):
        for c in range(3):
            out[p, c] = force_near[c, start + p]
        out[p, 3] = kappa_near[start + p]
        out[p, 4] = agg_near[start + p].astype(F32)


def split_matrix_kernel(rows, high, low):
    a = rows[...].T
    h = a.astype(BF16)
    high[...] = h
    low[...] = (a - h.astype(F32)).astype(BF16)


def solve_kernel(kept, passed, swapped, high, low, out, rhs):
    sums = kept[0:24] + passed[...] + swapped[...]
    other = pltpu.roll(sums, 64, 1)
    rhs[...] = jnp.zeros((8, NAGG), F32)
    left = lax.broadcasted_iota(jnp.int32, (1, 128), 1) < 64
    for c in range(3):
        for t in range(4):
            at = 8 * c + 2 * t
            rhs[c : c + 1, 128 * t : 128 * t + 128] = jnp.where(left, sums[at : at + 1], other[at + 1 : at + 2])
    gain = (16 * 8 * 512 / NAGG) ** -0.5
    scale = jnp.concatenate([kept[24 + b : 25 + b] for b in range(4)], 1)
    step = jnp.broadcast_to(COARSE_OMEGA / scale, (8, NAGG))
    start = (rhs[...] * gain) * step
    x = start
    for _ in range(3):
        xh, xl = split(x)
        both = jnp.concatenate([xh, xl], 0)
        first = jnp.dot(both, high[...], preferred_element_type=F32)
        second = jnp.dot(xh, low[...], preferred_element_type=F32)
        product = first[0:8] + first[8:16] + second
        x = (1.0 - COARSE_OMEGA) * x + (start - step * product)
    out[...] = x


def table(rows):
    return [
        [jnp.broadcast_to(rows[c : c + 1, 128 * t : 128 * t + 128], (8, 128)) * PROLONG_GAIN for t in range(4)]
        for c in range(3)
    ]


def where_in(labels):
    return labels & 127, lax.shift_right_logical(labels, 7)


def pick(rows, at):
    lane, tile = at
    got = [jnp.take_along_axis(row, lane, axis=1, mode="promise_in_bounds") for row in rows]
    return jnp.where(tile < 2, jnp.where(tile == 0, got[0], got[1]), jnp.where(tile == 2, got[2], got[3]))


def reload_kernel(after, far, near, sem):
    copy = pltpu.make_async_copy(far, near, sem)
    copy.start()
    copy.wait()


def ring(axis, by):
    n = lax.axis_size(axis)
    return [(i, (i + by) % n) for i in range(n)]


def swaps(axis, first):
    n = lax.axis_size(axis)
    pairs = []
    for i in range(first, first + n, 2):
        a, b = i % n, (i + 1) % n
        pairs += [(a, b), (b, a)]
    return pairs


def trade(y1, y2, z1, z2):
    got_z = lax.ppermute(z2, "gz", swaps("gz", 1))
    got = [lax.ppermute(y1, "gy", swaps("gy", 0)), lax.ppermute(y2, "gy", swaps("gy", 1))]
    return got + [lax.ppermute(z1, "gz", swaps("gz", 0)), got_z]


def by_core(x, rule_zero, rule_one):
    nx, ny, nz = lax.axis_size("gx"), lax.axis_size("gy"), lax.axis_size("gz")
    pairs = []
    for g in range(nx):
        for y in range(ny):
            for z in range(nz):
                dx, dy, dz = rule_one if z % 2 else rule_zero
                to = (((g + dx) % nx) * ny + (y + dy) % ny) * nz + (z + dz) % nz
                pairs.append(((g * ny + y) * nz + z, to))
    return lax.ppermute(x, ("gx", "gy", "gz"), pairs)


def shards(force, kappa, mortar_blocks, mortar_index, mortar_count, agg_map, coarse_matrix, coarse_diag):
    tail_in, force, kappa, agg_map, flags = call(
        pack_kernel,
        [((TAIL, 5, 8, 128), F32), (force.shape, F32), (kappa.shape, F32), (agg_map.shape, jnp.int32),
         ((8, 128), jnp.int32)],
        [pltpu.SemaphoreType.DMA((3,))],
        n_far=3,
    )(force, kappa, agg_map)
    rows, flags = lax.optimization_barrier((coarse_matrix.reshape(128, NAGG), flags))
    rows = lax.all_gather(rows, "gz", tiled=True)
    tail_in = lax.ppermute(tail_in, "gx", ring("gx", 1))

    by_row, spots, place = call(
        prepare_kernel,
        [((2, 4096, 128), F32), ((8, 256), jnp.int32), ((128, 256), BF16)],
        [pltpu.VMEM((4, 192, 1024), F32), pltpu.VMEM((2, 192, 128), F32), pltpu.VMEM((8, 128), jnp.int32),
         pltpu.VMEM((4, 48), jnp.int32), pltpu.VMEM((1, 48), jnp.int32), pltpu.SemaphoreType.DMA((6,))],
        n_in=1,
        n_far=3,
    )(
        flags,
        mortar_blocks.reshape(192, 4096),
        jnp.transpose(mortar_index.reshape(48, 4), (1, 0)),
        mortar_count.reshape(1, 48),
    )

    k_high, k_low = call(split_matrix_kernel, [((NAGG, NAGG), BF16)] * 2, n_in=1)(rows)
    by_row_again = call(
        reload_kernel, [((2, 4096, 128), F32)], [pltpu.SemaphoreType.DMA], n_in=1, n_far=1
    )(k_high, by_row)[0]

    field = ((NP, 3, 8, 128), F32)
    plane = ((3, 8, 128), F32)
    turned = ((64, 128), F32)
    y_msg, z_msg = ((LINES, 128), F32), ((8, 128), F32)
    y_more, z_more = ((LINES + ROWS, 128), F32), ((16, 128), F32)
    out = call(
        first_sweep_kernel,
        [field, ((NP, 8, 128), F32), ((NP, 8, 128), F32), ((NP, 8, 128), jnp.int32), field, plane, plane,
         turned, turned, y_more, y_more, z_more, z_more],
        n_in=8,
    )(flags, force, kappa, agg_map, tail_in, by_row, spots, place)
    force_e, weight, inverse, agg, velocity, mult, mult_up, face, inverse_t = out[:9]
    labels = trade(*out[9:])
    velocity, mult, mult_up, *msgs = call(
        second_sweep_kernel, [field, plane, plane, y_msg, y_msg, z_msg, z_msg], n_in=16
    )(flags, force_e, weight, inverse, velocity, mult, mult_up, face, inverse_t, by_row, spots, place, *labels)
    edges = trade(*msgs)
    sums = call(
        restrict_kernel, [((32, 128), F32)], [pltpu.VMEM((NP, 3, 8, 128), F32)], n_in=12
    )(flags, force_e, weight, velocity, mult, mult_up, agg, coarse_diag.reshape(1, 128), *edges)[0]
    sums = add(sums, lax.ppermute(sums, "gz", swaps("gz", 0)))
    first = by_core(sums, (0, 0, 2), (-1, 0, 0))
    second = by_core(sums, (-1, 0, 2), (0, 0, 2))
    kept, passed = call(gather_sums_kernel, [((32, 128), F32), ((24, 128), F32)], n_in=4)(flags, sums, first, second)
    swapped = lax.ppermute(passed, "gz", swaps("gz", 0))
    iterate = call(solve_kernel, [((8, NAGG), F32)], [pltpu.VMEM((8, NAGG), F32)], n_in=5)(
        kept, passed, swapped, k_high, k_low
    )[0]
    got = [
        by_core(iterate, (1, 0, 0), (0, 1, 0)),
        by_core(iterate, (0, -1, 0), (1, 1, 0)),
        by_core(iterate, (1, -1, 0), (1, 0, 0)),
    ]
    got = call(join_kernel, [((24, NAGG), F32)], n_in=4)(*got, by_row_again)[0]
    swapped = lax.ppermute(got, "gz", swaps("gz", 0))
    velocity, mult, mult_up, *msgs = call(
        third_sweep_kernel, [field, plane, plane, y_msg, y_msg, z_msg, z_msg],
        [pltpu.VMEM((NP, 3, 8, 128), F32)], n_in=24,
    )(
        flags, force_e, weight, inverse, velocity, mult, mult_up, face, inverse_t, by_row_again, spots, place,
        *edges, *labels, agg, iterate, got, swapped,
    )
    edges = trade(*msgs)
    head, tail, mult = call(
        last_sweep_kernel, [((3, 16 - RET, 8, 128), F32), ((3, RET, 8, 128), F32), plane],
        [pltpu.VMEM((NP, 3, 8, 128), F32), pltpu.VMEM((3, 8, 128), F32)], n_in=16, results=(0, 2),
    )(flags, force_e, weight, inverse, velocity, mult, mult_up, face, inverse_t, by_row_again, spots, place, *edges)
    tail = lax.ppermute(tail, "gx", ring("gx", -1))
    return jnp.concatenate([head, tail], 1), mult[None]


def solution(mesh):
    in_specs = (
        P(None, "gx", "gy", "gz"),
        P("gx", "gy", "gz"),
        P("gx", "gy", "gz", None, None),
        P("gx", "gy", "gz", None, None),
        P("gx", "gy", "gz", None),
        P("gx", "gy", "gz"),
        P("gx", "gy", "gz", None),
        P("gx", "gy", "gz"),
    )
    out_specs = (P(None, "gx", "gy", "gz"), P("gx", None, "gy", "gz"))
    return jax.shard_map(shards, mesh=mesh, in_specs=in_specs, out_specs=out_specs, check_vma=False)
```

```python
import functools

import jax
import jax.numpy as jnp
from jax import lax
from jax.experimental import pallas as pl
from jax.experimental.pallas import tpu as pltpu
from jax.sharding import PartitionSpec as P

BLK = 64
NAGG = 512
TAIL = 7
HEAD = 15
NP = TAIL + HEAD
ROWS = 24
LINES = 3 * ROWS
LOW = TAIL
UPP = TAIL - 1
RET = 4
COARSE_OMEGA = 0.8
PROLONG_GAIN = 0.5
F32 = jnp.float32
BF16 = jnp.bfloat16

VMEM = pl.BlockSpec(memory_space=pltpu.VMEM)
SMEM = pl.BlockSpec(memory_space=pltpu.SMEM)
HBM = pl.BlockSpec(memory_space=pltpu.HBM)


def keep(x):
    return pltpu.with_memory_space_constraint(x, pltpu.VMEM)


def call(body, outs, scratch=(), n_smem=0, n_in=0, n_far=0, limit=12, results=()):
    kernel = pl.pallas_call(
        body,
        out_shape=[jax.ShapeDtypeStruct(s, d) if i in results else pltpu.VMEM(s, d) for i, (s, d) in enumerate(outs)],
        in_specs=[SMEM] * n_smem + [VMEM] * n_in + [HBM] * n_far,
        out_specs=[VMEM] * len(outs),
        scratch_shapes=list(scratch),
        compiler_params=pltpu.CompilerParams(vmem_limit_bytes=limit * 1024 * 1024),
    )

    def run(*args):
        near = n_smem + n_in
        far = [pltpu.with_memory_space_constraint(x, pltpu.HBM) for x in args[near:]]
        held = [keep(x) for x in args[n_smem:near]]
        return kernel(*args[:n_smem], *held, *far)

    return run


def prepare_kernel(flags, blocks, index, count, by_row, spots, place, near, piece, lists, index_near, count_near, sems):
    copies = [
        pltpu.make_async_copy(blocks.at[:, pl.ds(1024 * i, 1024)], near.at[i], sems.at[i]) for i in range(4)
    ]
    for copy in copies:
        copy.start()
    zero = jnp.zeros((8, 128), F32)
    lane = lax.broadcasted_iota(jnp.int32, (8, 128), 1)
    spot = lane & 31
    source = jnp.where(spot < 24, 2 * spot + (lax.shift_right_logical(lane, 5) & 1), 0)
    lists[...] = jnp.zeros((8, 128), jnp.int32)
    small = [
        pltpu.make_async_copy(index, index_near, sems.at[4]),
        pltpu.make_async_copy(count, count_near, sems.at[5]),
    ]
    for copy in small:
        copy.start()
    for copy in small:
        copy.wait()
    lists[0:4, 0:48] = index_near[...]
    lists[4:5, 0:48] = count_near[...]

    def pick(row):
        full = jnp.broadcast_to(lists[row : row + 1, :], (8, 128))
        return jnp.take_along_axis(full, source, axis=1, mode="promise_in_bounds")

    used = pick(4)
    down = lax.broadcasted_iota(jnp.int32, (128, 128), 0) & 63
    for tile in range(2):
        k = 2 * tile + lax.shift_right_logical(lane, 6)
        block = jnp.where(lane < 64, pick(2 * tile), pick(2 * tile + 1))
        at = (block & 1) * 32 + lax.shift_right_logical(block, 1)
        live = (k < used) & (spot < 24)
        at = jnp.where(live, at, 31)
        spots[:, 128 * tile : 128 * tile + 128] = at
        hit = (down == at[0:1]) & (at[0:1] != 31)
        place[:, 128 * tile : 128 * tile + 128] = jnp.where(hit, 1.0, 0.0).astype(BF16)

    for i, copy in enumerate(copies):
        copy.wait()

        def chunk(g, _):
            for s in range(2):
                at = pl.multiple_of((2 * g + s) * 128, 128)
                piece[s] = near[i, :, pl.ds(at, 128)]
                for tile in range(2):
                    rows = []
                    for k in (2 * tile, 2 * tile + 1):
                        for par in range(2):
                            rows += [piece[s, pl.ds(4 * par + k, 24, stride=8), :], zero]
                    by_row[tile, pl.ds(1024 * i + at, 128), :] = jnp.concatenate(rows, 0).T
            return 0

        lax.fori_loop(0, 4, chunk, 0)


def split(x):
    high = x.astype(BF16)
    return high, (x - high.astype(F32)).astype(BF16)


def fold(parts):
    sub = lax.broadcasted_iota(jnp.int32, (8, 128), 0)
    m = sub < 4
    a = [
        jnp.where(m, parts[i], parts[i + 4]) + pltpu.roll(jnp.where(m, parts[i + 4], parts[i]), 4, 0)
        for i in range(4)
    ]
    m = (sub & 2) == 0
    a = [
        jnp.where(m, a[i], pltpu.roll(a[i + 2], 2, 0)) + jnp.where(m, pltpu.roll(a[i], 6, 0), a[i + 2])
        for i in range(2)
    ]
    m = (sub & 1) == 0
    return jnp.where(m, a[0], pltpu.roll(a[1], 1, 0)) + jnp.where(m, pltpu.roll(a[0], 7, 0), a[1])


def project(by_row, spots, values):
    total = None
    for tile in range(2):
        picked = [
            jnp.take_along_axis(
                values[8 * g : 8 * g + 8], spots[:, 128 * tile : 128 * tile + 128], axis=1,
                mode="promise_in_bounds",
            )
            for g in range(8)
        ]
        rows = []
        for group in range(8):
            parts = []
            for s in range(8):
                base = 64 * (8 * group + s)
                terms = [by_row[tile, base + 8 * g : base + 8 * g + 8, :] * picked[g] for g in range(8)]
                while len(terms) > 1:
                    terms = [terms[i] + terms[i + 1] for i in range(0, len(terms), 2)]
                parts.append(terms[0])
            rows.append(fold(parts))
        part = jnp.concatenate(rows, 0)
        total = part if total is None else total + part
    return total + pltpu.roll(total, 64, 1)


def project_back(by_row, place, values):
    first = second = jnp.zeros((64, 128), F32)
    for i in range(64):
        row = jnp.broadcast_to(values[i : i + 1], (64, 128))
        first = first + by_row[0, 64 * i : 64 * i + 64, :] * row
        second = second + by_row[1, 64 * i : 64 * i + 64, :] * row
    high, low = split(jnp.concatenate([first, second], 1))
    both = lax.dot_general(
        jnp.concatenate([high, low], 0), place[...], (((1,), (1,)), ((), ())), preferred_element_type=F32
    )
    return both[0:64] + both[64:128]


def turn(lower, upper):
    left = lax.broadcasted_iota(jnp.int32, (24, 128), 1) < 64
    even = jnp.where(left, lower, pltpu.roll(upper, 64, 1))
    odd = jnp.where(left, pltpu.roll(lower, 64, 1), upper)
    zero = jnp.zeros((8, 128), F32)
    turned = jnp.concatenate([even, zero, odd, zero, even, zero, odd, zero], 0).T
    return turned[0:64], turned[64:128]


def turn_back(lower, upper):
    left = lax.broadcasted_iota(jnp.int32, (24, 128), 1) < 64
    rows = jnp.concatenate([lower, upper], 0).T
    even, odd = rows[0:24], rows[32:56]
    return (
        jnp.where(left, even, pltpu.roll(odd, 64, 1)),
        jnp.where(left, pltpu.roll(even, 64, 1), odd),
    )


def solve_interface(lower, upper, face, inverse, mortar):
    by_row, spots, place = mortar
    low_t, upp_t = turn(lower, upper)
    rhs = low_t - project(by_row, spots, upp_t)
    first = face * rhs
    back = project_back(by_row, place, first) * inverse
    rest = 0.6 * rhs - project(by_row, spots, back)
    increment = first + face * rest
    return turn_back(increment, project_back(by_row, place, increment))


def tall(plane):
    return jnp.concatenate([plane] * 3, 0)


def yes(flags, row, shape):
    line = jnp.concatenate([flags[row : row + 1, :]] * (shape[1] // 128), 1)
    return jnp.broadcast_to(line, shape) == 1


def sides(flags, y_first, y_second, z_first, z_second):
    tall_shape, zero = (LINES, 128), jnp.zeros((LINES, 128), F32)
    y_even, z_even = yes(flags, 0, tall_shape), yes(flags, 1, (8, 128))
    a, b, c, d = y_first[0:LINES], y_second[0:LINES], z_first[0:8], z_second[0:8]
    return (
        jnp.where(yes(flags, 2, tall_shape), jnp.where(y_even, b, a), zero),
        jnp.where(yes(flags, 3, tall_shape), jnp.where(y_even, a, b), zero),
        jnp.where(yes(flags, 4, (8, 128)), jnp.where(z_even, d, c), zero[0:8]),
        jnp.where(yes(flags, 5, (8, 128)), jnp.where(z_even, c, d), zero[0:8]),
    )


def place_of(p, c):
    return ROWS * c + p


def residual_of(p, c, force, weight, velocity, halo):
    y_low, y_high, z_low, z_high = halo
    i = place_of(p, c)
    sub = lax.broadcasted_iota(jnp.int32, (8, 128), 0)
    lane = lax.broadcasted_iota(jnp.int32, (8, 128), 1)
    v = velocity[p, c]
    total = force[p, c] - weight[p] * v
    if p not in (0, LOW):
        total = total + velocity[p - 1, c]
    if p not in (NP - 1, UPP):
        total = total + velocity[p + 1, c]
    total = total + jnp.where(sub == 0, y_low[i : i + 1], pltpu.roll(v, 1, 0))
    total = total + jnp.where(sub == 7, y_high[i : i + 1], pltpu.roll(v, 7, 0))
    total = total + jnp.where(lane == 0, pltpu.roll(z_low, (128 - i) % 128, 1), pltpu.roll(v, 1, 1))
    total = total + jnp.where(lane == 127, pltpu.roll(z_high, 127 - i, 1), pltpu.roll(v, 127, 1))
    return total


def write_lines(flags, get, y_first, y_second, row=0, count=3):
    y_even = yes(flags, 0, (1, 128))
    for c in range(count):
        for p in range(NP):
            v = get(p, c)
            i = row + place_of(p, c)
            y_first[i : i + 1] = jnp.where(y_even, v[7:8], v[0:1])
            y_second[i : i + 1] = jnp.where(y_even, v[0:1], v[7:8])
        i = row + place_of(NP, c)
        y_first[i : i + ROWS - NP] = jnp.zeros((ROWS - NP, 128), F32)
        y_second[i : i + ROWS - NP] = jnp.zeros((ROWS - NP, 128), F32)


def write_columns(flags, get, z_first, z_second, row=0):
    z_even = yes(flags, 1, (8, 128))
    lane = lax.broadcasted_iota(jnp.int32, (8, 128), 1)
    first = jnp.zeros((8, 128), F32)
    last = first
    for c in range(3):
        for p in range(NP):
            v, i = get(p, c), place_of(p, c)
            first = jnp.where(lane == i, pltpu.roll(v, i, 1) if i else v, first)
            last = jnp.where(lane == i, pltpu.roll(v, i + 1, 1), last)
    z_first[row : row + 8] = jnp.where(z_even, last, first)
    z_second[row : row + 8] = jnp.where(z_even, first, last)


def first_sweep_kernel(
    flags, force_in, kappa_in, agg_in, tail, by_row, spots, place,
    force, weight, inverse, agg, velocity, mult, mult_up, face, inverse_t, z1, z2,
):
    for p in range(NP):
        here = p - TAIL
        kappa = tail[p, 3] if here < 0 else kappa_in[here]
        w = 6.0 + kappa
        weight[p] = w
        inverse[p] = 1.0 / (1.5 * w)
        agg[p] = tail[p, 4].astype(jnp.int32) if here < 0 else agg_in[here]
        for c in range(3):
            f = tail[p, c] if here < 0 else force_in[c, here]
            force[p, c] = f
            velocity[p, c] = f * inverse[p]
    low_w, upp_inv = turn(tall(weight[LOW]), tall(inverse[UPP]))
    face[...] = 0.6 * low_w
    inverse_t[...] = upp_inv
    lower = velocity[LOW].reshape(24, 128)
    upper = velocity[UPP].reshape(24, 128)
    increment, pulled = solve_interface(
        lower, upper, face[...], upp_inv, (by_row, spots, place)
    )
    mult[...] = increment.reshape(3, 8, 128)
    mult_up[...] = pulled.reshape(3, 8, 128)
    velocity[LOW] = (lower - increment * tall(inverse[LOW])).reshape(3, 8, 128)
    velocity[UPP] = (upper + pulled * tall(inverse[UPP])).reshape(3, 8, 128)
    write_columns(flags, lambda p, c: velocity[p, c], z1, z2)
    write_columns(flags, lambda p, c: agg[p].astype(F32), z1, z2, 8)


def lines_kernel(flags, velocity, y1, y2):
    write_lines(flags, lambda p, c: velocity[p, c], y1, y2)


def lines_and_labels_kernel(flags, velocity, agg, y1, y2):
    write_lines(flags, lambda p, c: velocity[p, c], y1, y2)
    write_lines(flags, lambda p, c: agg[p].astype(F32), y1, y2, LINES, 1)


def sweep(
    flags, force, weight, inverse, velocity, mult, mult_up, face, inverse_t, by_row, spots, place,
    halo, out, out_mult, out_up,
):
    def residuals(p):
        return jnp.concatenate([residual_of(p, c, force, weight, velocity, halo) for c in range(3)], 0)

    res_low = residuals(LOW) - mult[...].reshape(24, 128)
    res_upp = residuals(UPP) + mult_up[...].reshape(24, 128)
    inv_low, inv_upp = tall(inverse[LOW]), tall(inverse[UPP])
    lower = velocity[LOW].reshape(24, 128) + res_low * inv_low
    upper = velocity[UPP].reshape(24, 128) + res_upp * inv_upp
    increment, pulled = solve_interface(
        lower, upper, face[...], inverse_t[...], (by_row, spots, place)
    )
    out_mult[...] = mult[...] + increment.reshape(3, 8, 128)
    out_up[...] = mult_up[...] + pulled.reshape(3, 8, 128)
    for p in range(NP):
        if p in (LOW, UPP):
            continue
        for c in range(3):
            out[p, c] = velocity[p, c] + residual_of(p, c, force, weight, velocity, halo) * inverse[p]
    out[LOW] = (lower - increment * inv_low).reshape(3, 8, 128)
    out[UPP] = (upper + pulled * inv_upp).reshape(3, 8, 128)


def second_sweep_kernel(
    flags, force, weight, inverse, velocity, mult, mult_up, face, inverse_t, by_row, spots, place,
    z2, y1, y2, z1, out, out_mult, out_up, oz1, oz2,
):
    halo = sides(flags, y1, y2, z1, z2)
    sweep(
        flags, force, weight, inverse, velocity, mult, mult_up, face, inverse_t, by_row, spots, place,
        halo, out, out_mult, out_up,
    )
    write_columns(flags, lambda p, c: out[p, c], oz1, oz2)


def third_sweep_kernel(
    flags, force, weight, inverse, old, mult, mult_up, face, inverse_t, by_row, spots, place,
    z2, y1, y2, z1, az2, ay1, ay2, az1, agg, iterate, got, swapped,
    out, out_mult, out_up, oz1, oz2, velocity,
):
    core_zero = yes(flags, 1, (24, NAGG))
    a = jnp.where(core_zero, got[...], swapped[...])
    b = jnp.where(core_zero, swapped[...], got[...])
    own, prev = table(iterate[...]), table(a[8:16])
    low, low_prev = table(b[8:16]), table(b[0:8])
    high, high_prev = table(a[16:24]), table(a[0:8])
    for p in range(NP):
        at = where_in(agg[p])
        for c in range(3):
            velocity[p, c] = old[p, c] + pick((prev if p < TAIL else own)[c], at)

    y_low, y_high, z_low, z_high = sides(flags, y1, y2, z1, z2)
    y_even, z_even = yes(flags, 0, (ROWS, 128)), yes(flags, 1, (8, 128))
    ay1, ay2, az1, az2 = ay1[LINES : LINES + ROWS], ay2[LINES : LINES + ROWS], az1[8:16], az2[8:16]
    sub = lax.broadcasted_iota(jnp.int32, (8, 128), 0)
    lane = lax.broadcasted_iota(jnp.int32, (8, 128), 1)

    def lines(values, labels, mine, below, flag):
        labels = labels.astype(jnp.int32)
        parts = []
        for c in range(3):
            for block in range(ROWS // 8):
                at = where_in(labels[8 * block : 8 * block + 8])
                extra = pick(mine[c], at)
                if block == 0:
                    extra = jnp.where(sub < TAIL, pick(below[c], at), extra)
                row = place_of(8 * block, c)
                parts.append(jnp.where(yes(flags, flag, (8, 128)), values[row : row + 8] + extra, 0.0))
        return jnp.concatenate(parts, 0)

    def column(values, labels, flag):
        at = where_in(labels.astype(jnp.int32))
        extra = jnp.zeros((8, 128), F32)
        for c in range(3):
            here = lane - ROWS * c
            extra = jnp.where((here >= 0) & (here < TAIL), pick(prev[c], at), extra)
            extra = jnp.where((here >= TAIL) & (here < NP), pick(own[c], at), extra)
        return jnp.where(yes(flags, flag, (8, 128)), values + extra, 0.0)

    halo = (
        lines(y_low, jnp.where(y_even, ay2, ay1), low, low_prev, 2),
        lines(y_high, jnp.where(y_even, ay1, ay2), high, high_prev, 3),
        column(z_low, jnp.where(z_even, az2, az1), 4),
        column(z_high, jnp.where(z_even, az1, az2), 5),
    )
    sweep(
        flags, force, weight, inverse, velocity, mult, mult_up, face, inverse_t, by_row, spots, place,
        halo, out, out_mult, out_up,
    )
    write_columns(flags, lambda p, c: out[p, c], oz1, oz2)


def last_sweep_kernel(
    flags, force, weight, inverse, velocity, mult, mult_up, face, inverse_t, by_row, spots, place,
    z2, y1, y2, z1, head, tail, out_mult, out, out_up,
):
    halo = sides(flags, y1, y2, z1, z2)
    sweep(
        flags, force, weight, inverse, velocity, mult, mult_up, face, inverse_t, by_row, spots, place,
        halo, out, out_mult, out_up,
    )
    for c in range(3):
        for p in range(16 - RET):
            head[c, p] = out[LOW + p, c]
        for p in range(RET):
            tail[c, p] = out[TAIL - RET + p, c]


def restrict_kernel(
    flags, force, weight, velocity, mult, mult_up, agg, diag, z2, y1, y2, z1, out, res,
):
    halo = sides(flags, y1, y2, z1, z2)
    for p in range(TAIL - 3, NP - 2):
        for c in range(3):
            r = residual_of(p, c, force, weight, velocity, halo)
            if p == LOW:
                r = r - mult[c]
            if p == UPP:
                r = r + mult_up[c]
            res[p, c] = r
    down = lax.broadcasted_iota(jnp.int32, (64, 128), 0)
    sub = lax.broadcasted_iota(jnp.int32, (8, 128), 0)

    def plane(p, total):
        labels = agg[p]
        lows = labels & 63
        highs = lax.shift_right_logical(labels, 6)
        values = []
        for c in range(3):
            r = res[p, c]
            high = r.astype(BF16).astype(F32)
            values += [high, r - high]
        for pair in range(4):
            tables, terms = [], []
            for y in (2 * pair, 2 * pair + 1):
                tables.append(jnp.where(down == lows[y : y + 1], 1.0, 0.0).astype(BF16))
                here = highs[y : y + 1] == sub
                terms.append(jnp.concatenate([jnp.where(here, v[y : y + 1], 0.0) for v in values], 0).astype(BF16))
            total = total + lax.dot_general(
                jnp.concatenate(tables, 1), jnp.concatenate(terms, 1), (((1,), (1,)), ((), ())),
                preferred_element_type=F32,
            )
        return total

    def four(i, total):
        for s in range(4):
            total = plane(LOW + 4 * i + s, total)
        return total

    below = jnp.zeros((64, 48), F32)
    for p in range(TAIL - 3, TAIL):
        below = plane(p, below)
    own = lax.fori_loop(0, 3, four, plane(NP - 3, jnp.zeros((64, 48), F32)))
    both = jnp.concatenate([own, below], 0)
    turned = jnp.concatenate([both, jnp.zeros((128, 80), F32)], 1).T
    for c in range(3):
        out[8 * c : 8 * c + 8] = turned[16 * c : 16 * c + 8] + turned[16 * c + 8 : 16 * c + 16]
    out[24:32] = jnp.where(sub == flags[6:7], jnp.broadcast_to(diag[...], (8, 128)), 0.0)


def gather_sums_kernel(mine, above, across, after, kept, passed):
    kept[...] = mine[...] + across[...]
    lane = lax.broadcasted_iota(jnp.int32, (24, 128), 1)
    passed[...] = jnp.where(lane < 64, pltpu.roll(above[0:24], 64, 1), 0.0)


def add_kernel(one, two, out):
    out[...] = one[...] + two[...]


def join_kernel(a, b, c, after, out):
    out[0:8], out[8:16], out[16:24] = a[...], b[...], c[...]


def add(one, two):
    return call(add_kernel, [(one.shape, F32)], n_in=2)(one, two)[0]


def pack_kernel(force, kappa, agg, out, force_near, kappa_near, agg_near, flags, sems):
    copies = [
        pltpu.make_async_copy(far, near, sems.at[i])
        for i, (far, near) in enumerate(((force, force_near), (kappa, kappa_near), (agg, agg_near)))
    ]
    for copy in copies:
        copy.start()
    gy, gz = lax.axis_index("gy"), lax.axis_index("gz")
    ny, nz = lax.axis_size("gy"), lax.axis_size("gz")
    facts = (gy % 2 == 0, gz % 2 == 0, gy > 0, gy < ny - 1, gz > 0, gz < nz - 1, gz, gz)
    for row, fact in enumerate(facts):
        flags[row : row + 1, :] = jnp.full((1, 128), fact.astype(jnp.int32), jnp.int32)
    for copy in copies:
        copy.wait()
    start = kappa.shape[0] - TAIL
    for p in range(TAIL):
        for c in range(3):
            out[p, c] = force_near[c, start + p]
        out[p, 3] = kappa_near[start + p]
        out[p, 4] = agg_near[start + p].astype(F32)


def split_matrix_kernel(rows, high, low):
    a = rows[...].T
    h = a.astype(BF16)
    high[...] = h
    low[...] = (a - h.astype(F32)).astype(BF16)


def solve_kernel(kept, passed, swapped, high, low, out, rhs):
    sums = kept[0:24] + passed[...] + swapped[...]
    other = pltpu.roll(sums, 64, 1)
    rhs[...] = jnp.zeros((8, NAGG), F32)
    left = lax.broadcasted_iota(jnp.int32, (1, 128), 1) < 64
    for c in range(3):
        for t in range(4):
            at = 8 * c + 2 * t
            rhs[c : c + 1, 128 * t : 128 * t + 128] = jnp.where(left, sums[at : at + 1], other[at + 1 : at + 2])
    gain = (16 * 8 * 512 / NAGG) ** -0.5
    scale = jnp.concatenate([kept[24 + b : 25 + b] for b in range(4)], 1)
    step = jnp.broadcast_to(COARSE_OMEGA / scale, (8, NAGG))
    start = (rhs[...] * gain) * step
    x = start
    for _ in range(3):
        xh, xl = split(x)
        both = jnp.concatenate([xh, xl], 0)
        first = jnp.dot(both, high[...], preferred_element_type=F32)
        second = jnp.dot(xh, low[...], preferred_element_type=F32)
        product = first[0:8] + first[8:16] + second
        x = (1.0 - COARSE_OMEGA) * x + (start - step * product)
    out[...] = x


def table(rows):
    return [
        [jnp.broadcast_to(rows[c : c + 1, 128 * t : 128 * t + 128], (8, 128)) * PROLONG_GAIN for t in range(4)]
        for c in range(3)
    ]


def where_in(labels):
    return labels & 127, lax.shift_right_logical(labels, 7)


def pick(rows, at):
    lane, tile = at
    got = [jnp.take_along_axis(row, lane, axis=1, mode="promise_in_bounds") for row in rows]
    return jnp.where(tile < 2, jnp.where(tile == 0, got[0], got[1]), jnp.where(tile == 2, got[2], got[3]))


def reload_kernel(after, far, near, sem):
    copy = pltpu.make_async_copy(far, near, sem)
    copy.start()
    copy.wait()


def write_head_kernel(head, mult, velocity, out_mult, sems):
    copies = [
        pltpu.make_async_copy(head, velocity.at[:, pl.ds(0, 16 - RET)], sems.at[0]),
        pltpu.make_async_copy(mult, out_mult, sems.at[1]),
    ]
    for copy in copies:
        copy.start()
    for copy in copies:
        copy.wait()


def write_tail_kernel(tail, before, velocity, sem):
    copy = pltpu.make_async_copy(tail, velocity.at[:, pl.ds(16 - RET, RET)], sem)
    copy.start()
    copy.wait()


def ring(axis, by):
    n = lax.axis_size(axis)
    return [(i, (i + by) % n) for i in range(n)]


def swaps(axis, first):
    n = lax.axis_size(axis)
    pairs = []
    for i in range(first, first + n, 2):
        a, b = i % n, (i + 1) % n
        pairs += [(a, b), (b, a)]
    return pairs


def trade(y1, y2, z1, z2):
    return [
        lax.ppermute(z2, "gz", swaps("gz", 1)),
        lax.ppermute(y1, "gy", swaps("gy", 0)),
        lax.ppermute(y2, "gy", swaps("gy", 1)),
        lax.ppermute(z1, "gz", swaps("gz", 0)),
    ]


def by_core(x, rule_zero, rule_one):
    nx, ny, nz = lax.axis_size("gx"), lax.axis_size("gy"), lax.axis_size("gz")
    pairs = []
    for g in range(nx):
        for y in range(ny):
            for z in range(nz):
                dx, dy, dz = rule_one if z % 2 else rule_zero
                to = (((g + dx) % nx) * ny + (y + dy) % ny) * nz + (z + dz) % nz
                pairs.append(((g * ny + y) * nz + z, to))
    return lax.ppermute(x, ("gx", "gy", "gz"), pairs)


def shards(force, kappa, mortar_blocks, mortar_index, mortar_count, agg_map, coarse_matrix, coarse_diag):
    tail_in, force, kappa, agg_map, flags = call(
        pack_kernel,
        [((TAIL, 5, 8, 128), F32), (force.shape, F32), (kappa.shape, F32), (agg_map.shape, jnp.int32),
         ((8, 128), jnp.int32)],
        [pltpu.SemaphoreType.DMA((3,))],
        n_far=3,
    )(force, kappa, agg_map)
    rows, flags = lax.optimization_barrier((coarse_matrix.reshape(128, NAGG), flags))
    rows = lax.all_gather(rows, "gz", tiled=True)
    tail_in = lax.ppermute(tail_in, "gx", ring("gx", 1))

    by_row, spots, place = call(
        prepare_kernel,
        [((2, 4096, 128), F32), ((8, 256), jnp.int32), ((128, 256), BF16)],
        [pltpu.VMEM((4, 192, 1024), F32), pltpu.VMEM((2, 192, 128), F32), pltpu.VMEM((8, 128), jnp.int32),
         pltpu.VMEM((4, 48), jnp.int32), pltpu.VMEM((1, 48), jnp.int32), pltpu.SemaphoreType.DMA((6,))],
        n_in=1,
        n_far=3,
    )(
        flags,
        mortar_blocks.reshape(192, 4096),
        jnp.transpose(mortar_index.reshape(48, 4), (1, 0)),
        mortar_count.reshape(1, 48),
    )

    k_high, k_low = call(split_matrix_kernel, [((NAGG, NAGG), BF16)] * 2, n_in=1)(rows)
    by_row_again = call(
        reload_kernel, [((2, 4096, 128), F32)], [pltpu.SemaphoreType.DMA], n_in=1, n_far=1
    )(k_high, by_row)[0]

    field = ((NP, 3, 8, 128), F32)
    plane = ((3, 8, 128), F32)
    turned = ((64, 128), F32)
    y_msg, z_msg = ((LINES, 128), F32), ((8, 128), F32)
    y_more, z_more = ((LINES + ROWS, 128), F32), ((16, 128), F32)
    out = call(
        first_sweep_kernel,
        [field, ((NP, 8, 128), F32), ((NP, 8, 128), F32), ((NP, 8, 128), jnp.int32), field, plane, plane,
         turned, turned, z_more, z_more],
        n_in=8,
    )(flags, force, kappa, agg_map, tail_in, by_row, spots, place)
    force_e, weight, inverse, agg, velocity, mult, mult_up, face, inverse_t = out[:9]
    lines = call(lines_and_labels_kernel, [y_more, y_more], n_in=3)(flags, velocity, agg)
    labels = trade(*lines, *out[9:])
    velocity, mult, mult_up, *msgs = call(
        second_sweep_kernel, [field, plane, plane, z_msg, z_msg], n_in=16
    )(flags, force_e, weight, inverse, velocity, mult, mult_up, face, inverse_t, by_row, spots, place, *labels)
    edges = trade(*call(lines_kernel, [y_msg, y_msg], n_in=2)(flags, velocity), *msgs)
    sums = call(
        restrict_kernel, [((32, 128), F32)], [pltpu.VMEM((NP, 3, 8, 128), F32)], n_in=12
    )(flags, force_e, weight, velocity, mult, mult_up, agg, coarse_diag.reshape(1, 128), *edges)[0]
    sums = add(sums, lax.ppermute(sums, "gz", swaps("gz", 0)))
    above = by_core(sums, (-1, 0, 2), (-1, 0, 0))
    across = lax.ppermute(sums, "gz", ring("gz", 2))
    kept, passed = call(gather_sums_kernel, [((32, 128), F32), ((24, 128), F32)], n_in=4)(
        sums, above, across, k_high
    )
    swapped = lax.ppermute(passed, "gz", swaps("gz", 0))
    iterate = call(solve_kernel, [((8, NAGG), F32)], [pltpu.VMEM((8, NAGG), F32)], n_in=5)(
        kept, passed, swapped, k_high, k_low
    )[0]
    got = [
        by_core(iterate, (1, -1, 0), (1, 1, 0)),
        by_core(iterate, (1, 0, 0), (0, 1, 0)),
        by_core(iterate, (0, -1, 0), (0, 1, 0)),
    ]
    got = call(join_kernel, [((24, NAGG), F32)], n_in=4)(*got, by_row_again)[0]
    swapped = lax.ppermute(got, "gz", swaps("gz", 0))
    velocity, mult, mult_up, *msgs = call(
        third_sweep_kernel, [field, plane, plane, z_msg, z_msg],
        [pltpu.VMEM((NP, 3, 8, 128), F32)], n_in=24,
    )(
        flags, force_e, weight, inverse, velocity, mult, mult_up, face, inverse_t, by_row_again, spots, place,
        *edges, *labels, agg, iterate, got, swapped,
    )
    edges = trade(*call(lines_kernel, [y_msg, y_msg], n_in=2)(flags, velocity), *msgs)
    head, tail, mult = call(
        last_sweep_kernel, [((3, 16 - RET, 8, 128), F32), ((3, RET, 8, 128), F32), plane],
        [pltpu.VMEM((NP, 3, 8, 128), F32), pltpu.VMEM((3, 8, 128), F32)], n_in=16,
    )(flags, force_e, weight, inverse, velocity, mult, mult_up, face, inverse_t, by_row_again, spots, place, *edges)
    tail = lax.ppermute(tail, "gx", ring("gx", -1))
    shapes = [pltpu.HBM((3, 16, 8, 128), F32), pltpu.HBM((3, 8, 128), F32)]
    velocity, mult = pl.pallas_call(
        write_head_kernel, out_shape=shapes, in_specs=[VMEM] * 2, out_specs=[HBM] * 2,
        scratch_shapes=[pltpu.SemaphoreType.DMA((2,))],
        compiler_params=pltpu.CompilerParams(vmem_limit_bytes=12 * 1024 * 1024),
    )(keep(head), keep(mult))
    velocity = pl.pallas_call(
        write_tail_kernel, out_shape=shapes[0], in_specs=[VMEM, HBM], out_specs=HBM,
        scratch_shapes=[pltpu.SemaphoreType.DMA], input_output_aliases={1: 0},
        compiler_params=pltpu.CompilerParams(vmem_limit_bytes=12 * 1024 * 1024),
    )(keep(tail), pltpu.with_memory_space_constraint(velocity, pltpu.HBM))
    return velocity, mult[None]


def solution(mesh):
    in_specs = (
        P(None, "gx", "gy", "gz"),
        P("gx", "gy", "gz"),
        P("gx", "gy", "gz", None, None),
        P("gx", "gy", "gz", None, None),
        P("gx", "gy", "gz", None),
        P("gx", "gy", "gz"),
        P("gx", "gy", "gz", None),
        P("gx", "gy", "gz"),
    )
    out_specs = (P(None, "gx", "gy", "gz"), P("gx", None, "gy", "gz"))
    return jax.shard_map(shards, mesh=mesh, in_specs=in_specs, out_specs=out_specs, check_vma=False)
```

```python
import functools

import jax
import jax.numpy as jnp
from jax import lax
from jax.experimental import pallas as pl
from jax.experimental.pallas import tpu as pltpu
from jax.sharding import PartitionSpec as P

BLK = 64
NAGG = 512
TAIL = 7
HEAD = 15
NP = TAIL + HEAD
ROWS = 24
LINES = 3 * ROWS
LOW = TAIL
UPP = TAIL - 1
RET = 4
COARSE_OMEGA = 0.8
PROLONG_GAIN = 0.5
F32 = jnp.float32
BF16 = jnp.bfloat16

VMEM = pl.BlockSpec(memory_space=pltpu.VMEM)
SMEM = pl.BlockSpec(memory_space=pltpu.SMEM)
HBM = pl.BlockSpec(memory_space=pltpu.HBM)


def keep(x):
    return pltpu.with_memory_space_constraint(x, pltpu.VMEM)


def call(body, outs, scratch=(), n_smem=0, n_in=0, n_far=0, limit=12, results=()):
    kernel = pl.pallas_call(
        body,
        out_shape=[jax.ShapeDtypeStruct(s, d) if i in results else pltpu.VMEM(s, d) for i, (s, d) in enumerate(outs)],
        in_specs=[SMEM] * n_smem + [VMEM] * n_in + [HBM] * n_far,
        out_specs=[VMEM] * len(outs),
        scratch_shapes=list(scratch),
        compiler_params=pltpu.CompilerParams(vmem_limit_bytes=limit * 1024 * 1024),
    )

    def run(*args):
        near = n_smem + n_in
        far = [pltpu.with_memory_space_constraint(x, pltpu.HBM) for x in args[near:]]
        held = [keep(x) for x in args[n_smem:near]]
        return kernel(*args[:n_smem], *held, *far)

    return run


def prepare_kernel(flags, blocks, index, count, by_row, spots, place, near, piece, lists, index_near, count_near, sems):
    copies = [
        pltpu.make_async_copy(blocks.at[:, pl.ds(1024 * i, 1024)], near.at[i], sems.at[i]) for i in range(4)
    ]
    for copy in copies:
        copy.start()
    zero = jnp.zeros((8, 128), F32)
    lane = lax.broadcasted_iota(jnp.int32, (8, 128), 1)
    spot = lane & 31
    source = jnp.where(spot < 24, 2 * spot + (lax.shift_right_logical(lane, 5) & 1), 0)
    lists[...] = jnp.zeros((8, 128), jnp.int32)
    small = [
        pltpu.make_async_copy(index, index_near, sems.at[4]),
        pltpu.make_async_copy(count, count_near, sems.at[5]),
    ]
    for copy in small:
        copy.start()
    for copy in small:
        copy.wait()
    lists[0:4, 0:48] = index_near[...]
    lists[4:5, 0:48] = count_near[...]

    def pick(row):
        full = jnp.broadcast_to(lists[row : row + 1, :], (8, 128))
        return jnp.take_along_axis(full, source, axis=1, mode="promise_in_bounds")

    used = pick(4)
    down = lax.broadcasted_iota(jnp.int32, (128, 128), 0) & 63
    for tile in range(2):
        k = 2 * tile + lax.shift_right_logical(lane, 6)
        block = jnp.where(lane < 64, pick(2 * tile), pick(2 * tile + 1))
        at = (block & 1) * 32 + lax.shift_right_logical(block, 1)
        live = (k < used) & (spot < 24)
        at = jnp.where(live, at, 31)
        spots[:, 128 * tile : 128 * tile + 128] = at
        hit = (down == at[0:1]) & (at[0:1] != 31)
        place[:, 128 * tile : 128 * tile + 128] = jnp.where(hit, 1.0, 0.0).astype(BF16)

    for i, copy in enumerate(copies):
        copy.wait()

        def chunk(g, _):
            for s in range(2):
                at = pl.multiple_of((2 * g + s) * 128, 128)
                piece[s] = near[i, :, pl.ds(at, 128)]
                for tile in range(2):
                    rows = []
                    for k in (2 * tile, 2 * tile + 1):
                        for par in range(2):
                            rows += [piece[s, pl.ds(4 * par + k, 24, stride=8), :], zero]
                    by_row[tile, pl.ds(1024 * i + at, 128), :] = jnp.concatenate(rows, 0).T
            return 0

        lax.fori_loop(0, 4, chunk, 0)


def split(x):
    high = x.astype(BF16)
    return high, (x - high.astype(F32)).astype(BF16)


def fold(parts):
    sub = lax.broadcasted_iota(jnp.int32, (8, 128), 0)
    m = sub < 4
    a = [
        jnp.where(m, parts[i], parts[i + 4]) + pltpu.roll(jnp.where(m, parts[i + 4], parts[i]), 4, 0)
        for i in range(4)
    ]
    m = (sub & 2) == 0
    a = [
        jnp.where(m, a[i], pltpu.roll(a[i + 2], 2, 0)) + jnp.where(m, pltpu.roll(a[i], 6, 0), a[i + 2])
        for i in range(2)
    ]
    m = (sub & 1) == 0
    return jnp.where(m, a[0], pltpu.roll(a[1], 1, 0)) + jnp.where(m, pltpu.roll(a[0], 7, 0), a[1])


def project(by_row, spots, values):
    total = None
    for tile in range(2):
        picked = [
            jnp.take_along_axis(
                values[8 * g : 8 * g + 8], spots[:, 128 * tile : 128 * tile + 128], axis=1,
                mode="promise_in_bounds",
            )
            for g in range(8)
        ]
        rows = []
        for group in range(8):
            parts = []
            for s in range(8):
                base = 64 * (8 * group + s)
                terms = [by_row[tile, base + 8 * g : base + 8 * g + 8, :] * picked[g] for g in range(8)]
                while len(terms) > 1:
                    terms = [terms[i] + terms[i + 1] for i in range(0, len(terms), 2)]
                parts.append(terms[0])
            rows.append(fold(parts))
        part = jnp.concatenate(rows, 0)
        total = part if total is None else total + part
    return total + pltpu.roll(total, 64, 1)


def project_back(by_row, place, values):
    first = second = jnp.zeros((64, 128), F32)
    for i in range(64):
        row = jnp.broadcast_to(values[i : i + 1], (64, 128))
        first = first + by_row[0, 64 * i : 64 * i + 64, :] * row
        second = second + by_row[1, 64 * i : 64 * i + 64, :] * row
    high, low = split(jnp.concatenate([first, second], 1))
    both = lax.dot_general(
        jnp.concatenate([high, low], 0), place[...], (((1,), (1,)), ((), ())), preferred_element_type=F32
    )
    return both[0:64] + both[64:128]


def turn(lower, upper):
    left = lax.broadcasted_iota(jnp.int32, (24, 128), 1) < 64
    even = jnp.where(left, lower, pltpu.roll(upper, 64, 1))
    odd = jnp.where(left, pltpu.roll(lower, 64, 1), upper)
    zero = jnp.zeros((8, 128), F32)
    turned = jnp.concatenate([even, zero, odd, zero, even, zero, odd, zero], 0).T
    return turned[0:64], turned[64:128]


def turn_back(lower, upper):
    left = lax.broadcasted_iota(jnp.int32, (24, 128), 1) < 64
    rows = jnp.concatenate([lower, upper], 0).T
    even, odd = rows[0:24], rows[32:56]
    return (
        jnp.where(left, even, pltpu.roll(odd, 64, 1)),
        jnp.where(left, pltpu.roll(even, 64, 1), odd),
    )


def solve_interface(lower, upper, face, inverse, mortar):
    by_row, spots, place = mortar
    low_t, upp_t = turn(lower, upper)
    rhs = low_t - project(by_row, spots, upp_t)
    first = face * rhs
    back = project_back(by_row, place, first) * inverse
    rest = 0.6 * rhs - project(by_row, spots, back)
    increment = first + face * rest
    return turn_back(increment, project_back(by_row, place, increment))


def tall(plane):
    return jnp.concatenate([plane] * 3, 0)


def yes(flags, row, shape):
    line = jnp.concatenate([flags[row : row + 1, :]] * (shape[1] // 128), 1)
    return jnp.broadcast_to(line, shape) == 1


def sides(flags, y_first, y_second, z_first, z_second):
    tall_shape, zero = (LINES, 128), jnp.zeros((LINES, 128), F32)
    y_even, z_even = yes(flags, 0, tall_shape), yes(flags, 1, (8, 128))
    a, b, c, d = y_first[0:LINES], y_second[0:LINES], z_first[0:8], z_second[0:8]
    return (
        jnp.where(yes(flags, 2, tall_shape), jnp.where(y_even, b, a), zero),
        jnp.where(yes(flags, 3, tall_shape), jnp.where(y_even, a, b), zero),
        jnp.where(yes(flags, 4, (8, 128)), jnp.where(z_even, d, c), zero[0:8]),
        jnp.where(yes(flags, 5, (8, 128)), jnp.where(z_even, c, d), zero[0:8]),
    )


def place_of(p, c):
    return ROWS * c + p


def residual_of(p, c, force, weight, velocity, halo):
    y_low, y_high, z_low, z_high = halo
    i = place_of(p, c)
    sub = lax.broadcasted_iota(jnp.int32, (8, 128), 0)
    lane = lax.broadcasted_iota(jnp.int32, (8, 128), 1)
    v = velocity[p, c]
    total = force[p, c] - weight[p] * v
    if p not in (0, LOW):
        total = total + velocity[p - 1, c]
    if p not in (NP - 1, UPP):
        total = total + velocity[p + 1, c]
    total = total + jnp.where(sub == 0, y_low[i : i + 1], pltpu.roll(v, 1, 0))
    total = total + jnp.where(sub == 7, y_high[i : i + 1], pltpu.roll(v, 7, 0))
    total = total + jnp.where(lane == 0, pltpu.roll(z_low, (128 - i) % 128, 1), pltpu.roll(v, 1, 1))
    total = total + jnp.where(lane == 127, pltpu.roll(z_high, 127 - i, 1), pltpu.roll(v, 127, 1))
    return total


def write_lines(flags, get, y_first, y_second, row=0, count=3):
    y_even = yes(flags, 0, (1, 128))
    for c in range(count):
        for p in range(NP):
            v = get(p, c)
            i = row + place_of(p, c)
            y_first[i : i + 1] = jnp.where(y_even, v[7:8], v[0:1])
            y_second[i : i + 1] = jnp.where(y_even, v[0:1], v[7:8])
        i = row + place_of(NP, c)
        y_first[i : i + ROWS - NP] = jnp.zeros((ROWS - NP, 128), F32)
        y_second[i : i + ROWS - NP] = jnp.zeros((ROWS - NP, 128), F32)


def write_columns(flags, get, z_first, z_second, row=0):
    z_even = yes(flags, 1, (8, 128))
    lane = lax.broadcasted_iota(jnp.int32, (8, 128), 1)
    first = jnp.zeros((8, 128), F32)
    last = first
    for c in range(3):
        for p in range(NP):
            v, i = get(p, c), place_of(p, c)
            first = jnp.where(lane == i, pltpu.roll(v, i, 1) if i else v, first)
            last = jnp.where(lane == i, pltpu.roll(v, i + 1, 1), last)
    z_first[row : row + 8] = jnp.where(z_even, last, first)
    z_second[row : row + 8] = jnp.where(z_even, first, last)


def first_sweep_kernel(
    flags, force_in, kappa_in, agg_in, tail, by_row, spots, place,
    force, weight, inverse, agg, velocity, mult, mult_up, face, inverse_t, z1, z2,
):
    for p in range(NP):
        here = p - TAIL
        kappa = tail[p, 3] if here < 0 else kappa_in[here]
        w = 6.0 + kappa
        weight[p] = w
        inverse[p] = 1.0 / (1.5 * w)
        agg[p] = tail[p, 4].astype(jnp.int32) if here < 0 else agg_in[here]
        for c in range(3):
            f = tail[p, c] if here < 0 else force_in[c, here]
            force[p, c] = f
            velocity[p, c] = f * inverse[p]
    low_w, upp_inv = turn(tall(weight[LOW]), tall(inverse[UPP]))
    face[...] = 0.6 * low_w
    inverse_t[...] = upp_inv
    lower = velocity[LOW].reshape(24, 128)
    upper = velocity[UPP].reshape(24, 128)
    increment, pulled = solve_interface(
        lower, upper, face[...], upp_inv, (by_row, spots, place)
    )
    mult[...] = increment.reshape(3, 8, 128)
    mult_up[...] = pulled.reshape(3, 8, 128)
    velocity[LOW] = (lower - increment * tall(inverse[LOW])).reshape(3, 8, 128)
    velocity[UPP] = (upper + pulled * tall(inverse[UPP])).reshape(3, 8, 128)
    write_columns(flags, lambda p, c: velocity[p, c], z1, z2)
    write_columns(flags, lambda p, c: agg[p].astype(F32), z1, z2, 8)


def lines_kernel(flags, velocity, y1, y2):
    write_lines(flags, lambda p, c: velocity[p, c], y1, y2)


def lines_and_labels_kernel(flags, velocity, agg, y1, y2):
    write_lines(flags, lambda p, c: velocity[p, c], y1, y2)
    write_lines(flags, lambda p, c: agg[p].astype(F32), y1, y2, LINES, 1)


def sweep(
    flags, force, weight, inverse, velocity, mult, mult_up, face, inverse_t, by_row, spots, place,
    halo, out, out_mult, out_up,
):
    def residuals(p):
        return jnp.concatenate([residual_of(p, c, force, weight, velocity, halo) for c in range(3)], 0)

    res_low = residuals(LOW) - mult[...].reshape(24, 128)
    res_upp = residuals(UPP) + mult_up[...].reshape(24, 128)
    inv_low, inv_upp = tall(inverse[LOW]), tall(inverse[UPP])
    lower = velocity[LOW].reshape(24, 128) + res_low * inv_low
    upper = velocity[UPP].reshape(24, 128) + res_upp * inv_upp
    increment, pulled = solve_interface(
        lower, upper, face[...], inverse_t[...], (by_row, spots, place)
    )
    out_mult[...] = mult[...] + increment.reshape(3, 8, 128)
    out_up[...] = mult_up[...] + pulled.reshape(3, 8, 128)
    for p in range(NP):
        if p in (LOW, UPP):
            continue
        for c in range(3):
            out[p, c] = velocity[p, c] + residual_of(p, c, force, weight, velocity, halo) * inverse[p]
    out[LOW] = (lower - increment * inv_low).reshape(3, 8, 128)
    out[UPP] = (upper + pulled * inv_upp).reshape(3, 8, 128)


def second_sweep_kernel(
    flags, force, weight, inverse, velocity, mult, mult_up, face, inverse_t, by_row, spots, place,
    z2, y1, y2, z1, out, out_mult, out_up, oz1, oz2,
):
    halo = sides(flags, y1, y2, z1, z2)
    sweep(
        flags, force, weight, inverse, velocity, mult, mult_up, face, inverse_t, by_row, spots, place,
        halo, out, out_mult, out_up,
    )
    write_columns(flags, lambda p, c: out[p, c], oz1, oz2)


def third_sweep_kernel(
    flags, force, weight, inverse, old, mult, mult_up, face, inverse_t, by_row, spots, place,
    z2, y1, y2, z1, az2, ay1, ay2, az1, agg, iterate, got, swapped,
    out, out_mult, out_up, oz1, oz2, velocity,
):
    core_zero = yes(flags, 1, (24, NAGG))
    a = jnp.where(core_zero, got[...], swapped[...])
    b = jnp.where(core_zero, swapped[...], got[...])
    own, prev = table(iterate[...]), table(a[8:16])
    low, low_prev = table(b[8:16]), table(b[0:8])
    high, high_prev = table(a[16:24]), table(a[0:8])
    for p in range(NP):
        at = where_in(agg[p])
        for c in range(3):
            velocity[p, c] = old[p, c] + pick((prev if p < TAIL else own)[c], at)

    y_low, y_high, z_low, z_high = sides(flags, y1, y2, z1, z2)
    y_even, z_even = yes(flags, 0, (ROWS, 128)), yes(flags, 1, (8, 128))
    ay1, ay2, az1, az2 = ay1[LINES : LINES + ROWS], ay2[LINES : LINES + ROWS], az1[8:16], az2[8:16]
    sub = lax.broadcasted_iota(jnp.int32, (8, 128), 0)
    lane = lax.broadcasted_iota(jnp.int32, (8, 128), 1)

    def lines(values, labels, mine, below, flag):
        labels = labels.astype(jnp.int32)
        parts = []
        for c in range(3):
            for block in range(ROWS // 8):
                at = where_in(labels[8 * block : 8 * block + 8])
                extra = pick(mine[c], at)
                if block == 0:
                    extra = jnp.where(sub < TAIL, pick(below[c], at), extra)
                row = place_of(8 * block, c)
                parts.append(jnp.where(yes(flags, flag, (8, 128)), values[row : row + 8] + extra, 0.0))
        return jnp.concatenate(parts, 0)

    def column(values, labels, flag):
        at = where_in(labels.astype(jnp.int32))
        extra = jnp.zeros((8, 128), F32)
        for c in range(3):
            here = lane - ROWS * c
            extra = jnp.where((here >= 0) & (here < TAIL), pick(prev[c], at), extra)
            extra = jnp.where((here >= TAIL) & (here < NP), pick(own[c], at), extra)
        return jnp.where(yes(flags, flag, (8, 128)), values + extra, 0.0)

    halo = (
        lines(y_low, jnp.where(y_even, ay2, ay1), low, low_prev, 2),
        lines(y_high, jnp.where(y_even, ay1, ay2), high, high_prev, 3),
        column(z_low, jnp.where(z_even, az2, az1), 4),
        column(z_high, jnp.where(z_even, az1, az2), 5),
    )
    sweep(
        flags, force, weight, inverse, velocity, mult, mult_up, face, inverse_t, by_row, spots, place,
        halo, out, out_mult, out_up,
    )
    write_columns(flags, lambda p, c: out[p, c], oz1, oz2)


def last_sweep_kernel(
    flags, force, weight, inverse, velocity, mult, mult_up, face, inverse_t, by_row, spots, place,
    z2, y1, y2, z1, head, tail, out_mult, out, out_up,
):
    halo = sides(flags, y1, y2, z1, z2)
    sweep(
        flags, force, weight, inverse, velocity, mult, mult_up, face, inverse_t, by_row, spots, place,
        halo, out, out_mult, out_up,
    )
    for c in range(3):
        for p in range(16 - RET):
            head[c, p] = out[LOW + p, c]
        for p in range(RET):
            tail[c, p] = out[TAIL - RET + p, c]


def restrict_kernel(
    after, flags, force, weight, velocity, mult, mult_up, agg, diag, z2, y1, y2, z1, out, res,
):
    halo = sides(flags, y1, y2, z1, z2)
    for p in range(TAIL - 3, NP - 2):
        for c in range(3):
            r = residual_of(p, c, force, weight, velocity, halo)
            if p == LOW:
                r = r - mult[c]
            if p == UPP:
                r = r + mult_up[c]
            res[p, c] = r
    down = lax.broadcasted_iota(jnp.int32, (64, 128), 0)
    sub = lax.broadcasted_iota(jnp.int32, (8, 128), 0)

    def plane(p, total):
        labels = agg[p]
        lows = labels & 63
        highs = lax.shift_right_logical(labels, 6)
        values = []
        for c in range(3):
            r = res[p, c]
            high = r.astype(BF16).astype(F32)
            values += [high, r - high]
        for pair in range(4):
            tables, terms = [], []
            for y in (2 * pair, 2 * pair + 1):
                tables.append(jnp.where(down == lows[y : y + 1], 1.0, 0.0).astype(BF16))
                here = highs[y : y + 1] == sub
                terms.append(jnp.concatenate([jnp.where(here, v[y : y + 1], 0.0) for v in values], 0).astype(BF16))
            total = total + lax.dot_general(
                jnp.concatenate(tables, 1), jnp.concatenate(terms, 1), (((1,), (1,)), ((), ())),
                preferred_element_type=F32,
            )
        return total

    def four(i, total):
        for s in range(4):
            total = plane(LOW + 4 * i + s, total)
        return total

    below = jnp.zeros((64, 48), F32)
    for p in range(TAIL - 3, TAIL):
        below = plane(p, below)
    own = lax.fori_loop(0, 3, four, plane(NP - 3, jnp.zeros((64, 48), F32)))
    both = jnp.concatenate([own, below], 0)
    turned = jnp.concatenate([both, jnp.zeros((128, 80), F32)], 1).T
    for c in range(3):
        out[8 * c : 8 * c + 8] = turned[16 * c : 16 * c + 8] + turned[16 * c + 8 : 16 * c + 16]
    out[24:32] = jnp.where(sub == flags[6:7], jnp.broadcast_to(diag[...], (8, 128)), 0.0)


def gather_sums_kernel(mine, above, across, kept, passed):
    kept[...] = mine[...] + across[...]
    lane = lax.broadcasted_iota(jnp.int32, (24, 128), 1)
    passed[...] = jnp.where(lane < 64, pltpu.roll(above[0:24], 64, 1), 0.0)


def add_kernel(one, two, out):
    out[...] = one[...] + two[...]


def join_kernel(a, b, c, out):
    out[0:8], out[8:16], out[16:24] = a[...], b[...], c[...]


def add(one, two):
    return call(add_kernel, [(one.shape, F32)], n_in=2)(one, two)[0]


def pack_kernel(force, kappa, agg, matrix, out, force_near, kappa_near, agg_near, rows, flags, sems):
    copies = [
        pltpu.make_async_copy(far, near, sems.at[i])
        for i, (far, near) in enumerate(
            ((force, force_near), (kappa, kappa_near), (agg, agg_near), (matrix, rows))
        )
    ]
    for copy in copies:
        copy.start()
    gy, gz = lax.axis_index("gy"), lax.axis_index("gz")
    ny, nz = lax.axis_size("gy"), lax.axis_size("gz")
    facts = (gy % 2 == 1, gz % 2 == 0, gy > 0, gy < ny - 1, gz > 0, gz < nz - 1, gz, gz < nz // 2)
    for row, fact in enumerate(facts):
        flags[row : row + 1, :] = jnp.full((1, 128), fact.astype(jnp.int32), jnp.int32)
    for copy in copies:
        copy.wait()
    start = kappa.shape[0] - TAIL
    for p in range(TAIL):
        for c in range(3):
            out[p, c] = force_near[c, start + p]
        out[p, 3] = kappa_near[start + p]
        out[p, 4] = agg_near[start + p].astype(F32)


def stack_kernel(one, two, out):
    out[0:128], out[128:256] = one[...], two[...]


def split_matrix_kernel(flags, mine, other, high, low):
    core_zero, first_half = yes(flags, 1, (256, NAGG)), yes(flags, 7, (128, NAGG))
    sets = jnp.where(core_zero, mine[...], other[...]), jnp.where(core_zero, other[...], mine[...])
    for b in range(4):
        rows = sets[b % 2]
        near, far = (rows[0:128], rows[128:256]) if b < 2 else (rows[128:256], rows[0:128])
        a = jnp.where(first_half, near, far).T
        h = a.astype(BF16)
        high[:, 128 * b : 128 * b + 128] = h
        low[:, 128 * b : 128 * b + 128] = (a - h.astype(F32)).astype(BF16)


def solve_kernel(kept, passed, swapped, high, low, out, rhs):
    sums = kept[0:24] + passed[...] + swapped[...]
    other = pltpu.roll(sums, 64, 1)
    rhs[...] = jnp.zeros((8, NAGG), F32)
    left = lax.broadcasted_iota(jnp.int32, (1, 128), 1) < 64
    for c in range(3):
        for t in range(4):
            at = 8 * c + 2 * t
            rhs[c : c + 1, 128 * t : 128 * t + 128] = jnp.where(left, sums[at : at + 1], other[at + 1 : at + 2])
    gain = (16 * 8 * 512 / NAGG) ** -0.5
    scale = jnp.concatenate([kept[24 + b : 25 + b] for b in range(4)], 1)
    step = jnp.broadcast_to(COARSE_OMEGA / scale, (8, NAGG))
    start = (rhs[...] * gain) * step
    x = start
    for _ in range(3):
        xh, xl = split(x)
        both = jnp.concatenate([xh, xl], 0)
        first = jnp.dot(both, high[...], preferred_element_type=F32)
        second = jnp.dot(xh, low[...], preferred_element_type=F32)
        product = first[0:8] + first[8:16] + second
        x = (1.0 - COARSE_OMEGA) * x + (start - step * product)
    out[...] = x


def table(rows):
    return [
        [jnp.broadcast_to(rows[c : c + 1, 128 * t : 128 * t + 128], (8, 128)) * PROLONG_GAIN for t in range(4)]
        for c in range(3)
    ]


def where_in(labels):
    return labels & 127, lax.shift_right_logical(labels, 7)


def pick(rows, at):
    lane, tile = at
    got = [jnp.take_along_axis(row, lane, axis=1, mode="promise_in_bounds") for row in rows]
    return jnp.where(tile < 2, jnp.where(tile == 0, got[0], got[1]), jnp.where(tile == 2, got[2], got[3]))


def write_head_kernel(head, mult, velocity, out_mult, sems):
    copies = [
        pltpu.make_async_copy(head, velocity.at[:, pl.ds(0, 16 - RET)], sems.at[0]),
        pltpu.make_async_copy(mult, out_mult, sems.at[1]),
    ]
    for copy in copies:
        copy.start()
    for copy in copies:
        copy.wait()


def write_tail_kernel(tail, before, velocity, sem):
    copy = pltpu.make_async_copy(tail, velocity.at[:, pl.ds(16 - RET, RET)], sem)
    copy.start()
    copy.wait()


def ring(axis, by):
    n = lax.axis_size(axis)
    return [(i, (i + by) % n) for i in range(n)]


def swaps(axis, first):
    n = lax.axis_size(axis)
    pairs = []
    for i in range(first, first + n, 2):
        a, b = i % n, (i + 1) % n
        pairs += [(a, b), (b, a)]
    return pairs


def trade(y1, y2, z1, z2):
    return [
        lax.ppermute(z2, "gz", swaps("gz", 1)),
        lax.ppermute(y1, "gy", swaps("gy", 1)),
        lax.ppermute(y2, "gy", swaps("gy", 0)),
        lax.ppermute(z1, "gz", swaps("gz", 0)),
    ]


def by_core(x, rule_zero, rule_one):
    nx, ny, nz = lax.axis_size("gx"), lax.axis_size("gy"), lax.axis_size("gz")
    pairs = []
    for g in range(nx):
        for y in range(ny):
            for z in range(nz):
                dx, dy, dz = rule_one if z % 2 else rule_zero
                to = (((g + dx) % nx) * ny + (y + dy) % ny) * nz + (z + dz) % nz
                pairs.append(((g * ny + y) * nz + z, to))
    return lax.ppermute(x, ("gx", "gy", "gz"), pairs)


def shards(force, kappa, mortar_blocks, mortar_index, mortar_count, agg_map, coarse_matrix, coarse_diag):
    tail_in, force, kappa, agg_map, rows, flags = call(
        pack_kernel,
        [((TAIL, 5, 8, 128), F32), (force.shape, F32), (kappa.shape, F32), (agg_map.shape, jnp.int32),
         ((128, NAGG), F32), ((8, 128), jnp.int32)],
        [pltpu.SemaphoreType.DMA((4,))],
        n_far=4,
    )(force, kappa, agg_map, coarse_matrix.reshape(128, NAGG))
    tail_in = lax.ppermute(tail_in, "gx", ring("gx", 1))
    half = lax.ppermute(rows, "gz", ring("gz", 2))

    by_row, spots, place = call(
        prepare_kernel,
        [((2, 4096, 128), F32), ((8, 256), jnp.int32), ((128, 256), BF16)],
        [pltpu.VMEM((4, 192, 1024), F32), pltpu.VMEM((2, 192, 128), F32), pltpu.VMEM((8, 128), jnp.int32),
         pltpu.VMEM((4, 48), jnp.int32), pltpu.VMEM((1, 48), jnp.int32), pltpu.SemaphoreType.DMA((6,))],
        n_in=1,
        n_far=3,
    )(
        flags,
        mortar_blocks.reshape(192, 4096),
        jnp.transpose(mortar_index.reshape(48, 4), (1, 0)),
        mortar_count.reshape(1, 48),
    )

    field = ((NP, 3, 8, 128), F32)
    plane = ((3, 8, 128), F32)
    turned = ((64, 128), F32)
    y_msg, z_msg = ((LINES, 128), F32), ((8, 128), F32)
    y_more, z_more = ((LINES + ROWS, 128), F32), ((16, 128), F32)
    out = call(
        first_sweep_kernel,
        [field, ((NP, 8, 128), F32), ((NP, 8, 128), F32), ((NP, 8, 128), jnp.int32), field, plane, plane,
         turned, turned, z_more, ((LINES + ROWS + 8, 128), F32)],
        n_in=8,
    )(flags, force, kappa, agg_map, tail_in, by_row, spots, place)
    force_e, weight, inverse, agg, velocity, mult, mult_up, face, inverse_t = out[:9]
    half, velocity = lax.optimization_barrier((half, velocity))
    rows = call(stack_kernel, [((256, NAGG), F32)], n_in=2)(rows, half)[0]
    k_high, k_low = call(split_matrix_kernel, [((NAGG, NAGG), BF16)] * 2, n_in=3)(
        flags, rows, lax.ppermute(rows, "gz", swaps("gz", 0))
    )
    lines = call(lines_and_labels_kernel, [y_more, y_more], n_in=3)(flags, velocity, agg)
    labels = trade(*lines, *out[9:])
    velocity, mult, mult_up, *msgs = call(
        second_sweep_kernel, [field, plane, plane, z_msg, ((LINES + 8, 128), F32)], n_in=16
    )(flags, force_e, weight, inverse, velocity, mult, mult_up, face, inverse_t, by_row, spots, place, *labels)
    edges = trade(*call(lines_kernel, [y_msg, y_msg], n_in=2)(flags, velocity), *msgs)
    sums = call(
        restrict_kernel, [((32, 128), F32)], [pltpu.VMEM((NP, 3, 8, 128), F32)], n_in=13
    )(k_high, flags, force_e, weight, velocity, mult, mult_up, agg, coarse_diag.reshape(1, 128), *edges)[0]
    sums = add(sums, lax.ppermute(sums, "gz", swaps("gz", 0)))
    above = by_core(sums, (-1, 0, 2), (-1, 0, 0))
    across = lax.ppermute(sums, "gz", ring("gz", 2))
    kept, passed = call(gather_sums_kernel, [((32, 128), F32), ((24, 128), F32)], n_in=3)(
        sums, above, across
    )
    swapped = lax.ppermute(passed, "gz", swaps("gz", 0))
    iterate = call(solve_kernel, [((8, NAGG), F32)], [pltpu.VMEM((8, NAGG), F32)], n_in=5)(
        kept, passed, swapped, k_high, k_low
    )[0]
    got = [
        by_core(iterate, (1, -1, 0), (1, 1, 0)),
        by_core(iterate, (1, 0, 0), (0, 1, 0)),
        by_core(iterate, (0, -1, 0), (0, 1, 0)),
    ]
    got = call(join_kernel, [((24, NAGG), F32)], n_in=3)(*got)[0]
    swapped = lax.ppermute(got, "gz", swaps("gz", 0))
    velocity, mult, mult_up, *msgs = call(
        third_sweep_kernel, [field, plane, plane, z_msg, ((LINES + 8, 128), F32)],
        [pltpu.VMEM((NP, 3, 8, 128), F32)], n_in=24,
    )(
        flags, force_e, weight, inverse, velocity, mult, mult_up, face, inverse_t, by_row, spots, place,
        *edges, *labels, agg, iterate, got, swapped,
    )
    edges = trade(*call(lines_kernel, [y_msg, y_msg], n_in=2)(flags, velocity), *msgs)
    head, tail, mult = call(
        last_sweep_kernel, [((3, 16 - RET, 8, 128), F32), ((3, RET, 8, 128), F32), plane],
        [pltpu.VMEM((NP, 3, 8, 128), F32), pltpu.VMEM((3, 8, 128), F32)], n_in=16,
    )(flags, force_e, weight, inverse, velocity, mult, mult_up, face, inverse_t, by_row, spots, place, *edges)
    tail = lax.ppermute(tail, "gx", ring("gx", -1))
    shapes = [pltpu.HBM((3, 16, 8, 128), F32), pltpu.HBM((3, 8, 128), F32)]
    velocity, mult = pl.pallas_call(
        write_head_kernel, out_shape=shapes, in_specs=[VMEM] * 2, out_specs=[HBM] * 2,
        scratch_shapes=[pltpu.SemaphoreType.DMA((2,))],
        compiler_params=pltpu.CompilerParams(vmem_limit_bytes=12 * 1024 * 1024),
    )(keep(head), keep(mult))
    velocity = pl.pallas_call(
        write_tail_kernel, out_shape=shapes[0], in_specs=[VMEM, HBM], out_specs=HBM,
        scratch_shapes=[pltpu.SemaphoreType.DMA], input_output_aliases={1: 0},
        compiler_params=pltpu.CompilerParams(vmem_limit_bytes=12 * 1024 * 1024),
    )(keep(tail), pltpu.with_memory_space_constraint(velocity, pltpu.HBM))
    return velocity, mult[None]


def solution(mesh):
    in_specs = (
        P(None, "gx", "gy", "gz"),
        P("gx", "gy", "gz"),
        P("gx", "gy", "gz", None, None),
        P("gx", "gy", "gz", None, None),
        P("gx", "gy", "gz", None),
        P("gx", "gy", "gz"),
        P("gx", "gy", "gz", None),
        P("gx", "gy", "gz"),
    )
    out_specs = (P(None, "gx", "gy", "gz"), P("gx", None, "gy", "gz"))
    return jax.shard_map(shards, mesh=mesh, in_specs=in_specs, out_specs=out_specs, check_vma=False)
```

```python
import functools

import jax
import jax.numpy as jnp
from jax import lax
from jax.experimental import pallas as pl
from jax.experimental.pallas import tpu as pltpu
from jax.sharding import PartitionSpec as P

BLK = 64
NAGG = 512
TAIL = 7
HEAD = 15
NP = TAIL + HEAD
ROWS = 24
LINES = 3 * ROWS
LOW = TAIL
UPP = TAIL - 1
RET = 4
COARSE_OMEGA = 0.8
PROLONG_GAIN = 0.5
F32 = jnp.float32
BF16 = jnp.bfloat16

VMEM = pl.BlockSpec(memory_space=pltpu.VMEM)
SMEM = pl.BlockSpec(memory_space=pltpu.SMEM)
HBM = pl.BlockSpec(memory_space=pltpu.HBM)


def keep(x):
    return pltpu.with_memory_space_constraint(x, pltpu.VMEM)


def call(body, outs, scratch=(), n_smem=0, n_in=0, n_far=0, limit=12, results=()):
    kernel = pl.pallas_call(
        body,
        out_shape=[jax.ShapeDtypeStruct(s, d) if i in results else pltpu.VMEM(s, d) for i, (s, d) in enumerate(outs)],
        in_specs=[SMEM] * n_smem + [VMEM] * n_in + [HBM] * n_far,
        out_specs=[VMEM] * len(outs),
        scratch_shapes=list(scratch),
        compiler_params=pltpu.CompilerParams(vmem_limit_bytes=limit * 1024 * 1024),
    )

    def run(*args):
        near = n_smem + n_in
        far = [pltpu.with_memory_space_constraint(x, pltpu.HBM) for x in args[near:]]
        held = [keep(x) for x in args[n_smem:near]]
        return kernel(*args[:n_smem], *held, *far)

    return run


def prepare_kernel(flags, blocks, index, count, by_row, spots, place, near, piece, lists, index_near, count_near, sems):
    copies = [
        pltpu.make_async_copy(blocks.at[:, pl.ds(1024 * i, 1024)], near.at[i], sems.at[i]) for i in range(4)
    ]
    for copy in copies:
        copy.start()
    zero = jnp.zeros((8, 128), F32)
    lane = lax.broadcasted_iota(jnp.int32, (8, 128), 1)
    spot = lane & 31
    source = jnp.where(spot < 24, 2 * spot + (lax.shift_right_logical(lane, 5) & 1), 0)
    lists[...] = jnp.zeros((8, 128), jnp.int32)
    small = [
        pltpu.make_async_copy(index, index_near, sems.at[4]),
        pltpu.make_async_copy(count, count_near, sems.at[5]),
    ]
    for copy in small:
        copy.start()
    for copy in small:
        copy.wait()
    lists[0:4, 0:48] = index_near[...]
    lists[4:5, 0:48] = count_near[...]

    def pick(row):
        full = jnp.broadcast_to(lists[row : row + 1, :], (8, 128))
        return jnp.take_along_axis(full, source, axis=1, mode="promise_in_bounds")

    used = pick(4)
    down = lax.broadcasted_iota(jnp.int32, (128, 128), 0) & 63
    for tile in range(2):
        k = 2 * tile + lax.shift_right_logical(lane, 6)
        block = jnp.where(lane < 64, pick(2 * tile), pick(2 * tile + 1))
        at = (block & 1) * 32 + lax.shift_right_logical(block, 1)
        live = (k < used) & (spot < 24)
        at = jnp.where(live, at, 31)
        spots[:, 128 * tile : 128 * tile + 128] = at
        hit = (down == at[0:1]) & (at[0:1] != 31)
        place[:, 128 * tile : 128 * tile + 128] = jnp.where(hit, 1.0, 0.0).astype(BF16)

    for i, copy in enumerate(copies):
        copy.wait()

        def chunk(g, _):
            for s in range(2):
                at = pl.multiple_of((2 * g + s) * 128, 128)
                piece[s] = near[i, :, pl.ds(at, 128)]
                for tile in range(2):
                    rows = []
                    for k in (2 * tile, 2 * tile + 1):
                        for par in range(2):
                            rows += [piece[s, pl.ds(4 * par + k, 24, stride=8), :], zero]
                    by_row[tile, pl.ds(1024 * i + at, 128), :] = jnp.concatenate(rows, 0).T
            return 0

        lax.fori_loop(0, 4, chunk, 0)


def split(x):
    high = x.astype(BF16)
    return high, (x - high.astype(F32)).astype(BF16)


def fold(parts):
    sub = lax.broadcasted_iota(jnp.int32, (8, 128), 0)
    m = sub < 4
    a = [
        jnp.where(m, parts[i], parts[i + 4]) + pltpu.roll(jnp.where(m, parts[i + 4], parts[i]), 4, 0)
        for i in range(4)
    ]
    m = (sub & 2) == 0
    a = [
        jnp.where(m, a[i], pltpu.roll(a[i + 2], 2, 0)) + jnp.where(m, pltpu.roll(a[i], 6, 0), a[i + 2])
        for i in range(2)
    ]
    m = (sub & 1) == 0
    return jnp.where(m, a[0], pltpu.roll(a[1], 1, 0)) + jnp.where(m, pltpu.roll(a[0], 7, 0), a[1])


def project(by_row, spots, values):
    total = None
    for tile in range(2):
        picked = [
            jnp.take_along_axis(
                values[8 * g : 8 * g + 8], spots[:, 128 * tile : 128 * tile + 128], axis=1,
                mode="promise_in_bounds",
            )
            for g in range(8)
        ]
        rows = []
        for group in range(8):
            parts = []
            for s in range(8):
                base = 64 * (8 * group + s)
                terms = [by_row[tile, base + 8 * g : base + 8 * g + 8, :] * picked[g] for g in range(8)]
                while len(terms) > 1:
                    terms = [terms[i] + terms[i + 1] for i in range(0, len(terms), 2)]
                parts.append(terms[0])
            rows.append(fold(parts))
        part = jnp.concatenate(rows, 0)
        total = part if total is None else total + part
    return total + pltpu.roll(total, 64, 1)


def project_back(by_row, place, values):
    first = second = jnp.zeros((64, 128), F32)
    for i in range(64):
        row = jnp.broadcast_to(values[i : i + 1], (64, 128))
        first = first + by_row[0, 64 * i : 64 * i + 64, :] * row
        second = second + by_row[1, 64 * i : 64 * i + 64, :] * row
    high, low = split(jnp.concatenate([first, second], 1))
    both = lax.dot_general(
        jnp.concatenate([high, low], 0), place[...], (((1,), (1,)), ((), ())), preferred_element_type=F32
    )
    return both[0:64] + both[64:128]


def turn(lower, upper):
    left = lax.broadcasted_iota(jnp.int32, (24, 128), 1) < 64
    even = jnp.where(left, lower, pltpu.roll(upper, 64, 1))
    odd = jnp.where(left, pltpu.roll(lower, 64, 1), upper)
    zero = jnp.zeros((8, 128), F32)
    turned = jnp.concatenate([even, zero, odd, zero, even, zero, odd, zero], 0).T
    return turned[0:64], turned[64:128]


def turn_back(lower, upper):
    left = lax.broadcasted_iota(jnp.int32, (24, 128), 1) < 64
    rows = jnp.concatenate([lower, upper], 0).T
    even, odd = rows[0:24], rows[32:56]
    return (
        jnp.where(left, even, pltpu.roll(odd, 64, 1)),
        jnp.where(left, pltpu.roll(even, 64, 1), odd),
    )


def solve_interface(lower, upper, face, inverse, mortar):
    by_row, spots, place = mortar
    low_t, upp_t = turn(lower, upper)
    rhs = low_t - project(by_row, spots, upp_t)
    first = face * rhs
    back = project_back(by_row, place, first) * inverse
    rest = 0.6 * rhs - project(by_row, spots, back)
    increment = first + face * rest
    return turn_back(increment, project_back(by_row, place, increment))


def tall(plane):
    return jnp.concatenate([plane] * 3, 0)


def yes(flags, row, shape):
    line = jnp.concatenate([flags[row : row + 1, :]] * (shape[1] // 128), 1)
    return jnp.broadcast_to(line, shape) == 1


def sides(flags, y_first, y_second, z_first, z_second):
    tall_shape, zero = (LINES, 128), jnp.zeros((LINES, 128), F32)
    y_even, z_even = yes(flags, 0, tall_shape), yes(flags, 1, (8, 128))
    a, b, c, d = y_first[0:LINES], y_second[0:LINES], z_first[0:8, 0:128], z_second[0:8]
    return (
        jnp.where(yes(flags, 2, tall_shape), jnp.where(y_even, b, a), zero),
        jnp.where(yes(flags, 3, tall_shape), jnp.where(y_even, a, b), zero),
        jnp.where(yes(flags, 4, (8, 128)), jnp.where(z_even, d, c), zero[0:8]),
        jnp.where(yes(flags, 5, (8, 128)), jnp.where(z_even, c, d), zero[0:8]),
    )


def place_of(p, c):
    return ROWS * c + p


def residual_of(p, c, force, weight, velocity, halo):
    y_low, y_high, z_low, z_high = halo
    i = place_of(p, c)
    sub = lax.broadcasted_iota(jnp.int32, (8, 128), 0)
    lane = lax.broadcasted_iota(jnp.int32, (8, 128), 1)
    v = velocity[p, c]
    total = force[p, c] - weight[p] * v
    if p not in (0, LOW):
        total = total + velocity[p - 1, c]
    if p not in (NP - 1, UPP):
        total = total + velocity[p + 1, c]
    total = total + jnp.where(sub == 0, y_low[i : i + 1], pltpu.roll(v, 1, 0))
    total = total + jnp.where(sub == 7, y_high[i : i + 1], pltpu.roll(v, 7, 0))
    total = total + jnp.where(lane == 0, pltpu.roll(z_low, (128 - i) % 128, 1), pltpu.roll(v, 1, 1))
    total = total + jnp.where(lane == 127, pltpu.roll(z_high, 127 - i, 1), pltpu.roll(v, 127, 1))
    return total


def write_lines(flags, get, y_first, y_second, row=0, count=3):
    y_even = yes(flags, 0, (1, 128))
    for c in range(count):
        for p in range(NP):
            v = get(p, c)
            i = row + place_of(p, c)
            y_first[i : i + 1] = jnp.where(y_even, v[7:8], v[0:1])
            y_second[i : i + 1] = jnp.where(y_even, v[0:1], v[7:8])
        i = row + place_of(NP, c)
        y_first[i : i + ROWS - NP] = jnp.zeros((ROWS - NP, 128), F32)
        y_second[i : i + ROWS - NP] = jnp.zeros((ROWS - NP, 128), F32)


def write_columns(flags, get, z_first, z_second, row=0):
    z_even = yes(flags, 1, (8, 128))
    lane = lax.broadcasted_iota(jnp.int32, (8, 128), 1)
    first = jnp.zeros((8, 128), F32)
    last = first
    for c in range(3):
        for p in range(NP):
            v, i = get(p, c), place_of(p, c)
            first = jnp.where(lane == i, pltpu.roll(v, i, 1) if i else v, first)
            last = jnp.where(lane == i, pltpu.roll(v, i + 1, 1), last)
    z_first[row : row + 8] = jnp.where(z_even, last, first)
    z_second[row : row + 8] = jnp.where(z_even, first, last)


def first_sweep_kernel(
    flags, force_in, kappa_in, agg_in, tail, by_row, spots, place,
    force, weight, inverse, agg, velocity, mult, mult_up, face, inverse_t, z1, z2,
):
    for p in range(NP):
        here = p - TAIL
        kappa = tail[p, 3] if here < 0 else kappa_in[here]
        w = 6.0 + kappa
        weight[p] = w
        inverse[p] = 1.0 / (1.5 * w)
        agg[p] = tail[p, 4].astype(jnp.int32) if here < 0 else agg_in[here]
        for c in range(3):
            f = tail[p, c] if here < 0 else force_in[c, here]
            force[p, c] = f
            velocity[p, c] = f * inverse[p]
    low_w, upp_inv = turn(tall(weight[LOW]), tall(inverse[UPP]))
    face[...] = 0.6 * low_w
    inverse_t[...] = upp_inv
    lower = velocity[LOW].reshape(24, 128)
    upper = velocity[UPP].reshape(24, 128)
    increment, pulled = solve_interface(
        lower, upper, face[...], upp_inv, (by_row, spots, place)
    )
    mult[...] = increment.reshape(3, 8, 128)
    mult_up[...] = pulled.reshape(3, 8, 128)
    velocity[LOW] = (lower - increment * tall(inverse[LOW])).reshape(3, 8, 128)
    velocity[UPP] = (upper + pulled * tall(inverse[UPP])).reshape(3, 8, 128)
    write_columns(flags, lambda p, c: velocity[p, c], z1, z2)
    write_columns(flags, lambda p, c: agg[p].astype(F32), z1, z2, 8)


def lines_kernel(flags, velocity, y1, y2):
    write_lines(flags, lambda p, c: velocity[p, c], y1, y2)


def lines_and_labels_kernel(flags, velocity, agg, y1, y2):
    write_lines(flags, lambda p, c: velocity[p, c], y1, y2)
    write_lines(flags, lambda p, c: agg[p].astype(F32), y1, y2, LINES, 1)


def sweep(
    flags, force, weight, inverse, velocity, mult, mult_up, face, inverse_t, by_row, spots, place,
    halo, out, out_mult, out_up,
):
    def residuals(p):
        return jnp.concatenate([residual_of(p, c, force, weight, velocity, halo) for c in range(3)], 0)

    res_low = residuals(LOW) - mult[...].reshape(24, 128)
    res_upp = residuals(UPP) + mult_up[...].reshape(24, 128)
    inv_low, inv_upp = tall(inverse[LOW]), tall(inverse[UPP])
    lower = velocity[LOW].reshape(24, 128) + res_low * inv_low
    upper = velocity[UPP].reshape(24, 128) + res_upp * inv_upp
    increment, pulled = solve_interface(
        lower, upper, face[...], inverse_t[...], (by_row, spots, place)
    )
    out_mult[...] = mult[...] + increment.reshape(3, 8, 128)
    out_up[...] = mult_up[...] + pulled.reshape(3, 8, 128)
    for p in range(NP):
        if p in (LOW, UPP):
            continue
        for c in range(3):
            out[p, c] = velocity[p, c] + residual_of(p, c, force, weight, velocity, halo) * inverse[p]
    out[LOW] = (lower - increment * inv_low).reshape(3, 8, 128)
    out[UPP] = (upper + pulled * inv_upp).reshape(3, 8, 128)


def second_sweep_kernel(
    flags, force, weight, inverse, velocity, mult, mult_up, face, inverse_t, by_row, spots, place,
    z2, y1, y2, z1, out, out_mult, out_up, oz1, oz2,
):
    halo = sides(flags, y1, y2, z1, z2)
    sweep(
        flags, force, weight, inverse, velocity, mult, mult_up, face, inverse_t, by_row, spots, place,
        halo, out, out_mult, out_up,
    )
    write_columns(flags, lambda p, c: out[p, c], oz1, oz2)


def third_sweep_kernel(
    flags, force, weight, inverse, old, mult, mult_up, face, inverse_t, by_row, spots, place,
    z2, y1, y2, z1, az2, ay1, ay2, az1, agg, iterate, got, swapped,
    out, out_mult, out_up, oz1, oz2, velocity,
):
    core_zero = yes(flags, 1, (24, NAGG))
    a = jnp.where(core_zero, got[...], swapped[...])
    b = jnp.where(core_zero, swapped[...], got[...])
    own, prev = table(iterate[...]), table(a[8:16])
    low, low_prev = table(b[8:16]), table(b[0:8])
    high, high_prev = table(a[16:24]), table(a[0:8])
    for p in range(NP):
        at = where_in(agg[p])
        for c in range(3):
            velocity[p, c] = old[p, c] + pick((prev if p < TAIL else own)[c], at)

    y_low, y_high, z_low, z_high = sides(flags, y1, y2, z1, z2)
    y_even, z_even = yes(flags, 0, (ROWS, 128)), yes(flags, 1, (8, 128))
    ay1, ay2, az1, az2 = ay1[LINES : LINES + ROWS], ay2[LINES : LINES + ROWS], az1[0:8, 128:256], az2[8:16]
    sub = lax.broadcasted_iota(jnp.int32, (8, 128), 0)
    lane = lax.broadcasted_iota(jnp.int32, (8, 128), 1)

    def lines(values, labels, mine, below, flag):
        labels = labels.astype(jnp.int32)
        parts = []
        for c in range(3):
            for block in range(ROWS // 8):
                at = where_in(labels[8 * block : 8 * block + 8])
                extra = pick(mine[c], at)
                if block == 0:
                    extra = jnp.where(sub < TAIL, pick(below[c], at), extra)
                row = place_of(8 * block, c)
                parts.append(jnp.where(yes(flags, flag, (8, 128)), values[row : row + 8] + extra, 0.0))
        return jnp.concatenate(parts, 0)

    def column(values, labels, flag):
        at = where_in(labels.astype(jnp.int32))
        extra = jnp.zeros((8, 128), F32)
        for c in range(3):
            here = lane - ROWS * c
            extra = jnp.where((here >= 0) & (here < TAIL), pick(prev[c], at), extra)
            extra = jnp.where((here >= TAIL) & (here < NP), pick(own[c], at), extra)
        return jnp.where(yes(flags, flag, (8, 128)), values + extra, 0.0)

    halo = (
        lines(y_low, jnp.where(y_even, ay2, ay1), low, low_prev, 2),
        lines(y_high, jnp.where(y_even, ay1, ay2), high, high_prev, 3),
        column(z_low, jnp.where(z_even, az2, az1), 4),
        column(z_high, jnp.where(z_even, az1, az2), 5),
    )
    sweep(
        flags, force, weight, inverse, velocity, mult, mult_up, face, inverse_t, by_row, spots, place,
        halo, out, out_mult, out_up,
    )
    write_columns(flags, lambda p, c: out[p, c], oz1, oz2)


def last_sweep_kernel(
    flags, force, weight, inverse, velocity, mult, mult_up, face, inverse_t, by_row, spots, place,
    z2, y1, y2, z1, head, tail, out_mult, out, out_up,
):
    halo = sides(flags, y1, y2, z1, z2)
    sweep(
        flags, force, weight, inverse, velocity, mult, mult_up, face, inverse_t, by_row, spots, place,
        halo, out, out_mult, out_up,
    )
    for c in range(3):
        for p in range(16 - RET):
            head[c, p] = out[LOW + p, c]
        for p in range(RET):
            tail[c, p] = out[TAIL - RET + p, c]


def restrict_kernel(
    after, flags, force, weight, velocity, mult, mult_up, agg, diag, z2, y1, y2, z1, out, res,
):
    halo = sides(flags, y1, y2, z1, z2)
    for p in range(TAIL - 3, NP - 2):
        for c in range(3):
            r = residual_of(p, c, force, weight, velocity, halo)
            if p == LOW:
                r = r - mult[c]
            if p == UPP:
                r = r + mult_up[c]
            res[p, c] = r
    down = lax.broadcasted_iota(jnp.int32, (64, 128), 0)
    sub = lax.broadcasted_iota(jnp.int32, (8, 128), 0)

    def plane(p, total):
        labels = agg[p]
        lows = labels & 63
        highs = lax.shift_right_logical(labels, 6)
        values = []
        for c in range(3):
            r = res[p, c]
            high = r.astype(BF16).astype(F32)
            values += [high, r - high]
        for pair in range(4):
            tables, terms = [], []
            for y in (2 * pair, 2 * pair + 1):
                tables.append(jnp.where(down == lows[y : y + 1], 1.0, 0.0).astype(BF16))
                here = highs[y : y + 1] == sub
                terms.append(jnp.concatenate([jnp.where(here, v[y : y + 1], 0.0) for v in values], 0).astype(BF16))
            total = total + lax.dot_general(
                jnp.concatenate(tables, 1), jnp.concatenate(terms, 1), (((1,), (1,)), ((), ())),
                preferred_element_type=F32,
            )
        return total

    def four(i, total):
        for s in range(4):
            total = plane(LOW + 4 * i + s, total)
        return total

    below = jnp.zeros((64, 48), F32)
    for p in range(TAIL - 3, TAIL):
        below = plane(p, below)
    own = lax.fori_loop(0, 3, four, plane(NP - 3, jnp.zeros((64, 48), F32)))
    both = jnp.concatenate([own, below], 0)
    turned = jnp.concatenate([both, jnp.zeros((128, 80), F32)], 1).T
    for c in range(3):
        out[8 * c : 8 * c + 8] = turned[16 * c : 16 * c + 8] + turned[16 * c + 8 : 16 * c + 16]
    out[24:32] = jnp.where(sub == flags[6:7], jnp.broadcast_to(diag[...], (8, 128)), 0.0)


def gather_sums_kernel(mine, above, across, kept, passed):
    kept[...] = mine[...] + across[...]
    lane = lax.broadcasted_iota(jnp.int32, (24, 128), 1)
    passed[...] = jnp.where(lane < 64, pltpu.roll(above[0:24], 64, 1), 0.0)


def add_kernel(one, two, out):
    out[...] = one[...] + two[...]


def join_kernel(a, b, c, out):
    out[0:8], out[8:16], out[16:24] = a[...], b[...], c[...]


def add(one, two):
    return call(add_kernel, [(one.shape, F32)], n_in=2)(one, two)[0]


def pack_kernel(force, kappa, agg, matrix, out, force_near, kappa_near, agg_near, rows, more_rows, flags, sems):
    copies = [
        pltpu.make_async_copy(far, near, sems.at[i])
        for i, (far, near) in enumerate(
            (
                (force, force_near), (kappa, kappa_near), (agg, agg_near),
                (matrix.at[pl.ds(0, 64)], rows), (matrix.at[pl.ds(64, 64)], more_rows),
            )
        )
    ]
    for copy in copies:
        copy.start()
    gy, gz = lax.axis_index("gy"), lax.axis_index("gz")
    ny, nz = lax.axis_size("gy"), lax.axis_size("gz")
    facts = (gy % 2 == 1, gz % 2 == 0, gy > 0, gy < ny - 1, gz > 0, gz < nz - 1, gz, gz < nz // 2)
    for row, fact in enumerate(facts):
        flags[row : row + 1, :] = jnp.full((1, 128), fact.astype(jnp.int32), jnp.int32)
    for copy in copies:
        copy.wait()
    start = kappa.shape[0] - TAIL
    for p in range(TAIL):
        for c in range(3):
            out[p, c] = force_near[c, start + p]
        out[p, 3] = kappa_near[start + p]
        out[p, 4] = agg_near[start + p].astype(F32)


def stack_kernel(columns, one, two, three, four, out):
    out[0:8, 0:128], out[0:8, 128:256] = columns[0:8], columns[8:16]
    out[0:8, 256:NAGG] = jnp.zeros((8, NAGG - 256), F32)
    for i, part in enumerate((one, two, three, four)):
        out[8 + 64 * i : 72 + 64 * i] = part[...]


def split_matrix_kernel(flags, mine, other, high, low):
    core_zero, first_half = yes(flags, 1, (256, NAGG)), yes(flags, 7, (128, NAGG))
    one, two = mine[8:264], other[8:264]
    sets = jnp.where(core_zero, one, two), jnp.where(core_zero, two, one)
    for b in range(4):
        rows = sets[b % 2]
        near, far = (rows[0:128], rows[128:256]) if b < 2 else (rows[128:256], rows[0:128])
        a = jnp.where(first_half, near, far).T
        h = a.astype(BF16)
        high[:, 128 * b : 128 * b + 128] = h
        low[:, 128 * b : 128 * b + 128] = (a - h.astype(F32)).astype(BF16)


def solve_kernel(kept, passed, swapped, high, low, out, rhs):
    sums = kept[0:24] + passed[...] + swapped[...]
    other = pltpu.roll(sums, 64, 1)
    rhs[...] = jnp.zeros((8, NAGG), F32)
    left = lax.broadcasted_iota(jnp.int32, (1, 128), 1) < 64
    for c in range(3):
        for t in range(4):
            at = 8 * c + 2 * t
            rhs[c : c + 1, 128 * t : 128 * t + 128] = jnp.where(left, sums[at : at + 1], other[at + 1 : at + 2])
    gain = (16 * 8 * 512 / NAGG) ** -0.5
    scale = jnp.concatenate([kept[24 + b : 25 + b] for b in range(4)], 1)
    step = jnp.broadcast_to(COARSE_OMEGA / scale, (8, NAGG))
    start = (rhs[...] * gain) * step
    x = start
    for _ in range(3):
        xh, xl = split(x)
        both = jnp.concatenate([xh, xl], 0)
        first = jnp.dot(both, high[...], preferred_element_type=F32)
        second = jnp.dot(xh, low[...], preferred_element_type=F32)
        product = first[0:8] + first[8:16] + second
        x = (1.0 - COARSE_OMEGA) * x + (start - step * product)
    out[...] = x


def table(rows):
    return [
        [jnp.broadcast_to(rows[c : c + 1, 128 * t : 128 * t + 128], (8, 128)) * PROLONG_GAIN for t in range(4)]
        for c in range(3)
    ]


def where_in(labels):
    return labels & 127, lax.shift_right_logical(labels, 7)


def pick(rows, at):
    lane, tile = at
    got = [jnp.take_along_axis(row, lane, axis=1, mode="promise_in_bounds") for row in rows]
    return jnp.where(tile < 2, jnp.where(tile == 0, got[0], got[1]), jnp.where(tile == 2, got[2], got[3]))


def write_head_kernel(head, mult, velocity, out_mult, sems):
    copies = [
        pltpu.make_async_copy(head, velocity.at[:, pl.ds(0, 16 - RET)], sems.at[0]),
        pltpu.make_async_copy(mult, out_mult, sems.at[1]),
    ]
    for copy in copies:
        copy.start()
    for copy in copies:
        copy.wait()


def write_tail_kernel(tail, before, velocity, sem):
    copy = pltpu.make_async_copy(tail, velocity.at[:, pl.ds(16 - RET, RET)], sem)
    copy.start()
    copy.wait()


def ring(axis, by):
    n = lax.axis_size(axis)
    return [(i, (i + by) % n) for i in range(n)]


def swaps(axis, first):
    n = lax.axis_size(axis)
    pairs = []
    for i in range(first, first + n, 2):
        a, b = i % n, (i + 1) % n
        pairs += [(a, b), (b, a)]
    return pairs


def trade(y1, y2, z1, z2):
    return [
        lax.ppermute(z2, "gz", swaps("gz", 1)),
        lax.ppermute(y1, "gy", swaps("gy", 1)),
        lax.ppermute(y2, "gy", swaps("gy", 0)),
        lax.ppermute(z1, "gz", swaps("gz", 0)),
    ]


def by_core(x, rule_zero, rule_one):
    nx, ny, nz = lax.axis_size("gx"), lax.axis_size("gy"), lax.axis_size("gz")
    pairs = []
    for g in range(nx):
        for y in range(ny):
            for z in range(nz):
                dx, dy, dz = rule_one if z % 2 else rule_zero
                to = (((g + dx) % nx) * ny + (y + dy) % ny) * nz + (z + dz) % nz
                pairs.append(((g * ny + y) * nz + z, to))
    return lax.ppermute(x, ("gx", "gy", "gz"), pairs)


def shards(force, kappa, mortar_blocks, mortar_index, mortar_count, agg_map, coarse_matrix, coarse_diag):
    tail_in, force, kappa, agg_map, rows, more_rows, flags = call(
        pack_kernel,
        [((TAIL, 5, 8, 128), F32), (force.shape, F32), (kappa.shape, F32), (agg_map.shape, jnp.int32),
         ((64, NAGG), F32), ((64, NAGG), F32), ((8, 128), jnp.int32)],
        [pltpu.SemaphoreType.DMA((5,))],
        n_far=4,
    )(force, kappa, agg_map, coarse_matrix.reshape(128, NAGG))
    tail_in = lax.ppermute(tail_in, "gx", ring("gx", 1))
    half, more_half = [lax.ppermute(x, "gz", ring("gz", 2)) for x in (rows, more_rows)]

    by_row, spots, place = call(
        prepare_kernel,
        [((2, 4096, 128), F32), ((8, 256), jnp.int32), ((128, 256), BF16)],
        [pltpu.VMEM((4, 192, 1024), F32), pltpu.VMEM((2, 192, 128), F32), pltpu.VMEM((8, 128), jnp.int32),
         pltpu.VMEM((4, 48), jnp.int32), pltpu.VMEM((1, 48), jnp.int32), pltpu.SemaphoreType.DMA((6,))],
        n_in=1,
        n_far=3,
    )(
        flags,
        mortar_blocks.reshape(192, 4096),
        jnp.transpose(mortar_index.reshape(48, 4), (1, 0)),
        mortar_count.reshape(1, 48),
    )

    field = ((NP, 3, 8, 128), F32)
    plane = ((3, 8, 128), F32)
    turned = ((64, 128), F32)
    y_msg, z_msg = ((LINES, 128), F32), ((8, 128), F32)
    y_more, z_more = ((LINES + ROWS, 128), F32), ((16, 128), F32)
    out = call(
        first_sweep_kernel,
        [field, ((NP, 8, 128), F32), ((NP, 8, 128), F32), ((NP, 8, 128), jnp.int32), field, plane, plane,
         turned, turned, z_more, ((LINES + ROWS + 8, 128), F32)],
        n_in=8,
    )(flags, force, kappa, agg_map, tail_in, by_row, spots, place)
    force_e, weight, inverse, agg, velocity, mult, mult_up, face, inverse_t = out[:9]
    lines = call(lines_and_labels_kernel, [y_more, y_more], n_in=3)(flags, velocity, agg)
    stacked = call(stack_kernel, [((264, NAGG), F32)], n_in=5)(out[9], rows, more_rows, half, more_half)[0]
    labels = trade(*lines, stacked, out[10])
    k_high, k_low = call(split_matrix_kernel, [((NAGG, NAGG), BF16)] * 2, n_in=3)(flags, stacked, labels[3])
    velocity, mult, mult_up, *msgs = call(
        second_sweep_kernel, [field, plane, plane, z_msg, ((LINES + 8, 128), F32)], n_in=16
    )(flags, force_e, weight, inverse, velocity, mult, mult_up, face, inverse_t, by_row, spots, place, *labels)
    edges = trade(*call(lines_kernel, [y_msg, y_msg], n_in=2)(flags, velocity), *msgs)
    sums = call(
        restrict_kernel, [((32, 128), F32)], [pltpu.VMEM((NP, 3, 8, 128), F32)], n_in=13
    )(k_high, flags, force_e, weight, velocity, mult, mult_up, agg, coarse_diag.reshape(1, 128), *edges)[0]
    sums = add(sums, lax.ppermute(sums, "gz", swaps("gz", 0)))
    above = by_core(sums, (-1, 0, 2), (-1, 0, 0))
    across = lax.ppermute(sums, "gz", ring("gz", 2))
    kept, passed = call(gather_sums_kernel, [((32, 128), F32), ((24, 128), F32)], n_in=3)(
        sums, above, across
    )
    swapped = lax.ppermute(passed, "gz", swaps("gz", 0))
    iterate = call(solve_kernel, [((8, NAGG), F32)], [pltpu.VMEM((8, NAGG), F32)], n_in=5)(
        kept, passed, swapped, k_high, k_low
    )[0]
    got = [
        by_core(iterate, (1, -1, 0), (1, 1, 0)),
        by_core(iterate, (1, 0, 0), (0, 1, 0)),
        by_core(iterate, (0, -1, 0), (0, 1, 0)),
    ]
    got = call(join_kernel, [((24, NAGG), F32)], n_in=3)(*got)[0]
    swapped = lax.ppermute(got, "gz", swaps("gz", 0))
    velocity, mult, mult_up, *msgs = call(
        third_sweep_kernel, [field, plane, plane, z_msg, ((LINES + 8, 128), F32)],
        [pltpu.VMEM((NP, 3, 8, 128), F32)], n_in=24,
    )(
        flags, force_e, weight, inverse, velocity, mult, mult_up, face, inverse_t, by_row, spots, place,
        *edges, *labels, agg, iterate, got, swapped,
    )
    edges = trade(*call(lines_kernel, [y_msg, y_msg], n_in=2)(flags, velocity), *msgs)
    head, tail, mult = call(
        last_sweep_kernel, [((3, 16 - RET, 8, 128), F32), ((3, RET, 8, 128), F32), plane],
        [pltpu.VMEM((NP, 3, 8, 128), F32), pltpu.VMEM((3, 8, 128), F32)], n_in=16,
    )(flags, force_e, weight, inverse, velocity, mult, mult_up, face, inverse_t, by_row, spots, place, *edges)
    tail = lax.ppermute(tail, "gx", ring("gx", -1))
    shapes = [pltpu.HBM((3, 16, 8, 128), F32), pltpu.HBM((3, 8, 128), F32)]
    velocity, mult = pl.pallas_call(
        write_head_kernel, out_shape=shapes, in_specs=[VMEM] * 2, out_specs=[HBM] * 2,
        scratch_shapes=[pltpu.SemaphoreType.DMA((2,))],
        compiler_params=pltpu.CompilerParams(vmem_limit_bytes=12 * 1024 * 1024),
    )(keep(head), keep(mult))
    velocity = pl.pallas_call(
        write_tail_kernel, out_shape=shapes[0], in_specs=[VMEM, HBM], out_specs=HBM,
        scratch_shapes=[pltpu.SemaphoreType.DMA], input_output_aliases={1: 0},
        compiler_params=pltpu.CompilerParams(vmem_limit_bytes=12 * 1024 * 1024),
    )(keep(tail), pltpu.with_memory_space_constraint(velocity, pltpu.HBM))
    return velocity, mult[None]


def solution(mesh):
    in_specs = (
        P(None, "gx", "gy", "gz"),
        P("gx", "gy", "gz"),
        P("gx", "gy", "gz", None, None),
        P("gx", "gy", "gz", None, None),
        P("gx", "gy", "gz", None),
        P("gx", "gy", "gz"),
        P("gx", "gy", "gz", None),
        P("gx", "gy", "gz"),
    )
    out_specs = (P(None, "gx", "gy", "gz"), P("gx", None, "gy", "gz"))
    return jax.shard_map(shards, mesh=mesh, in_specs=in_specs, out_specs=out_specs, check_vma=False)
```

```python
import functools

import jax
import jax.numpy as jnp
from jax import lax
from jax.experimental import pallas as pl
from jax.experimental.pallas import tpu as pltpu
from jax.sharding import PartitionSpec as P

BLK = 64
NAGG = 512
TAIL = 7
HEAD = 15
NP = TAIL + HEAD
ROWS = 24
LINES = 3 * ROWS
LOW = TAIL
UPP = TAIL - 1
RET = 4
COARSE_OMEGA = 0.8
PROLONG_GAIN = 0.5
F32 = jnp.float32
BF16 = jnp.bfloat16

VMEM = pl.BlockSpec(memory_space=pltpu.VMEM)
SMEM = pl.BlockSpec(memory_space=pltpu.SMEM)
HBM = pl.BlockSpec(memory_space=pltpu.HBM)


def keep(x):
    return pltpu.with_memory_space_constraint(x, pltpu.VMEM)


def call(body, outs, scratch=(), n_smem=0, n_in=0, n_far=0, limit=12, results=()):
    kernel = pl.pallas_call(
        body,
        out_shape=[jax.ShapeDtypeStruct(s, d) if i in results else pltpu.VMEM(s, d) for i, (s, d) in enumerate(outs)],
        in_specs=[SMEM] * n_smem + [VMEM] * n_in + [HBM] * n_far,
        out_specs=[VMEM] * len(outs),
        scratch_shapes=list(scratch),
        compiler_params=pltpu.CompilerParams(vmem_limit_bytes=limit * 1024 * 1024),
    )

    def run(*args):
        near = n_smem + n_in
        far = [pltpu.with_memory_space_constraint(x, pltpu.HBM) for x in args[near:]]
        held = [keep(x) for x in args[n_smem:near]]
        return kernel(*args[:n_smem], *held, *far)

    return run


def prepare_kernel(flags, blocks, index, count, by_row, spots, place, near, piece, lists, index_near, count_near, sems):
    copies = [
        pltpu.make_async_copy(blocks.at[:, pl.ds(1024 * i, 1024)], near.at[i], sems.at[i]) for i in range(4)
    ]
    for copy in copies:
        copy.start()
    zero = jnp.zeros((8, 128), F32)
    lane = lax.broadcasted_iota(jnp.int32, (8, 128), 1)
    spot = lane & 31
    source = jnp.where(spot < 24, 2 * spot + (lax.shift_right_logical(lane, 5) & 1), 0)
    lists[...] = jnp.zeros((8, 128), jnp.int32)
    small = [
        pltpu.make_async_copy(index, index_near, sems.at[4]),
        pltpu.make_async_copy(count, count_near, sems.at[5]),
    ]
    for copy in small:
        copy.start()
    for copy in small:
        copy.wait()
    lists[0:4, 0:48] = index_near[...]
    lists[4:5, 0:48] = count_near[...]

    def pick(row):
        full = jnp.broadcast_to(lists[row : row + 1, :], (8, 128))
        return jnp.take_along_axis(full, source, axis=1, mode="promise_in_bounds")

    used = pick(4)
    down = lax.broadcasted_iota(jnp.int32, (128, 128), 0) & 63
    for tile in range(2):
        k = 2 * tile + lax.shift_right_logical(lane, 6)
        block = jnp.where(lane < 64, pick(2 * tile), pick(2 * tile + 1))
        at = (block & 1) * 32 + lax.shift_right_logical(block, 1)
        live = (k < used) & (spot < 24)
        at = jnp.where(live, at, 31)
        spots[:, 128 * tile : 128 * tile + 128] = at
        hit = (down == at[0:1]) & (at[0:1] != 31)
        place[:, 128 * tile : 128 * tile + 128] = jnp.where(hit, 1.0, 0.0).astype(BF16)

    for i, copy in enumerate(copies):
        copy.wait()

        def chunk(g, _):
            for s in range(2):
                at = pl.multiple_of((2 * g + s) * 128, 128)
                piece[s] = near[i, :, pl.ds(at, 128)]
                for tile in range(2):
                    rows = []
                    for k in (2 * tile, 2 * tile + 1):
                        for par in range(2):
                            rows += [piece[s, pl.ds(4 * par + k, 24, stride=8), :], zero]
                    by_row[tile, pl.ds(1024 * i + at, 128), :] = jnp.concatenate(rows, 0).T
            return 0

        lax.fori_loop(0, 4, chunk, 0)


def split(x):
    high = x.astype(BF16)
    return high, (x - high.astype(F32)).astype(BF16)


def fold(parts):
    sub = lax.broadcasted_iota(jnp.int32, (8, 128), 0)
    m = sub < 4
    a = [
        jnp.where(m, parts[i], parts[i + 4]) + pltpu.roll(jnp.where(m, parts[i + 4], parts[i]), 4, 0)
        for i in range(4)
    ]
    m = (sub & 2) == 0
    a = [
        jnp.where(m, a[i], pltpu.roll(a[i + 2], 2, 0)) + jnp.where(m, pltpu.roll(a[i], 6, 0), a[i + 2])
        for i in range(2)
    ]
    m = (sub & 1) == 0
    return jnp.where(m, a[0], pltpu.roll(a[1], 1, 0)) + jnp.where(m, pltpu.roll(a[0], 7, 0), a[1])


def project(by_row, spots, values):
    total = None
    for tile in range(2):
        picked = [
            jnp.take_along_axis(
                values[8 * g : 8 * g + 8], spots[:, 128 * tile : 128 * tile + 128], axis=1,
                mode="promise_in_bounds",
            )
            for g in range(8)
        ]
        rows = []
        for group in range(8):
            parts = []
            for s in range(8):
                base = 64 * (8 * group + s)
                terms = [by_row[tile, base + 8 * g : base + 8 * g + 8, :] * picked[g] for g in range(8)]
                while len(terms) > 1:
                    terms = [terms[i] + terms[i + 1] for i in range(0, len(terms), 2)]
                parts.append(terms[0])
            rows.append(fold(parts))
        part = jnp.concatenate(rows, 0)
        total = part if total is None else total + part
    return total + pltpu.roll(total, 64, 1)


def project_back(by_row, place, values):
    first = second = jnp.zeros((64, 128), F32)
    for i in range(64):
        row = jnp.broadcast_to(values[i : i + 1], (64, 128))
        first = first + by_row[0, 64 * i : 64 * i + 64, :] * row
        second = second + by_row[1, 64 * i : 64 * i + 64, :] * row
    high, low = split(jnp.concatenate([first, second], 1))
    both = lax.dot_general(
        jnp.concatenate([high, low], 0), place[...], (((1,), (1,)), ((), ())), preferred_element_type=F32
    )
    return both[0:64] + both[64:128]


def turn(lower, upper):
    left = lax.broadcasted_iota(jnp.int32, (24, 128), 1) < 64
    even = jnp.where(left, lower, pltpu.roll(upper, 64, 1))
    odd = jnp.where(left, pltpu.roll(lower, 64, 1), upper)
    zero = jnp.zeros((8, 128), F32)
    turned = jnp.concatenate([even, zero, odd, zero, even, zero, odd, zero], 0).T
    return turned[0:64], turned[64:128]


def turn_back(lower, upper):
    left = lax.broadcasted_iota(jnp.int32, (24, 128), 1) < 64
    rows = jnp.concatenate([lower, upper], 0).T
    even, odd = rows[0:24], rows[32:56]
    return (
        jnp.where(left, even, pltpu.roll(odd, 64, 1)),
        jnp.where(left, pltpu.roll(even, 64, 1), odd),
    )


def solve_interface(lower, upper, face, inverse, mortar):
    by_row, spots, place = mortar
    low_t, upp_t = turn(lower, upper)
    rhs = low_t - project(by_row, spots, upp_t)
    first = face * rhs
    back = project_back(by_row, place, first) * inverse
    rest = 0.6 * rhs - project(by_row, spots, back)
    increment = first + face * rest
    return turn_back(increment, project_back(by_row, place, increment))


def tall(plane):
    return jnp.concatenate([plane] * 3, 0)


def yes(flags, row, shape):
    line = jnp.concatenate([flags[row : row + 1, :]] * (shape[1] // 128), 1)
    return jnp.broadcast_to(line, shape) == 1


def sides(flags, y_first, y_second, z_first, z_second):
    tall_shape, zero = (LINES, 128), jnp.zeros((LINES, 128), F32)
    y_even, z_even = yes(flags, 0, tall_shape), yes(flags, 1, (8, 128))
    a, b, c, d = y_first[0:LINES], y_second[0:LINES], z_first[0:8, 0:128], z_second[0:8]
    return (
        jnp.where(yes(flags, 2, tall_shape), jnp.where(y_even, b, a), zero),
        jnp.where(yes(flags, 3, tall_shape), jnp.where(y_even, a, b), zero),
        jnp.where(yes(flags, 4, (8, 128)), jnp.where(z_even, d, c), zero[0:8]),
        jnp.where(yes(flags, 5, (8, 128)), jnp.where(z_even, c, d), zero[0:8]),
    )


def place_of(p, c):
    return ROWS * c + p


def residual_of(p, c, force, weight, velocity, halo):
    y_low, y_high, z_low, z_high = halo
    i = place_of(p, c)
    sub = lax.broadcasted_iota(jnp.int32, (8, 128), 0)
    lane = lax.broadcasted_iota(jnp.int32, (8, 128), 1)
    v = velocity[p, c]
    total = force[p, c] - weight[p] * v
    if p not in (0, LOW):
        total = total + velocity[p - 1, c]
    if p not in (NP - 1, UPP):
        total = total + velocity[p + 1, c]
    total = total + jnp.where(sub == 0, y_low[i : i + 1], pltpu.roll(v, 1, 0))
    total = total + jnp.where(sub == 7, y_high[i : i + 1], pltpu.roll(v, 7, 0))
    total = total + jnp.where(lane == 0, pltpu.roll(z_low, (128 - i) % 128, 1), pltpu.roll(v, 1, 1))
    total = total + jnp.where(lane == 127, pltpu.roll(z_high, 127 - i, 1), pltpu.roll(v, 127, 1))
    return total


def write_lines(flags, get, y_first, y_second, row=0, count=3):
    y_even = yes(flags, 0, (1, 128))
    for c in range(count):
        for p in range(NP):
            v = get(p, c)
            i = row + place_of(p, c)
            y_first[i : i + 1] = jnp.where(y_even, v[7:8], v[0:1])
            y_second[i : i + 1] = jnp.where(y_even, v[0:1], v[7:8])
        i = row + place_of(NP, c)
        y_first[i : i + ROWS - NP] = jnp.zeros((ROWS - NP, 128), F32)
        y_second[i : i + ROWS - NP] = jnp.zeros((ROWS - NP, 128), F32)


def write_columns(flags, get, z_first, z_second, row=0):
    z_even = yes(flags, 1, (8, 128))
    lane = lax.broadcasted_iota(jnp.int32, (8, 128), 1)
    first = jnp.zeros((8, 128), F32)
    last = first
    for c in range(3):
        for p in range(NP):
            v, i = get(p, c), place_of(p, c)
            first = jnp.where(lane == i, pltpu.roll(v, i, 1) if i else v, first)
            last = jnp.where(lane == i, pltpu.roll(v, i + 1, 1), last)
    z_first[row : row + 8] = jnp.where(z_even, last, first)
    z_second[row : row + 8] = jnp.where(z_even, first, last)


def first_sweep_kernel(
    flags, force_in, kappa_in, agg_in, tail, by_row, spots, place,
    force, weight, inverse, agg, velocity, mult, mult_up, face, inverse_t, z1, z2,
):
    for p in range(NP):
        here = p - TAIL
        kappa = tail[p, 3] if here < 0 else kappa_in[here]
        w = 6.0 + kappa
        weight[p] = w
        inverse[p] = 1.0 / (1.5 * w)
        agg[p] = tail[p, 4].astype(jnp.int32) if here < 0 else agg_in[here]
        for c in range(3):
            f = tail[p, c] if here < 0 else force_in[c, here]
            force[p, c] = f
            velocity[p, c] = f * inverse[p]
    low_w, upp_inv = turn(tall(weight[LOW]), tall(inverse[UPP]))
    face[...] = 0.6 * low_w
    inverse_t[...] = upp_inv
    lower = velocity[LOW].reshape(24, 128)
    upper = velocity[UPP].reshape(24, 128)
    increment, pulled = solve_interface(
        lower, upper, face[...], upp_inv, (by_row, spots, place)
    )
    mult[...] = increment.reshape(3, 8, 128)
    mult_up[...] = pulled.reshape(3, 8, 128)
    velocity[LOW] = (lower - increment * tall(inverse[LOW])).reshape(3, 8, 128)
    velocity[UPP] = (upper + pulled * tall(inverse[UPP])).reshape(3, 8, 128)
    write_columns(flags, lambda p, c: velocity[p, c], z1, z2)
    write_columns(flags, lambda p, c: agg[p].astype(F32), z1, z2, 8)


def lines_kernel(flags, velocity, y1, y2):
    write_lines(flags, lambda p, c: velocity[p, c], y1, y2)


def lines_and_labels_kernel(flags, velocity, agg, y1, y2):
    write_lines(flags, lambda p, c: velocity[p, c], y1, y2)
    write_lines(flags, lambda p, c: agg[p].astype(F32), y1, y2, LINES, 1)


def sweep(
    flags, force, weight, inverse, velocity, mult, mult_up, face, inverse_t, by_row, spots, place,
    halo, out, out_mult, out_up,
):
    def residuals(p):
        return jnp.concatenate([residual_of(p, c, force, weight, velocity, halo) for c in range(3)], 0)

    res_low = residuals(LOW) - mult[...].reshape(24, 128)
    res_upp = residuals(UPP) + mult_up[...].reshape(24, 128)
    inv_low, inv_upp = tall(inverse[LOW]), tall(inverse[UPP])
    lower = velocity[LOW].reshape(24, 128) + res_low * inv_low
    upper = velocity[UPP].reshape(24, 128) + res_upp * inv_upp
    increment, pulled = solve_interface(
        lower, upper, face[...], inverse_t[...], (by_row, spots, place)
    )
    out_mult[...] = mult[...] + increment.reshape(3, 8, 128)
    out_up[...] = mult_up[...] + pulled.reshape(3, 8, 128)
    for p in range(NP):
        if p in (LOW, UPP):
            continue
        for c in range(3):
            out[p, c] = velocity[p, c] + residual_of(p, c, force, weight, velocity, halo) * inverse[p]
    out[LOW] = (lower - increment * inv_low).reshape(3, 8, 128)
    out[UPP] = (upper + pulled * inv_upp).reshape(3, 8, 128)


def second_sweep_kernel(
    flags, force, weight, inverse, velocity, mult, mult_up, face, inverse_t, by_row, spots, place,
    z2, y1, y2, z1, out, out_mult, out_up, oz1, oz2,
):
    halo = sides(flags, y1, y2, z1, z2)
    sweep(
        flags, force, weight, inverse, velocity, mult, mult_up, face, inverse_t, by_row, spots, place,
        halo, out, out_mult, out_up,
    )
    write_columns(flags, lambda p, c: out[p, c], oz1, oz2)


class Joined:
    def __init__(self, tail, head):
        self.tail, self.head = tail, head

    def __getitem__(self, at):
        p, *rest = at if isinstance(at, tuple) else (at,)
        array, p = (self.tail, p) if p < TAIL else (self.head, p - TAIL)
        return array[(p, *rest)]


def spread_kernel(velocity, agg, iterate, out):
    own = table(iterate[...])
    for p in range(HEAD):
        at = where_in(agg[TAIL + p])
        for c in range(3):
            out[p, c] = velocity[TAIL + p, c] + pick(own[c], at)


def third_sweep_kernel(
    flags, force, weight, inverse, old, mult, mult_up, face, inverse_t, by_row, spots, place,
    z2, y1, y2, z1, az2, ay1, ay2, az1, agg, iterate, got, swapped, lifted,
    out, out_mult, out_up, oz1, oz2, lower_part,
):
    core_zero = yes(flags, 1, (24, NAGG))
    a = jnp.where(core_zero, got[...], swapped[...])
    b = jnp.where(core_zero, swapped[...], got[...])
    own, prev = table(iterate[...]), table(a[8:16])
    low, low_prev = table(b[8:16]), table(b[0:8])
    high, high_prev = table(a[16:24]), table(a[0:8])
    for p in range(TAIL):
        at = where_in(agg[p])
        for c in range(3):
            lower_part[p, c] = old[p, c] + pick(prev[c], at)
    velocity = Joined(lower_part, lifted)

    y_low, y_high, z_low, z_high = sides(flags, y1, y2, z1, z2)
    y_even, z_even = yes(flags, 0, (ROWS, 128)), yes(flags, 1, (8, 128))
    ay1, ay2, az1, az2 = ay1[LINES : LINES + ROWS], ay2[LINES : LINES + ROWS], az1[0:8, 128:256], az2[8:16]
    sub = lax.broadcasted_iota(jnp.int32, (8, 128), 0)
    lane = lax.broadcasted_iota(jnp.int32, (8, 128), 1)

    def lines(values, labels, mine, below, flag):
        labels = labels.astype(jnp.int32)
        parts = []
        for c in range(3):
            for block in range(ROWS // 8):
                at = where_in(labels[8 * block : 8 * block + 8])
                extra = pick(mine[c], at)
                if block == 0:
                    extra = jnp.where(sub < TAIL, pick(below[c], at), extra)
                row = place_of(8 * block, c)
                parts.append(jnp.where(yes(flags, flag, (8, 128)), values[row : row + 8] + extra, 0.0))
        return jnp.concatenate(parts, 0)

    def column(values, labels, flag):
        at = where_in(labels.astype(jnp.int32))
        extra = jnp.zeros((8, 128), F32)
        for c in range(3):
            here = lane - ROWS * c
            extra = jnp.where((here >= 0) & (here < TAIL), pick(prev[c], at), extra)
            extra = jnp.where((here >= TAIL) & (here < NP), pick(own[c], at), extra)
        return jnp.where(yes(flags, flag, (8, 128)), values + extra, 0.0)

    halo = (
        lines(y_low, jnp.where(y_even, ay2, ay1), low, low_prev, 2),
        lines(y_high, jnp.where(y_even, ay1, ay2), high, high_prev, 3),
        column(z_low, jnp.where(z_even, az2, az1), 4),
        column(z_high, jnp.where(z_even, az1, az2), 5),
    )
    sweep(
        flags, force, weight, inverse, velocity, mult, mult_up, face, inverse_t, by_row, spots, place,
        halo, out, out_mult, out_up,
    )
    write_columns(flags, lambda p, c: out[p, c], oz1, oz2)


def last_sweep_kernel(
    flags, force, weight, inverse, velocity, mult, mult_up, face, inverse_t, by_row, spots, place,
    z2, y1, y2, z1, head, tail, out_mult, out, out_up,
):
    halo = sides(flags, y1, y2, z1, z2)
    sweep(
        flags, force, weight, inverse, velocity, mult, mult_up, face, inverse_t, by_row, spots, place,
        halo, out, out_mult, out_up,
    )
    for c in range(3):
        for p in range(16 - RET):
            head[c, p] = out[LOW + p, c]
        for p in range(RET):
            tail[c, p] = out[TAIL - RET + p, c]


def restrict_kernel(
    after, flags, force, weight, velocity, mult, mult_up, agg, diag, z2, y1, y2, z1, out, res,
):
    halo = sides(flags, y1, y2, z1, z2)
    for p in range(TAIL - 3, NP - 2):
        for c in range(3):
            r = residual_of(p, c, force, weight, velocity, halo)
            if p == LOW:
                r = r - mult[c]
            if p == UPP:
                r = r + mult_up[c]
            res[p, c] = r
    down = lax.broadcasted_iota(jnp.int32, (64, 128), 0)
    sub = lax.broadcasted_iota(jnp.int32, (8, 128), 0)

    def plane(p, total):
        labels = agg[p]
        lows = labels & 63
        highs = lax.shift_right_logical(labels, 6)
        values = []
        for c in range(3):
            r = res[p, c]
            high = r.astype(BF16).astype(F32)
            values += [high, r - high]
        for pair in range(4):
            tables, terms = [], []
            for y in (2 * pair, 2 * pair + 1):
                tables.append(jnp.where(down == lows[y : y + 1], 1.0, 0.0).astype(BF16))
                here = highs[y : y + 1] == sub
                terms.append(jnp.concatenate([jnp.where(here, v[y : y + 1], 0.0) for v in values], 0).astype(BF16))
            total = total + lax.dot_general(
                jnp.concatenate(tables, 1), jnp.concatenate(terms, 1), (((1,), (1,)), ((), ())),
                preferred_element_type=F32,
            )
        return total

    def four(i, total):
        for s in range(4):
            total = plane(LOW + 4 * i + s, total)
        return total

    below = jnp.zeros((64, 48), F32)
    for p in range(TAIL - 3, TAIL):
        below = plane(p, below)
    own = lax.fori_loop(0, 3, four, plane(NP - 3, jnp.zeros((64, 48), F32)))
    both = jnp.concatenate([own, below], 0)
    turned = jnp.concatenate([both, jnp.zeros((128, 80), F32)], 1).T
    for c in range(3):
        out[8 * c : 8 * c + 8] = turned[16 * c : 16 * c + 8] + turned[16 * c + 8 : 16 * c + 16]
    out[24:32] = jnp.where(sub == flags[6:7], jnp.broadcast_to(diag[...], (8, 128)), 0.0)


def gather_sums_kernel(mine, above, across, kept, passed):
    kept[...] = mine[...] + across[...]
    lane = lax.broadcasted_iota(jnp.int32, (24, 128), 1)
    passed[...] = jnp.where(lane < 64, pltpu.roll(above[0:24], 64, 1), 0.0)


def add_kernel(one, two, out):
    out[...] = one[...] + two[...]


def join_kernel(a, b, c, out):
    out[0:8], out[8:16], out[16:24] = a[...], b[...], c[...]


def add(one, two):
    return call(add_kernel, [(one.shape, F32)], n_in=2)(one, two)[0]


def pack_kernel(force, kappa, agg, matrix, out, force_near, kappa_near, agg_near, rows, more_rows, flags, sems):
    copies = [
        pltpu.make_async_copy(far, near, sems.at[i])
        for i, (far, near) in enumerate(
            (
                (force, force_near), (kappa, kappa_near), (agg, agg_near),
                (matrix.at[pl.ds(0, 64)], rows), (matrix.at[pl.ds(64, 64)], more_rows),
            )
        )
    ]
    for copy in copies:
        copy.start()
    gy, gz = lax.axis_index("gy"), lax.axis_index("gz")
    ny, nz = lax.axis_size("gy"), lax.axis_size("gz")
    facts = (gy % 2 == 1, gz % 2 == 0, gy > 0, gy < ny - 1, gz > 0, gz < nz - 1, gz, gz < nz // 2)
    for row, fact in enumerate(facts):
        flags[row : row + 1, :] = jnp.full((1, 128), fact.astype(jnp.int32), jnp.int32)
    for copy in copies:
        copy.wait()
    start = kappa.shape[0] - TAIL
    for p in range(TAIL):
        for c in range(3):
            out[p, c] = force_near[c, start + p]
        out[p, 3] = kappa_near[start + p]
        out[p, 4] = agg_near[start + p].astype(F32)


def stack_kernel(columns, one, two, three, four, out):
    out[0:8, 0:128], out[0:8, 128:256] = columns[0:8], columns[8:16]
    out[0:8, 256:NAGG] = jnp.zeros((8, NAGG - 256), F32)
    for i, part in enumerate((one, two, three, four)):
        out[8 + 64 * i : 72 + 64 * i] = part[...]


def split_matrix_kernel(flags, mine, other, high, low):
    core_zero, first_half = yes(flags, 1, (256, NAGG)), yes(flags, 7, (128, NAGG))
    one, two = mine[8:264], other[8:264]
    sets = jnp.where(core_zero, one, two), jnp.where(core_zero, two, one)
    for b in range(4):
        rows = sets[b % 2]
        near, far = (rows[0:128], rows[128:256]) if b < 2 else (rows[128:256], rows[0:128])
        a = jnp.where(first_half, near, far).T
        h = a.astype(BF16)
        high[:, 128 * b : 128 * b + 128] = h
        low[:, 128 * b : 128 * b + 128] = (a - h.astype(F32)).astype(BF16)


def solve_kernel(kept, passed, swapped, high, low, out, rhs):
    sums = kept[0:24] + passed[...] + swapped[...]
    other = pltpu.roll(sums, 64, 1)
    rhs[...] = jnp.zeros((8, NAGG), F32)
    left = lax.broadcasted_iota(jnp.int32, (1, 128), 1) < 64
    for c in range(3):
        for t in range(4):
            at = 8 * c + 2 * t
            rhs[c : c + 1, 128 * t : 128 * t + 128] = jnp.where(left, sums[at : at + 1], other[at + 1 : at + 2])
    gain = (16 * 8 * 512 / NAGG) ** -0.5
    scale = jnp.concatenate([kept[24 + b : 25 + b] for b in range(4)], 1)
    step = jnp.broadcast_to(COARSE_OMEGA / scale, (8, NAGG))
    start = (rhs[...] * gain) * step
    x = start
    for _ in range(3):
        xh, xl = split(x)
        both = jnp.concatenate([xh, xl], 0)
        first = jnp.dot(both, high[...], preferred_element_type=F32)
        second = jnp.dot(xh, low[...], preferred_element_type=F32)
        product = first[0:8] + first[8:16] + second
        x = (1.0 - COARSE_OMEGA) * x + (start - step * product)
    out[...] = x


def table(rows):
    return [
        [jnp.broadcast_to(rows[c : c + 1, 128 * t : 128 * t + 128], (8, 128)) * PROLONG_GAIN for t in range(4)]
        for c in range(3)
    ]


def where_in(labels):
    return labels & 127, lax.shift_right_logical(labels, 7)


def pick(rows, at):
    lane, tile = at
    got = [jnp.take_along_axis(row, lane, axis=1, mode="promise_in_bounds") for row in rows]
    return jnp.where(tile < 2, jnp.where(tile == 0, got[0], got[1]), jnp.where(tile == 2, got[2], got[3]))


def write_head_kernel(head, mult, velocity, out_mult, sems):
    copies = [
        pltpu.make_async_copy(head, velocity.at[:, pl.ds(0, 16 - RET)], sems.at[0]),
        pltpu.make_async_copy(mult, out_mult, sems.at[1]),
    ]
    for copy in copies:
        copy.start()
    for copy in copies:
        copy.wait()


def write_tail_kernel(tail, before, velocity, sem):
    copy = pltpu.make_async_copy(tail, velocity.at[:, pl.ds(16 - RET, RET)], sem)
    copy.start()
    copy.wait()


def ring(axis, by):
    n = lax.axis_size(axis)
    return [(i, (i + by) % n) for i in range(n)]


def swaps(axis, first):
    n = lax.axis_size(axis)
    pairs = []
    for i in range(first, first + n, 2):
        a, b = i % n, (i + 1) % n
        pairs += [(a, b), (b, a)]
    return pairs


def trade(y1, y2, z1, z2):
    return [
        lax.ppermute(z2, "gz", swaps("gz", 1)),
        lax.ppermute(y1, "gy", swaps("gy", 1)),
        lax.ppermute(y2, "gy", swaps("gy", 0)),
        lax.ppermute(z1, "gz", swaps("gz", 0)),
    ]


def by_core(x, rule_zero, rule_one):
    nx, ny, nz = lax.axis_size("gx"), lax.axis_size("gy"), lax.axis_size("gz")
    pairs = []
    for g in range(nx):
        for y in range(ny):
            for z in range(nz):
                dx, dy, dz = rule_one if z % 2 else rule_zero
                to = (((g + dx) % nx) * ny + (y + dy) % ny) * nz + (z + dz) % nz
                pairs.append(((g * ny + y) * nz + z, to))
    return lax.ppermute(x, ("gx", "gy", "gz"), pairs)


def shards(force, kappa, mortar_blocks, mortar_index, mortar_count, agg_map, coarse_matrix, coarse_diag):
    tail_in, force, kappa, agg_map, rows, more_rows, flags = call(
        pack_kernel,
        [((TAIL, 5, 8, 128), F32), (force.shape, F32), (kappa.shape, F32), (agg_map.shape, jnp.int32),
         ((64, NAGG), F32), ((64, NAGG), F32), ((8, 128), jnp.int32)],
        [pltpu.SemaphoreType.DMA((5,))],
        n_far=4,
    )(force, kappa, agg_map, coarse_matrix.reshape(128, NAGG))
    tail_in = lax.ppermute(tail_in, "gx", ring("gx", 1))
    half, more_half = [lax.ppermute(x, "gz", ring("gz", 2)) for x in (rows, more_rows)]

    by_row, spots, place = call(
        prepare_kernel,
        [((2, 4096, 128), F32), ((8, 256), jnp.int32), ((128, 256), BF16)],
        [pltpu.VMEM((4, 192, 1024), F32), pltpu.VMEM((2, 192, 128), F32), pltpu.VMEM((8, 128), jnp.int32),
         pltpu.VMEM((4, 48), jnp.int32), pltpu.VMEM((1, 48), jnp.int32), pltpu.SemaphoreType.DMA((6,))],
        n_in=1,
        n_far=3,
    )(
        flags,
        mortar_blocks.reshape(192, 4096),
        jnp.transpose(mortar_index.reshape(48, 4), (1, 0)),
        mortar_count.reshape(1, 48),
    )

    field = ((NP, 3, 8, 128), F32)
    plane = ((3, 8, 128), F32)
    turned = ((64, 128), F32)
    y_msg, z_msg = ((LINES, 128), F32), ((8, 128), F32)
    y_more, z_more = ((LINES + ROWS, 128), F32), ((16, 128), F32)
    out = call(
        first_sweep_kernel,
        [field, ((NP, 8, 128), F32), ((NP, 8, 128), F32), ((NP, 8, 128), jnp.int32), field, plane, plane,
         turned, turned, z_more, ((LINES + ROWS + 8, 128), F32)],
        n_in=8,
    )(flags, force, kappa, agg_map, tail_in, by_row, spots, place)
    force_e, weight, inverse, agg, velocity, mult, mult_up, face, inverse_t = out[:9]
    lines = call(lines_and_labels_kernel, [y_more, y_more], n_in=3)(flags, velocity, agg)
    stacked = call(stack_kernel, [((264, NAGG), F32)], n_in=5)(out[9], rows, more_rows, half, more_half)[0]
    labels = trade(*lines, stacked, out[10])
    k_high, k_low = call(split_matrix_kernel, [((NAGG, NAGG), BF16)] * 2, n_in=3)(flags, stacked, labels[3])
    velocity, mult, mult_up, *msgs = call(
        second_sweep_kernel, [field, plane, plane, z_msg, ((LINES + 8, 128), F32)], n_in=16
    )(flags, force_e, weight, inverse, velocity, mult, mult_up, face, inverse_t, by_row, spots, place, *labels)
    edges = trade(*call(lines_kernel, [y_msg, y_msg], n_in=2)(flags, velocity), *msgs)
    sums = call(
        restrict_kernel, [((32, 128), F32)], [pltpu.VMEM((NP, 3, 8, 128), F32)], n_in=13
    )(k_high, flags, force_e, weight, velocity, mult, mult_up, agg, coarse_diag.reshape(1, 128), *edges)[0]
    sums = add(sums, lax.ppermute(sums, "gz", swaps("gz", 0)))
    above = by_core(sums, (-1, 0, 2), (-1, 0, 0))
    across = lax.ppermute(sums, "gz", ring("gz", 2))
    kept, passed = call(gather_sums_kernel, [((32, 128), F32), ((24, 128), F32)], n_in=3)(
        sums, above, across
    )
    swapped = lax.ppermute(passed, "gz", swaps("gz", 0))
    iterate = call(solve_kernel, [((8, NAGG), F32)], [pltpu.VMEM((8, NAGG), F32)], n_in=5)(
        kept, passed, swapped, k_high, k_low
    )[0]
    lifted = call(spread_kernel, [((HEAD, 3, 8, 128), F32)], n_in=3)(velocity, agg, iterate)[0]
    got = [
        by_core(iterate, (1, -1, 0), (1, 1, 0)),
        by_core(iterate, (1, 0, 0), (0, 1, 0)),
        by_core(iterate, (0, -1, 0), (0, 1, 0)),
    ]
    got = call(join_kernel, [((24, NAGG), F32)], n_in=3)(*got)[0]
    swapped = lax.ppermute(got, "gz", swaps("gz", 0))
    velocity, mult, mult_up, *msgs = call(
        third_sweep_kernel, [field, plane, plane, z_msg, ((LINES + 8, 128), F32)],
        [pltpu.VMEM((TAIL, 3, 8, 128), F32)], n_in=25,
    )(
        flags, force_e, weight, inverse, velocity, mult, mult_up, face, inverse_t, by_row, spots, place,
        *edges, *labels, agg, iterate, got, swapped, lifted,
    )
    edges = trade(*call(lines_kernel, [y_msg, y_msg], n_in=2)(flags, velocity), *msgs)
    head, tail, mult = call(
        last_sweep_kernel, [((3, 16 - RET, 8, 128), F32), ((3, RET, 8, 128), F32), plane],
        [pltpu.VMEM((NP, 3, 8, 128), F32), pltpu.VMEM((3, 8, 128), F32)], n_in=16,
    )(flags, force_e, weight, inverse, velocity, mult, mult_up, face, inverse_t, by_row, spots, place, *edges)
    tail = lax.ppermute(tail, "gx", ring("gx", -1))
    shapes = [pltpu.HBM((3, 16, 8, 128), F32), pltpu.HBM((3, 8, 128), F32)]
    velocity, mult = pl.pallas_call(
        write_head_kernel, out_shape=shapes, in_specs=[VMEM] * 2, out_specs=[HBM] * 2,
        scratch_shapes=[pltpu.SemaphoreType.DMA((2,))],
        compiler_params=pltpu.CompilerParams(vmem_limit_bytes=12 * 1024 * 1024),
    )(keep(head), keep(mult))
    velocity = pl.pallas_call(
        write_tail_kernel, out_shape=shapes[0], in_specs=[VMEM, HBM], out_specs=HBM,
        scratch_shapes=[pltpu.SemaphoreType.DMA], input_output_aliases={1: 0},
        compiler_params=pltpu.CompilerParams(vmem_limit_bytes=12 * 1024 * 1024),
    )(keep(tail), pltpu.with_memory_space_constraint(velocity, pltpu.HBM))
    return velocity, mult[None]


def solution(mesh):
    in_specs = (
        P(None, "gx", "gy", "gz"),
        P("gx", "gy", "gz"),
        P("gx", "gy", "gz", None, None),
        P("gx", "gy", "gz", None, None),
        P("gx", "gy", "gz", None),
        P("gx", "gy", "gz"),
        P("gx", "gy", "gz", None),
        P("gx", "gy", "gz"),
    )
    out_specs = (P(None, "gx", "gy", "gz"), P("gx", None, "gy", "gz"))
    return jax.shard_map(shards, mesh=mesh, in_specs=in_specs, out_specs=out_specs, check_vma=False)
```
